32 devices in a mesh: dp: 4 (over x, core), region: 4 (over z), heads: 2 (over y).
Axes of the slice: x: 2, y: 2, z: 4, core: 2. Of those that a mesh axis runs over, the one named last changes fastest.
Arguments:
- enc_in: bfloat16 [8, 192, 1152], P('dp', 'region'), may hold values from -6 to 6
- kept_pos: int32 [8, 192], P('dp', 'region'), may hold values from 0 to 63, as said below
- slot_live: int32 [8, 192], P('dp', 'region'), may hold values from 0 to 1, as said below
- condition: bfloat16 [8, 1152], P('dp'), may hold values from -6 to 6
- mask_token: bfloat16 [1152], replicated, may hold values from -6 to 6
- enc_ada: bfloat16 [1152, 6912], P(None, ('region', 'heads')), may hold values from -0.1875 to 0.1875
- enc_qkv: bfloat16 [1152, 3, 1152], P(None, None, 'heads'), may hold values from -0.1875 to 0.1875
- enc_proj: bfloat16 [1152, 1152], P('heads'), may hold values from -0.5 to 0.5
- enc_up: bfloat16 [1152, 4608], P(None, 'heads'), may hold values from -0.1875 to 0.1875
- enc_down: bfloat16 [4608, 1152], P('heads'), may hold values from -0.09375 to 0.09375
- dec_ada: bfloat16 [1152, 6912], P(None, ('region', 'heads')), may hold values from -0.1875 to 0.1875
- dec_qkv: bfloat16 [1152, 3, 1152], P(None, None, 'heads'), may hold values from -0.1875 to 0.1875
- dec_proj: bfloat16 [1152, 1152], P('heads'), may hold values from -0.5 to 0.5
- dec_up: bfloat16 [1152, 4608], P(None, 'heads'), may hold values from -0.1875 to 0.1875
- dec_down: bfloat16 [4608, 1152], P('heads'), may hold values from -0.09375 to 0.09375
- cotangent: bfloat16 [8, 256, 1152], P('dp', 'region'), may hold values from -6 to 6
Outputs:
- out: bfloat16 [8, 256, 1152], P('dp', 'region')
- input_grad: float32 [8, 192, 1152], P('dp', 'region')
- mask_grad: float32 [1152], P(('dp', 'region'))
- enc_ada_grad: float32 [1152, 6912], P('dp', ('region', 'heads'))
- enc_qkv_grad: float32 [1152, 3, 1152], P(('dp', 'region'), None, 'heads')
- enc_proj_grad: float32 [1152, 1152], P('heads', ('dp', 'region'))
- enc_up_grad: float32 [1152, 4608], P(('dp', 'region'), 'heads')
- enc_down_grad: float32 [4608, 1152], P('heads', ('dp', 'region'))
- dec_ada_grad: float32 [1152, 6912], P('dp', ('region', 'heads'))
- dec_qkv_grad: float32 [1152, 3, 1152], P(('dp', 'region'), None, 'heads')
- dec_proj_grad: float32 [1152, 1152], P('heads', ('dp', 'region'))
- dec_up_grad: float32 [1152, 4608], P(('dp', 'region'), 'heads')
- dec_down_grad: float32 [4608, 1152], P('heads', ('dp', 'region'))
The draws below stay inside these ranges and needn't reach their ends.
Inputs may be any that keep to these rules, and one draw needn't show every extreme that they name: `kept_pos`: positions are counted within the image's region of 64 tokens; the 48 slots of one image in one region hold distinct positions. `slot_live`: in each image and region the live slots come first and number from 16 to 48; each image has 128 live slots in all, and in every image one region has all 48 slots live.
All inputs are finite; a program needn't handle non-finite values.
Results may differ from the reference program's by a relative error of at most 0.035.
Values may be sent and summed in bfloat16 or wider, within the bound.
No kernel may reach another device: no remote copies, remote signals or barrier semaphores. Data moves between devices by JAX's collectives and lax.ppermute only.
A program may use at most 320 MiB of HBM per device.

```python
import math
import jax
import jax.numpy as jnp
from jax import lax

D = 1152
HEADS = 16
HS = 72
FF = 4608
TOK_IMG = 256
REGIONS = 4
REG_TOK = 64
CAP = 48
IMAGES = 8


def kept_plan(key):
    first, second, third = jax.random.split(key, 3)
    big_region = jax.random.randint(first, (IMAGES,), 0, REGIONS)
    extra = REG_TOK // 2
    cuts = jnp.sort(jax.random.randint(second, (IMAGES, 2), 0, extra + 1), axis=1)
    shares = jnp.stack([cuts[:, 0], cuts[:, 1] - cuts[:, 0], extra - cuts[:, 1]], axis=1)
    region_ids = jnp.arange(REGIONS, dtype=jnp.int32)
    order = (region_ids[None, :] - big_region[:, None] - 1) % REGIONS
    picked = jnp.take_along_axis(shares, jnp.minimum(order, 2), axis=1)
    counts = jnp.where(order == REGIONS - 1, CAP, REG_TOK // 4 + picked)
    row_keys = jax.random.split(third, IMAGES * REGIONS)
    perms = jax.vmap(lambda row_key: jax.random.permutation(row_key, REG_TOK))(row_keys)[:, :CAP]
    positions = perms.reshape(IMAGES, REGIONS * CAP).astype(jnp.int32)
    slot_ids = jnp.arange(CAP, dtype=jnp.int32)
    live_slots = (slot_ids[None, None, :] < counts[:, :, None]).astype(jnp.int32)
    return (positions, live_slots.reshape(IMAGES, REGIONS * CAP))


def draw_kept_pos(key, part):
    return kept_plan(key)[0]


def draw_slot_live(key, part):
    return kept_plan(key)[1]


def raised(entries, key, source, target, parts, factor):
    owner, partner = [(jnp.arange(entries.shape[position]) // (entries.shape[position] // parts)).reshape([-1 if axis == position else 1 for axis in range(entries.ndim)]) for position in (source, target)]
    chosen = jax.random.permutation(key, parts)[partner]
    strong = (owner == chosen) | (owner == (partner + parts // 2) % parts)
    return jnp.where(strong, factor * entries, entries)


def level_of(own_key, extent, shards, smallest, high):
    factor_of = 1.0
    for dim, shards_of in shards:
        draws = jax.random.uniform(jax.random.fold_in(jax.random.fold_in(own_key, 6), dim), (shards_of,), jnp.float32, smallest / len(shards), high / len(shards))
        factor_of = factor_of * jnp.repeat(jnp.exp(draws), extent[dim] // shards_of).reshape((-1,) + (1,) * (len(extent) - 1 - dim))
    return factor_of


def noise(key, dims, scale, limit, shards=(), held_as=jnp.bfloat16):
    drawn = scale * jax.random.normal(key, dims, jnp.float32)
    if shards:
        drawn = drawn * level_of(key, dims, shards, -0.22, 0.18)
    return jnp.clip(drawn, -limit, limit).astype(held_as)


def gaussian_with(rng, extent, spread, reach, cuts, heavy, kind=jnp.bfloat16):
    entries = spread * jax.random.normal(rng, extent, jnp.float32)
    if cuts:
        entries = entries * level_of(rng, extent, cuts, -0.22, 0.18)
    return jnp.clip(raised(entries, jax.random.fold_in(rng, 3), *heavy), -reach, reach).astype(kind)


def setup_inputs(seed: int = 0) -> dict:
    splits = jax.random.split(jax.random.key(seed), 17)
    enc_in = noise(splits[0], (IMAGES, REGIONS * CAP, D), 1.0, 6.0, ((0, 4), (1, 4)))
    kept_pos = draw_kept_pos(jax.random.fold_in(splits[16], 71), 0)
    slot_live = draw_slot_live(jax.random.fold_in(splits[16], 71), 0)
    condition = noise(splits[3], (IMAGES, D), 1.0, 6.0, ((0, 4),))
    mask_token = noise(splits[4], (D,), 1.0, 6.0)
    enc_ada = noise(splits[5], (D, 6 * D), D ** -0.5, 0.1875, ((1, 8),))
    enc_qkv = noise(splits[6], (D, 3, D), D ** -0.5, 0.1875, ((2, 2),))
    enc_proj = noise(splits[7], (D, D), (D // 8) ** -0.5, 0.5, ((0, 2),))
    enc_up = noise(splits[8], (D, FF), D ** -0.5, 0.1875, ((1, 2),))
    enc_down = noise(splits[9], (FF, D), FF ** -0.5, 0.09375, ((0, 2),))
    dec_ada = noise(splits[10], (D, 6 * D), D ** -0.5, 0.1875, ((1, 8),))
    dec_qkv = noise(splits[11], (D, 3, D), D ** -0.5, 0.1875, ((2, 2),))
    dec_proj = noise(splits[12], (D, D), (D // 8) ** -0.5, 0.5, ((0, 2),))
    dec_up = noise(splits[13], (D, FF), D ** -0.5, 0.1875, ((1, 2),))
    dec_down = noise(splits[14], (FF, D), FF ** -0.5, 0.09375, ((0, 2),))
    cotangent = gaussian_with(splits[15], (IMAGES, TOK_IMG, D), 1.0, 6.0, ((0, 4), (1, 4)), (0, 2, 4, 2.0))
    return {"enc_in": enc_in, "kept_pos": kept_pos, "slot_live": slot_live, "condition": condition, "mask_token": mask_token, "enc_ada": enc_ada, "enc_qkv": enc_qkv, "enc_proj": enc_proj, "enc_up": enc_up, "enc_down": enc_down, "dec_ada": dec_ada, "dec_qkv": dec_qkv, "dec_proj": dec_proj, "dec_up": dec_up, "dec_down": dec_down, "cotangent": cotangent}


@jax.custom_vjp
def low(v):
    return lax.optimization_barrier(v.astype(jnp.bfloat16)).astype(jnp.float32)

@jax.custom_vjp
def low_back(v):
    return v

def low_keep(v):
    return (low(v), None)

def low_pass(kept, grad):
    return (grad,)

def back_keep(v):
    return (v, None)

def back_low(kept, grad):
    return (low(grad),)
low.defvjp(low_keep, low_pass)
low_back.defvjp(back_keep, back_low)
EPSILON = 1e-06

def product(form, left, right):
    return jnp.einsum(form, left, right, precision=lax.Precision.HIGHEST)

def normalize(token_row_block):
    mean_row = lax.optimization_barrier(jnp.mean(token_row_block, axis=-1, keepdims=True))
    centered = token_row_block - mean_row
    variance = lax.optimization_barrier(jnp.mean(centered * centered, axis=-1, keepdims=True))
    return centered * lax.rsqrt(variance + EPSILON)

def diffusion_transformer_block(token_row_block, modulation_input, query_key_value_matrix, projection_matrix, up_matrix, down_matrix, key_padding_mask):
    images, length, features = token_row_block.shape
    pieces = [modulation_input[:, index * features:(index + 1) * features][:, None, :] for index in range(6)]
    shift_attn, scale_attn, gate_attn, shift_mlp, scale_mlp, gate_mlp = pieces
    hidden = low(normalize(token_row_block) * (1.0 + scale_attn) + shift_attn)
    projected = low_back(low(product('bsd,dtf->bstf', hidden, query_key_value_matrix)))
    queries = projected[:, :, 0].reshape(images, length, HEADS, HS)
    key_heads = projected[:, :, 1].reshape(images, length, HEADS, HS)
    value_heads = projected[:, :, 2].reshape(images, length, HEADS, HS)
    scores = low_back(product('bqhe,bkhe->bhqk', queries, key_heads) * (1.0 / math.sqrt(HS)))
    scores = jnp.where(key_padding_mask[:, None, None, :], scores, -1e+30)
    shifted = scores - lax.optimization_barrier(jnp.max(scores, axis=-1, keepdims=True))
    exponent = jnp.exp(shifted)
    attn_probs = exponent / lax.optimization_barrier(jnp.sum(exponent, axis=-1, keepdims=True))
    attended = low_back(low(product('bhqk,bkhe->bqhe', low(attn_probs), value_heads)))
    attended = attended.reshape(images, length, features)
    branch = low_back(product('bsf,fd->bsd', attended, projection_matrix))
    residual = token_row_block + gate_attn * branch
    mlp_input = low(normalize(residual) * (1.0 + scale_mlp) + shift_mlp)
    pre_gelu = low_back(product('bsd,df->bsf', mlp_input, up_matrix))
    activated = low(jax.nn.gelu(pre_gelu, approximate=True))
    mlp_out = low_back(product('bsf,fd->bsd', activated, down_matrix))
    return residual + gate_mlp * mlp_out

def reference(enc_in, kept_pos, slot_live, condition, mask_token, enc_ada, enc_qkv, enc_proj, enc_up, enc_down, dec_ada, dec_qkv, dec_proj, dec_up, dec_down, cotangent):
    images = enc_in.shape[0]
    silu_cond = low(jax.nn.silu(condition.astype(jnp.float32)))
    kept_slots = kept_pos.reshape(images, REGIONS, CAP)
    live_slots = slot_live.reshape(images, REGIONS, CAP) > 0
    positions = jnp.arange(REG_TOK, dtype=jnp.int32)
    matches = ((kept_slots[:, :, None, :] == positions[None, None, :, None]) & live_slots[:, :, None, :]).astype(jnp.float32)
    uncovered = 1.0 - lax.optimization_barrier(jnp.sum(matches, axis=3))
    encoder_key_rows = slot_live > 0
    decoder_key_rows = jnp.ones((images, TOK_IMG), dtype=bool)

    def forward(encoder_token_rows, mask_vec, e_ada, encoder_query_key_value, encoder_projection_weight, encoder_up_weight, encoder_down_weight, d_ada, query_key_value_gradient, projection_weight_gradient, up_weight_gradient, down_weight_gradient):
        encoder_modulation = low_back(product('bc,ce->be', silu_cond, e_ada))
        decoder_modulation = low_back(product('bc,ce->be', silu_cond, d_ada))
        encoder_output = diffusion_transformer_block(encoder_token_rows, encoder_modulation, encoder_query_key_value, encoder_projection_weight, encoder_up_weight, encoder_down_weight, encoder_key_rows)
        enc_slots = encoder_output.reshape(images, REGIONS, CAP, -1)
        decoder_token_rows = product('grpc,grcd->grpd', matches, enc_slots) + uncovered[..., None] * mask_vec
        decoder_token_rows = decoder_token_rows.reshape(images, TOK_IMG, -1)
        return diffusion_transformer_block(decoder_token_rows, decoder_modulation, query_key_value_gradient, projection_weight_gradient, up_weight_gradient, down_weight_gradient, decoder_key_rows)
    primals = tuple((array.astype(jnp.float32) for array in (enc_in, mask_token, enc_ada, enc_qkv, enc_proj, enc_up, enc_down, dec_ada, dec_qkv, dec_proj, dec_up, dec_down)))
    result, pullback = jax.vjp(forward, *primals)
    gradients = pullback(cotangent.astype(jnp.float32))
    return (result.astype(jnp.bfloat16), gradients[0], gradients[1], gradients[2], gradients[3], gradients[4], gradients[5], gradients[6], gradients[7], gradients[8], gradients[9], gradients[10], gradients[11])
```

```python
import math

import jax
import jax.numpy as jnp
from jax import lax
from jax.sharding import PartitionSpec as P

HS = 72
EPSILON = 1e-06
BF16 = jnp.bfloat16
F32 = jnp.float32


def dot(a, b, dims=((1,), (0,)), **kw):
    return lax.dot_general(a, b, (dims, ((), ())), preferred_element_type=F32, **kw)


def rounded(a):
    return lax.reduce_precision(a, exponent_bits=8, mantissa_bits=7)


def norm(rows):
    mean = jnp.mean(rows, axis=-1, keepdims=True)
    centered = rows - mean
    inverse = lax.rsqrt(jnp.mean(centered * centered, axis=-1, keepdims=True) + EPSILON)
    return centered * inverse, inverse


def norm_back(grad, normed, inverse):
    return inverse * (
        grad
        - jnp.mean(grad, axis=-1, keepdims=True)
        - normed * jnp.mean(grad * normed, axis=-1, keepdims=True)
    )


def in_order(mine, other, bit):
    return jnp.stack([jnp.where(bit == 0, mine, other), jnp.where(bit == 0, other, mine)])


class Net:
    def __init__(self, mesh):
        self.ndp, self.nreg, self.nhead = (mesh.shape[a] for a in ("dp", "region", "heads"))
        assert self.nreg == 4 and self.nhead == 2 and self.ndp % 2 == 0
        self.nhi = self.ndp // 2
        self.core_perm = [(d, d ^ 1) for d in range(self.ndp)]
        self.near = [(z, z ^ 1) for z in range(4)]
        self.far = [(z, z ^ 2) for z in range(4)]
        self.spread = [
            [
                (d * 4 + r, (d - d % 2 + r // 2) * 4 + 2 * (d % 2) + (r + j) % 2)
                for d in range(self.ndp)
                for r in range(4)
            ]
            for j in range(2)
        ]

    def place(self):
        self.dp = lax.axis_index("dp")
        self.hi, self.core = self.dp // 2, self.dp % 2
        self.z = lax.axis_index("region")
        self.z1, self.z0 = self.z // 2, self.z % 2
        self.y = lax.axis_index("heads")

    def to_core(self, a):
        return lax.ppermute(a, "dp", self.core_perm)

    def to_near(self, a):
        return lax.ppermute(a, "region", self.near)

    def to_far(self, a):
        return lax.ppermute(a, "region", self.far)

    def to_heads(self, a):
        return lax.ppermute(a, "heads", [(0, 1), (1, 0)])

    def to_hi(self, a):
        return lax.ppermute(a, "dp", [(d, d ^ 2) for d in range(self.ndp)])

    def hi_groups(self):
        return [[c + 2 * h for h in range(self.nhi)] for c in range(2)]

    def gather_hi(self, a):
        if self.nhi == 1:
            return a[None]
        if self.nhi == 2:
            return in_order(a, self.to_hi(a), self.hi)
        return lax.all_gather(a, "dp", axis_index_groups=self.hi_groups(), axis=0)

    def heads_sum(self, part):
        part = rounded(part)
        return part + self.to_heads(part.astype(BF16)).astype(F32)

    def spread_images(self, a):
        even = self.z0 == 0
        first, second = jnp.where(even, a[0], a[1]), jnp.where(even, a[1], a[0])
        return [
            lax.ppermute(part, ("dp", "region"), perm)
            for part, perm in zip((first, second), self.spread)
        ]

    def collect_images(self, parts):
        back = [
            lax.ppermute(part, ("dp", "region"), [(t, s) for s, t in perm])
            for part, perm in zip(parts, self.spread)
        ]
        even = self.z0 == 0
        return jnp.stack([jnp.where(even, back[0], back[1]), jnp.where(even, back[1], back[0])])

    def gather_rows(self, wide, narrow):
        features = narrow.shape[1]
        own = features // self.ndp
        width = wide.shape[1]
        if self.nhi == 2:
            half = features // 2
            sent = lax.dynamic_slice_in_dim(narrow, (1 - self.hi) * half, half, 1)
            kept = lax.dynamic_slice_in_dim(narrow, self.hi * half, half, 1)
            got = self.to_hi(jnp.concatenate([wide, sent], axis=1))
            wide = jnp.concatenate([wide, got[:, :width]])
            narrow = jnp.concatenate([kept, got[:, width:]])
        else:
            both = jnp.concatenate([wide, narrow], axis=1)
            if self.nhi > 1:
                both = lax.all_gather(
                    both, "dp", axis_index_groups=self.hi_groups(), axis=0, tiled=True
                )
            wide = both[:, :width]
            narrow = lax.dynamic_slice_in_dim(both, width + self.hi * 2 * own, 2 * own, 1)
        sent = lax.dynamic_slice_in_dim(narrow, (1 - self.core) * own, own, 1)
        kept = lax.dynamic_slice_in_dim(narrow, self.core * own, own, 1)
        got = self.to_core(jnp.concatenate([wide, sent], axis=1))
        return jnp.concatenate([wide, got[:, :width]]), jnp.concatenate([kept, got[:, width:]])

    def reduce_regions(self, total):
        rows, width = total.shape[0] // 4, total.shape[1]
        total = total.reshape(2, 2, rows, width)
        sent = lax.dynamic_index_in_dim(total, 1 - self.z0, 1, False).astype(BF16)
        kept = lax.dynamic_index_in_dim(total, self.z0, 1, False)
        kept = kept + self.to_near(sent).astype(F32)
        sent = lax.dynamic_index_in_dim(kept, 1 - self.z1, 0, False).astype(BF16)
        kept = lax.dynamic_index_in_dim(kept, self.z1, 0, False)
        return kept + self.to_far(sent).astype(F32)


def heads_of(a):
    return a.reshape(a.shape[0], a.shape[1] // HS, HS)


def forward(net, x, mod, weights, live):
    qkv, proj, up, down = weights
    shift_attn, scale_attn, gate_attn, shift_mlp, scale_mlp, gate_mlp = (mod[i][None] for i in range(6))
    rows, features = x.shape
    normed, inverse = norm(x)
    hidden = (normed * (1.0 + scale_attn) + shift_attn).astype(BF16)
    width = qkv.shape[2]
    projected = dot(hidden, qkv.reshape(features, 3 * width)).astype(BF16)
    queries, keyvalue = projected[:, :width], projected[:, width:]
    if live is None:
        other = net.to_core(keyvalue)
        bias = None
    else:
        sent = jnp.concatenate(
            [keyvalue, jnp.broadcast_to(live.astype(BF16)[:, None], (rows, 128))], axis=1
        )
        other = net.to_core(sent)
        all_live = jnp.concatenate([live, other[:, 2 * width].astype(F32)])
        bias = all_live[None, None, :] > 0
        other = other[:, : 2 * width]
    keyvalue = jnp.concatenate([keyvalue, other])
    keys, values = keyvalue[:, :width], keyvalue[:, width:]
    scores = jnp.einsum(
        "qhe,khe->hqk", heads_of(queries), heads_of(keys), preferred_element_type=F32
    ) * (1.0 / math.sqrt(HS))
    if bias is not None:
        scores = jnp.where(bias, scores, -1e30)
    exponent = jnp.exp(scores - jnp.max(scores, axis=-1, keepdims=True))
    probs = exponent / jnp.sum(exponent, axis=-1, keepdims=True)
    attended = jnp.einsum(
        "hqk,khe->qhe", probs.astype(BF16), heads_of(values), preferred_element_type=F32
    )
    attended = attended.reshape(rows, width).astype(BF16)
    branch = net.heads_sum(dot(attended, proj))
    residual = x + gate_attn * branch
    normed_mlp, inverse_mlp = norm(residual)
    mlp_input = (normed_mlp * (1.0 + scale_mlp) + shift_mlp).astype(BF16)
    pre_gelu = dot(mlp_input, up)
    activated = jax.nn.gelu(pre_gelu, approximate=True).astype(BF16)
    mlp_out = net.heads_sum(dot(activated, down))
    result = residual + gate_mlp * mlp_out
    saved = dict(
        normed=normed, inverse=inverse, hidden=hidden, queries=queries, keys=keys, values=values,
        probs=probs, attended=attended, branch=branch, normed_mlp=normed_mlp,
        inverse_mlp=inverse_mlp, mlp_input=mlp_input, pre_gelu=pre_gelu, activated=activated,
        mlp_out=mlp_out,
    )
    return result, saved


def backward(net, grad_out, s, mod, weights):
    qkv, proj, up, down = weights
    shift_attn, scale_attn, gate_attn, shift_mlp, scale_mlp, gate_mlp = (mod[i][None] for i in range(6))
    rows, features = grad_out.shape
    width = qkv.shape[2]
    grad_gate_mlp = jnp.sum(grad_out * s["mlp_out"], axis=0)
    grad_mlp = (gate_mlp * grad_out).astype(BF16)
    grad_act = dot(grad_mlp, down, ((1,), (1,)))
    gelu_back = jax.vjp(lambda u: jax.nn.gelu(u, approximate=True), s["pre_gelu"])[1]
    grad_pre = gelu_back(grad_act)[0].astype(BF16)
    grad_input = net.heads_sum(dot(grad_pre, up, ((1,), (1,))))
    grad_scale_mlp = jnp.sum(grad_input * s["normed_mlp"], axis=0)
    grad_shift_mlp = jnp.sum(grad_input, axis=0)
    grad_residual = grad_out + norm_back(
        grad_input * (1.0 + scale_mlp), s["normed_mlp"], s["inverse_mlp"]
    )
    grad_gate_attn = jnp.sum(grad_residual * s["branch"], axis=0)
    grad_branch = (gate_attn * grad_residual).astype(BF16)
    grad_attended = dot(grad_branch, proj, ((1,), (1,))).astype(BF16)

    grad_heads, query_heads = heads_of(grad_attended), heads_of(s["queries"])
    key_heads, value_heads = heads_of(s["keys"]), heads_of(s["values"])
    probs = s["probs"]
    scale = 1.0 / math.sqrt(HS)
    grad_probs = jnp.einsum("qhe,khe->hqk", grad_heads, value_heads, preferred_element_type=F32)
    inner = jnp.sum(probs * grad_probs, axis=-1, keepdims=True)
    grad_scores = (probs * (grad_probs - inner)).astype(BF16)
    grad_keys = jnp.einsum("hqk,qhe->khe", grad_scores, query_heads, preferred_element_type=F32) * scale
    grad_values = jnp.einsum(
        "hqk,qhe->khe", probs.astype(BF16), grad_heads, preferred_element_type=F32
    )
    grad_keyvalue = jnp.concatenate(
        [grad_keys.reshape(2 * rows, width), grad_values.reshape(2 * rows, width)], axis=1
    )
    other = net.to_core(grad_keyvalue[rows:].astype(BF16))
    grad_keyvalue = (grad_keyvalue[:rows] + other.astype(F32)).astype(BF16)
    grad_queries = jnp.einsum("hqk,khe->qhe", grad_scores, key_heads, preferred_element_type=F32) * scale
    grad_projected = jnp.concatenate(
        [grad_queries.reshape(rows, width).astype(BF16), grad_keyvalue], axis=1
    )
    grad_hidden = net.heads_sum(dot(grad_projected, qkv.reshape(features, 3 * width), ((1,), (1,))))
    grad_scale_attn = jnp.sum(grad_hidden * s["normed"], axis=0)
    grad_shift_attn = jnp.sum(grad_hidden, axis=0)
    grad_x = grad_residual + norm_back(grad_hidden * (1.0 + scale_attn), s["normed"], s["inverse"])

    wide, mlp_sel = net.gather_rows(jnp.concatenate([s["activated"]], axis=1), s["mlp_input"])
    grad_wide, grad_mlp_sel = net.gather_rows(grad_pre, grad_mlp)
    mlp_grads = jnp.concatenate(
        [dot(mlp_sel, grad_wide, ((0,), (0,))), dot(grad_mlp_sel, wide, ((0,), (0,)))], axis=1
    )
    ff = up.shape[1]
    mlp_grads = net.reduce_regions(mlp_grads)
    att_all, hidden_sel = net.gather_rows(s["attended"], s["hidden"])
    grad_all, branch_sel = net.gather_rows(grad_projected, grad_branch)
    attn_grads = jnp.concatenate(
        [dot(hidden_sel, grad_all, ((0,), (0,))), dot(branch_sel, att_all, ((0,), (0,)))], axis=1
    )
    attn_grads = net.reduce_regions(attn_grads)
    grads = (
        attn_grads[:, : 3 * width].reshape(-1, 3, width),
        attn_grads[:, 3 * width :].T,
        mlp_grads[:, :ff],
        mlp_grads[:, ff:].T,
    )
    grad_mod = jnp.concatenate(
        [grad_shift_attn, grad_scale_attn, grad_gate_attn, grad_shift_mlp, grad_scale_mlp, grad_gate_mlp]
    )
    return grad_x, grads, grad_mod


def shards(
    net, enc_in, kept_pos, slot_live, condition, mask_token, enc_ada, enc_qkv, enc_proj, enc_up,
    enc_down, dec_ada, dec_qkv, dec_proj, dec_up, dec_down, cotangent,
):
    net.place()
    cap, features = enc_in.shape[1:]
    tokens = cotangent.shape[1]
    assert enc_in.shape[0] == 2
    enc_weights = (enc_qkv, enc_proj, enc_up, enc_down)
    dec_weights = (dec_qkv, dec_proj, dec_up, dec_down)

    code = jnp.where(slot_live > 0, kept_pos, -1).astype(BF16)
    sent = jnp.concatenate([enc_in, jnp.broadcast_to(code[..., None], code.shape + (128,))], axis=2)
    parts = net.spread_images(sent)
    slots = jnp.concatenate(parts)
    x = slots[:, :features].astype(F32)
    code = slots[:, features].astype(F32)
    live = (code >= 0).astype(F32)

    silu = jax.nn.silu(condition.astype(F32)).astype(BF16)
    silu = in_order(silu, net.to_core(silu), net.core).reshape(4, features)
    cols = jnp.concatenate([dot(silu, enc_ada), dot(silu, dec_ada)], axis=1)
    block = enc_ada.shape[1]
    cols = cols.reshape(2, 2, 2 * block)
    got = net.to_near(lax.dynamic_index_in_dim(cols, 1 - net.z0, 1, False))
    cols = in_order(lax.dynamic_index_in_dim(cols, net.z0, 1, False), got, net.z0)
    got = net.to_far(lax.dynamic_index_in_dim(cols, 1 - net.z1, 1, False))
    cols = in_order(lax.dynamic_index_in_dim(cols, net.z1, 1, False), got, net.z1)
    cols = in_order(cols, net.to_heads(cols), net.y)
    cols = jnp.moveaxis(cols, 0, 2).reshape(8, 2, block)
    enc_mod = cols[:, 0].reshape(6, features)
    dec_mod = cols[:, 1].reshape(6, features)

    enc_out, enc_saved = forward(net, x, enc_mod, enc_weights, live)

    positions = jnp.arange(tokens, dtype=jnp.int32).astype(F32)
    codes = code.reshape(2, cap)
    matches = (codes[:, None, :] == positions[None, :, None]).astype(F32)
    uncovered = 1.0 - jnp.sum(matches, axis=2)
    dec_in = jnp.einsum(
        "brc,bcd->brd", matches, enc_out.reshape(2, cap, features), precision=lax.Precision.HIGHEST
    ) + uncovered[:, :, None] * mask_token.astype(F32)
    dec_out, dec_saved = forward(
        net, dec_in.reshape(2 * tokens, features), dec_mod, dec_weights, None
    )
    out = net.collect_images([dec_out[:tokens].astype(BF16), dec_out[tokens:].astype(BF16)])

    grad_out = jnp.concatenate(net.spread_images(cotangent)).astype(F32)
    grad_dec_in, dec_grads, dec_mod_grad = backward(net, grad_out, dec_saved, dec_mod, dec_weights)
    grad_dec_in = grad_dec_in.reshape(2, tokens, features)
    grad_enc_out = jnp.einsum("brc,brd->bcd", matches, grad_dec_in, precision=lax.Precision.HIGHEST)
    mask_part = jnp.sum(uncovered[:, :, None] * grad_dec_in, axis=(0, 1))
    grad_in, enc_grads, enc_mod_grad = backward(
        net, grad_enc_out.reshape(2 * cap, features), enc_saved, enc_mod, enc_weights
    )
    input_grad = net.collect_images([grad_in[:cap], grad_in[cap:]])

    vector = jnp.concatenate([enc_mod_grad, dec_mod_grad, mask_part])
    vector = vector + net.to_core(vector)
    split = 6 * features
    own = features // (net.ndp * 4)
    rows = jnp.concatenate(
        [
            lax.dynamic_index_in_dim(vector[:split].reshape(4, 2, block), net.y, 1, False),
            lax.dynamic_index_in_dim(vector[split : 2 * split].reshape(4, 2, block), net.y, 1, False),
            jnp.moveaxis(vector[2 * split :].reshape(net.ndp, 4, own), 0, 1).reshape(4, -1),
        ],
        axis=1,
    )
    rows = rows.reshape(2, 2, -1)
    got = net.to_near(lax.dynamic_index_in_dim(rows, 1 - net.z0, 1, False))
    rows = in_order(lax.dynamic_index_in_dim(rows, net.z0, 1, False), got, net.z0)
    got = net.to_far(lax.dynamic_index_in_dim(rows, 1 - net.z1, 1, False))
    rows = in_order(lax.dynamic_index_in_dim(rows, net.z1, 1, False), got, net.z1)
    rows = net.gather_hi(rows.reshape(4, -1)).reshape(net.nhi * 4, -1)
    silu_all = net.gather_hi(silu).reshape(net.nhi * 4, features)
    share = features // net.ndp
    silu_own = lax.dynamic_slice_in_dim(silu_all, net.dp * share, share, 1)
    enc_ada_grad = dot(silu_own, rows[:, :block].astype(BF16), ((0,), (0,)))
    dec_ada_grad = dot(silu_own, rows[:, block : 2 * block].astype(BF16), ((0,), (0,)))
    mask_grad = lax.dynamic_slice_in_dim(jnp.sum(rows[:, 2 * block :], axis=0), net.dp * own, own, 0)
    return (out, input_grad, mask_grad, enc_ada_grad) + enc_grads + (dec_ada_grad,) + dec_grads


def solution(mesh):
    net = Net(mesh)
    in_specs = (
        P("dp", "region", None),
        P("dp", "region"),
        P("dp", "region"),
        P("dp", None),
        P(),
    ) + 2 * (
        P(None, ("region", "heads")),
        P(None, None, "heads"),
        P("heads", None),
        P(None, "heads"),
        P("heads", None),
    ) + (P("dp", "region", None),)
    out_specs = (
        P("dp", "region", None),
        P("dp", "region", None),
        P(("dp", "region")),
    ) + 2 * (
        P("dp", ("region", "heads")),
        P(("dp", "region"), None, "heads"),
        P("heads", ("dp", "region")),
        P(("dp", "region"), "heads"),
        P("heads", ("dp", "region")),
    )
    return jax.shard_map(
        lambda *args: shards(net, *args),
        mesh=mesh, in_specs=in_specs, out_specs=out_specs, check_vma=False,
    )
```

```python
import functools
import math

import jax
import jax.numpy as jnp
from jax import lax
from jax.experimental import pallas as pl
from jax.experimental.pallas import tpu as pltpu
from jax.sharding import PartitionSpec as P

HS = 72
SCALE = 1.0 / math.sqrt(HS)
EPSILON = 1e-06
BF16 = jnp.bfloat16
F32 = jnp.float32
VMEM_LIMIT = 28 * 2**20
NT = ((1,), (1,))
TN = ((0,), (0,))


def dot(a, b, dims=((1,), (0,)), **kw):
    return lax.dot_general(a, b, (dims, ((), ())), preferred_element_type=F32, **kw)


class Late:
    def __init__(self, copy, ref):
        self.copy, self.ref, self.waited = copy, ref, False
        copy.start()

    def get(self):
        if not self.waited:
            self.copy.wait()
            self.waited = True
        return self.ref


def here(ref):
    return ref.get() if isinstance(ref, Late) else ref


def call(kernel, outs, *ins, flops=0, scratch=(), late=(), limit=VMEM_LIMIT):
    shapes = [jax.ShapeDtypeStruct(shape, dtype) for shape, dtype in outs]
    moved = sum(math.prod(a.shape) * a.dtype.itemsize for a in list(ins) + shapes)
    fetched = [pltpu.VMEM(ins[i].shape, ins[i].dtype) for i in late]
    semaphores = [pltpu.SemaphoreType.DMA((len(late),))] if late else []

    def body(*refs):
        refs = list(refs)
        own = len(refs) - len(late) - len(semaphores)
        for at, i in enumerate(late):
            refs[i] = Late(pltpu.make_async_copy(refs[i], refs[own + at], refs[-1].at[at]), refs[own + at])
        kernel(*refs[:own])
        for i in late:
            refs[i].get()

    vmem, hbm = pl.BlockSpec(memory_space=pltpu.VMEM), pl.BlockSpec(memory_space=pl.ANY)
    return pl.pallas_call(
        body,
        out_shape=shapes,
        in_specs=[hbm if i in late else vmem for i in range(len(ins))],
        out_specs=[vmem] * len(outs),
        scratch_shapes=list(scratch) + fetched + semaphores,
        compiler_params=pltpu.CompilerParams(vmem_limit_bytes=limit),
        cost_estimate=pl.CostEstimate(flops=flops, bytes_accessed=0, transcendentals=0),
    )(*ins)


def load_kernel(*refs):
    count = len(refs) // 2
    copies = [
        pltpu.make_async_copy(refs[i], refs[count + i], refs[-1].at[i]) for i in range(count)
    ]
    for copy in copies:
        copy.start()
    for copy in copies:
        copy.wait()


def load(anchor, *weights):
    anchor, *weights = tie(anchor, *weights)
    loaded = pl.pallas_call(
        load_kernel,
        out_shape=[jax.ShapeDtypeStruct(w.shape, w.dtype) for w in weights],
        in_specs=[pl.BlockSpec(memory_space=pl.ANY)] * len(weights),
        out_specs=[pl.BlockSpec(memory_space=pltpu.VMEM)] * len(weights),
        scratch_shapes=[pltpu.SemaphoreType.DMA((len(weights),))],
        compiler_params=pltpu.CompilerParams(vmem_limit_bytes=VMEM_LIMIT),
        cost_estimate=pl.CostEstimate(
            flops=3*10**9, bytes_accessed=0, transcendentals=0
        ),
    )(*weights)
    return anchor, *loaded


def tie(*arrays):
    return lax.optimization_barrier(arrays)


def norm(rows):
    mean = jnp.mean(rows, axis=-1, keepdims=True)
    centered = rows - mean
    inverse = lax.rsqrt(jnp.mean(centered * centered, axis=-1, keepdims=True) + EPSILON)
    return centered * inverse, inverse


def norm_back(grad, normed, inverse):
    return inverse * (
        grad
        - jnp.mean(grad, axis=-1, keepdims=True)
        - normed * jnp.mean(grad * normed, axis=-1, keepdims=True)
    )


def padded(width):
    return -(-width // 128) * 128


def side(a):
    more = padded(a.shape[1]) - a.shape[1]
    return jnp.concatenate([a, jnp.zeros((a.shape[0], more), a.dtype)], axis=1) if more else a


def wide(ref):
    return here(ref)[...].astype(F32)


def row(ref, i):
    return ref[i : i + 1, :]


def total(ref, *columns):
    return jnp.sum(ref, axis=0, keepdims=True)


def qkv_rows(x, mod, qkv, hidden_ref, q_ref, kv_ref):
    width = q_ref.shape[1]
    hidden = (norm(x)[0] * (1.0 + row(mod, 1)) + row(mod, 0)).astype(BF16)
    hidden_ref[...] = hidden
    projected = dot(hidden, qkv[...], NT).astype(BF16)
    q_ref[...] = projected[:, :width]
    kv_ref[:, : 2 * width] = projected[:, width:]


def enc_qkv_kernel(first, second, mod, qkv, x_ref, hidden_ref, q_ref, kv_ref):
    features = x_ref.shape[1]
    both = jnp.concatenate([first[...], second[...]])
    x = both[:, :features].astype(F32)
    x_ref[...] = x
    qkv_rows(x, mod, qkv, hidden_ref, q_ref, kv_ref)
    width = q_ref.shape[1]
    kv_ref[:, 2 * width :] = (both[:, features:].astype(F32) >= 0.0).astype(F32).astype(BF16)


def block_end(residual, part, other, mod):
    return residual[...] + row(mod, 5) * (wide(part) + wide(other))


def dec_qkv_kernel(
    residual, part, other, enc_mod, matches, mask, mod, qkv, x_ref, hidden_ref, q_ref, kv_ref
):
    enc_out = block_end(residual, part, other, enc_mod)
    found = matches[...]
    uncovered = 1.0 - jnp.sum(found, axis=1, keepdims=True)
    x = dot(found, enc_out, precision=lax.Precision.HIGHEST) + uncovered * wide(mask)
    x_ref[...] = x
    qkv_rows(x, mod, qkv, hidden_ref, q_ref, kv_ref)


def window(head, width):
    first, last = head * HS, (head + 1) * HS
    start, stop = first // 128 * 128, min(-(-last // 128) * 128, width)
    lanes = lax.broadcasted_iota(jnp.int32, (1, stop - start), 1) + start
    return slice(start, stop), ((lanes >= first) & (lanes < last)).astype(F32)


def probs_of(queries, keys, live):
    scores = dot(keys, queries, NT) * SCALE
    if live is not None:
        scores = jnp.where(live, scores, -1e30)
    exponent = jnp.exp(scores - jnp.max(scores, axis=0, keepdims=True))
    return exponent / jnp.sum(exponent, axis=0, keepdims=True)


def live_of(kv, kv_other, width):
    if kv.shape[1] == 2 * width:
        return None
    own, other = (a[:, 2 * width : 2 * width + 128].astype(F32)[:, :1] for a in (kv, kv_other))
    return jnp.concatenate([own, other]) > 0.5


def attention_kernel(q, kv, kv_other, proj, hidden, *refs):
    width, features = q.shape[1], hidden.shape[1]
    if len(refs) > 3:
        first, second, mod, rows_ref, part_ref, grad_ref, total_ref = refs
        grad_out = jnp.concatenate([first[...], second[...]])
        grad_ref[...] = grad_out
        rows_ref[:, features : 2 * features] = (row(mod, 5) * grad_out.astype(F32)).astype(BF16)
    else:
        rows_ref, part_ref, total_ref = refs
    rows_ref[:, :features] = hidden[...]
    live = live_of(kv, kv_other, width)
    total_ref[...] = jnp.zeros_like(total_ref)
    for head in range(width // HS):
        at, mask = window(head, width)
        beside = slice(width + at.start, width + at.stop)
        queries = (wide(q.at[:, at]) * mask).astype(BF16)
        keys = jnp.concatenate([kv[:, at], kv_other[:, at]])
        values = jnp.concatenate([kv[:, beside], kv_other[:, beside]])
        probs = probs_of(queries, keys, live).astype(BF16)
        total_ref[:, at] += dot(probs, values, TN) * mask
    attended = total_ref[...].astype(BF16)
    rows_ref[:, rows_ref.shape[1] - padded(width) :] = side(attended)
    part_ref[...] = dot(attended, here(proj)[...]).astype(BF16)


def mlp_kernel(x, part, other, mod, up, down, *refs):
    before, (residual_ref, pre_ref, rows_ref, part_ref) = refs[:-4], refs[-4:]
    features = x.shape[1]
    if before:
        rows_ref[:, up.shape[1] + features :] = before[0][...]
    hidden_units = up.shape[1]
    residual = x[...] + row(mod, 2) * (wide(part) + wide(other))
    residual_ref[...] = residual
    mlp_input = (norm(residual)[0] * (1.0 + row(mod, 4)) + row(mod, 3)).astype(BF16)
    rows_ref[:, hidden_units : hidden_units + features] = mlp_input
    pre = dot(mlp_input, up[...])
    pre_ref[...] = pre
    activated = jax.nn.gelu(pre, approximate=True).astype(BF16)
    rows_ref[:, :hidden_units] = activated
    part_ref[...] = dot(activated, down[...]).astype(BF16)


def gelu_slope(u):
    c = math.sqrt(2.0 / math.pi)
    t = jnp.tanh(c * (u + 0.044715 * u * u * u))
    return 0.5 * (1.0 + t) + 0.5 * u * (1.0 - t * t) * c * (1.0 + 3 * 0.044715 * u * u)


def enc_mlp_back_kernel(grad_out, pre, mod, up, down, rows_ref, part_ref):
    hidden_units = up.shape[1]
    grad_mlp = (row(mod, 5) * wide(grad_out)).astype(BF16)
    rows_ref[:, hidden_units:] = grad_mlp
    mlp_back(grad_mlp, pre, up, down, rows_ref, part_ref)


def dec_mlp_back_kernel(attn_rows, pre, up, down, rows_ref, part_ref):
    features = up.shape[0]
    mlp_back(attn_rows[:, features : 2 * features], pre, up, down, rows_ref, part_ref)


def mlp_back(grad_mlp, pre, up, down, rows_ref, part_ref):
    hidden_units = up.shape[1]
    grad_pre = (dot(grad_mlp, down[...], NT) * gelu_slope(here(pre)[...])).astype(BF16)
    rows_ref[:, :hidden_units] = grad_pre
    part_ref[...] = dot(grad_pre, up[...], NT).astype(BF16)


def attention_back_kernel(
    grad_out, part, other, residual, branch, branch_other, mod, proj, q, kv, kv_other,
    grad_residual_ref, grad_branch_ref, dq_ref, dkv_ref, dkv_other_ref, sums_ref,
    dk_ref, dv_ref,
):
    rows, width = dq_ref.shape
    grad_input = wide(part) + wide(other)
    normed, inverse = norm(here(residual)[...])
    sums_ref[0:1, :] = jnp.sum(grad_input, axis=0, keepdims=True)
    sums_ref[1:2, :] = jnp.sum(grad_input * normed, axis=0, keepdims=True)
    grad_residual = wide(grad_out) + norm_back(grad_input * (1.0 + row(mod, 4)), normed, inverse)
    grad_residual_ref[...] = grad_residual
    sums_ref[2:3, :] = jnp.sum(
        grad_residual * (wide(branch) + wide(branch_other)), axis=0, keepdims=True
    )
    grad_branch = (row(mod, 2) * grad_residual).astype(BF16)
    grad_branch_ref[...] = grad_branch
    grad_attended = dot(grad_branch, here(proj)[...], NT).astype(BF16).astype(F32)
    q, kv, kv_other = here(q), here(kv), here(kv_other)

    live = live_of(kv, kv_other, width)
    dk_ref[...] = jnp.zeros_like(dk_ref)
    dv_ref[...] = jnp.zeros_like(dv_ref)
    dq_total = []
    for head in range(width // HS):
        at, mask = window(head, width)
        beside = slice(width + at.start, width + at.stop)
        queries = (wide(q.at[:, at]) * mask).astype(BF16)
        grad_head = (grad_attended[:, at] * mask).astype(BF16)
        keys = jnp.concatenate([kv[:, at], kv_other[:, at]])
        values = jnp.concatenate([kv[:, beside], kv_other[:, beside]])
        probs = probs_of(queries, keys, live)
        grad_probs = dot(values, grad_head, NT)
        inner = jnp.sum(probs * grad_probs, axis=0, keepdims=True)
        grad_scores = (probs * (grad_probs - inner)).astype(BF16)
        dk_ref[:, at] += dot(grad_scores, queries)
        dv_ref[:, at] += dot(probs.astype(BF16), grad_head)
        dq_total.append((at, dot(grad_scores, keys, TN) * (mask * SCALE)))
    for tile in range(0, width, 128):
        stop = min(tile + 128, width)
        terms = [
            part_[:, tile - at.start : stop - at.start]
            for at, part_ in dq_total
            if at.start <= tile and stop <= at.stop
        ]
        dq_ref[:, tile:stop] = functools.reduce(lambda a, b: a + b, terms).astype(BF16)
    dkv_ref[:, :width] = dk_ref[:rows, :] * SCALE
    dkv_ref[:, width:] = dv_ref[:rows, :]
    dkv_other_ref[:, :width] = (dk_ref[rows:, :] * SCALE).astype(BF16)
    dkv_other_ref[:, width:] = dv_ref[rows:, :].astype(BF16)


def qkv_back_kernel(dq, dkv, dkv_other, grad_branch, qkv, rows_ref, part_ref):
    features = grad_branch.shape[1]
    grad_projected = jnp.concatenate(
        [dq[...], (dkv[...] + wide(dkv_other)).astype(BF16)], axis=1
    )
    rows_ref[:, :features] = grad_branch[...]
    rows_ref[:, features:] = side(grad_projected)
    part_ref[...] = dot(grad_projected, here(qkv)[...]).astype(BF16)


def block_back(part, other, grad_residual, x, mod, grad_out, mlp, mlp_other, sums_ref):
    grad_hidden = wide(part) + wide(other)
    normed, inverse = norm(here(x)[...])
    sums_ref[0:1, :] = jnp.sum(grad_hidden, axis=0, keepdims=True)
    sums_ref[1:2, :] = jnp.sum(grad_hidden * normed, axis=0, keepdims=True)
    sums_ref[2:3, :] = jnp.sum(wide(grad_out) * (wide(mlp) + wide(mlp_other)), axis=0, keepdims=True)
    return grad_residual[...] + norm_back(grad_hidden * (1.0 + row(mod, 1)), normed, inverse)


def dec_end_kernel(
    part, other, grad_residual, x, mod, grad_out, mlp, mlp_other, matches, grad_ref, sums_ref
):
    grad_x = block_back(part, other, grad_residual, x, mod, grad_out, mlp, mlp_other, sums_ref)
    found = matches[...]
    uncovered = 1.0 - jnp.sum(found, axis=1, keepdims=True)
    sums_ref[3:4, :] = jnp.sum(uncovered * grad_x, axis=0, keepdims=True)
    grad_ref[...] = dot(found, grad_x, TN, precision=lax.Precision.HIGHEST)


def enc_end_kernel(
    part, other, grad_residual, x, mod, grad_out, mlp, mlp_other, grad_ref, sums_ref
):
    grad_ref[...] = block_back(
        part, other, grad_residual, x, mod, grad_out, mlp, mlp_other, sums_ref
    )
    sums_ref[3:4, :] = jnp.zeros_like(sums_ref[3:4, :])


def out_kernel(residual, part, other, mod, out_ref):
    out_ref[...] = block_end(residual, part, other, mod).astype(BF16)


def weight_grad_kernel(products, *refs):
    count = 1 + max(max(p[0][0], p[1][0]) for p in products)
    bundles, refs = refs[: 4 * count], refs[4 * count :]
    select, sent_ref, kept_ref, *buffers, semaphores = refs
    features = select.shape[1]
    half = sent_ref.shape[0]
    copies = []
    for at, ((narrow, first), (full, start, span)) in enumerate(products):
        for bundle, begin, size, buffer in (
            (narrow, first, features, buffers[2 * at]),
            (full, start, padded(span), buffers[2 * at + 1]),
        ):
            for part in range(4):
                source = bundles[4 * bundle + part]
                rows = source.shape[0]
                copies.append(
                    pltpu.make_async_copy(
                        source.at[:, begin : begin + size],
                        buffer.at[part * rows : (part + 1) * rows, :],
                        semaphores.at[len(copies)],
                    )
                )
                copies[-1].start()
    column = 0
    for at, (_, (_, _, span)) in enumerate(products):
        features_all, rows_all = buffers[2 * at], buffers[2 * at + 1]
        for copy in copies[8 * at : 8 * at + 4]:
            copy.wait()
        chosen = dot(select[...], features_all[...], NT).astype(BF16)
        for copy in copies[8 * at + 4 : 8 * at + 8]:
            copy.wait()
        sent_ref[:, column : column + span] = dot(chosen[:half], rows_all[:, :span]).astype(BF16)
        kept_ref[:, column : column + span] = dot(chosen[half:], rows_all[:, :span])
        column += span


def halve_kernel(kept, got, sent_ref, kept_ref):
    rows = kept_ref.shape[0]
    sums = kept[...] + wide(got)
    kept_ref[...] = sums[:rows]
    sent_ref[...] = sums[rows:].astype(BF16)


def finish_kernel(kept, got, *outs):
    at = 0
    for out in outs:
        for part in range(out.shape[0] if len(out.shape) == 3 else 1):
            span = out.shape[-1]
            place = (part,) if len(out.shape) == 3 else ()
            out[place + (...,)] = kept[:, at : at + span] + wide(got.at[:, at : at + span])
            at += span


def in_order(mine, other, bit):
    return jnp.stack([jnp.where(bit == 0, mine, other), jnp.where(bit == 0, other, mine)])


class Net:
    def __init__(self, mesh):
        self.ndp, self.nreg, self.nhead = (mesh.shape[a] for a in ("dp", "region", "heads"))
        assert self.nreg == 4 and self.nhead == 2 and self.ndp % 2 == 0
        self.nhi = self.ndp // 2
        self.core_perm = [(d, d ^ 1) for d in range(self.ndp)]
        self.near = [(z, z ^ 1) for z in range(4)]
        self.far = [(z, z ^ 2) for z in range(4)]
        self.spread = [
            [
                (d * 4 + r, (d - d % 2 + r // 2) * 4 + 2 * (d % 2) + (r + j) % 2)
                for d in range(self.ndp)
                for r in range(4)
            ]
            for j in range(2)
        ]

    def place(self):
        self.dp = lax.axis_index("dp")
        self.hi, self.core = self.dp // 2, self.dp % 2
        self.z = lax.axis_index("region")
        self.z1, self.z0 = self.z // 2, self.z % 2
        self.y = lax.axis_index("heads")

    def to_core(self, a):
        return lax.ppermute(a, "dp", self.core_perm)

    def to_near(self, a):
        return lax.ppermute(a, "region", self.near)

    def to_far(self, a):
        return lax.ppermute(a, "region", self.far)

    def to_heads(self, a):
        return lax.ppermute(a, "heads", [(0, 1), (1, 0)])

    def to_hi(self, a):
        return lax.ppermute(a, "dp", [(d, d ^ 2) for d in range(self.ndp)])

    def hi_groups(self):
        return [[c + 2 * h for h in range(self.nhi)] for c in range(2)]

    def gather_hi(self, a):
        if self.nhi == 1:
            return a[None]
        if self.nhi == 2:
            return in_order(a, self.to_hi(a), self.hi)
        return lax.all_gather(a, "dp", axis_index_groups=self.hi_groups(), axis=0)

    def spread_images(self, a):
        even = self.z0 == 0
        first, second = jnp.where(even, a[0], a[1]), jnp.where(even, a[1], a[0])
        return [
            lax.ppermute(part, ("dp", "region"), perm)
            for part, perm in zip((first, second), self.spread)
        ]

    def collect_parts(self, parts):
        return [
            lax.ppermute(part, ("dp", "region"), [(t, s) for s, t in perm])
            for part, perm in zip(parts, self.spread)
        ]

    def collected(self, back):
        even = self.z0 == 0
        return jnp.stack([jnp.where(even, back[0], back[1]), jnp.where(even, back[1], back[0])])

    def gather(self, rows):
        if self.nhi == 2:
            return rows, self.to_near(rows)
        if self.nhi > 2:
            rows = lax.all_gather(
                rows, "dp", axis_index_groups=self.hi_groups(), axis=0, tiled=True
            )
        half = rows.shape[0] // 2
        return rows[:half], rows[half:]

    def selection(self, features):
        own = features // (self.ndp * 4)
        step = jnp.arange(4 * own)
        if self.nhi == 2:
            block = jnp.array([8, 10, 0, 2])[step // own]
        else:
            block = jnp.array([1, 3, 0, 2])[step // own]
        feature = ((self.dp * 4 + self.z) ^ block) * own + step % own
        return (feature[:, None] == jnp.arange(features)[None, :]).astype(BF16)

    def first_half(self, sent):
        return self.to_hi(sent) if self.nhi == 2 else self.to_near(sent)


def weight_grads(products, bundles, select):
    half = select.shape[0] // 2
    features = select.shape[1]
    width = sum(full[2] for _, full in products)
    rows = 4 * bundles[0][0].shape[0]
    operands = [a for bundle in bundles for a in bundle]
    vmem, hbm = pl.BlockSpec(memory_space=pltpu.VMEM), pl.BlockSpec(memory_space=pl.ANY)
    buffers = [
        pltpu.VMEM((rows, padded(span)), BF16)
        for _, (_, _, size) in products
        for span in (features, size)
    ]
    held = sum(2 * math.prod(buffer.shape) for buffer in buffers) + 16 * 2**20
    return pl.pallas_call(
        functools.partial(weight_grad_kernel, products),
        out_shape=[
            jax.ShapeDtypeStruct((half, width), BF16), jax.ShapeDtypeStruct((half, width), F32)
        ],
        in_specs=[hbm] * len(operands) + [vmem],
        out_specs=[vmem] * 2,
        scratch_shapes=buffers + [pltpu.SemaphoreType.DMA((8 * len(products),))],
        compiler_params=pltpu.CompilerParams(vmem_limit_bytes=max(VMEM_LIMIT, held)),
        cost_estimate=pl.CostEstimate(
            flops=4 * half * rows * (width + len(products) * features),
            bytes_accessed=0,
            transcendentals=0,
        ),
    )(*operands, select)


def finish(kept, got, *shapes):
    return call(finish_kernel, [(shape, F32) for shape in shapes], kept, got)


def halve(kept, got):
    rows, width = kept.shape
    return call(halve_kernel, [((rows // 2, width), BF16), ((rows // 2, width), F32)], kept, got)


def shards(
    net, enc_in, kept_pos, slot_live, condition, mask_token, enc_ada, enc_qkv, enc_proj, enc_up,
    enc_down, dec_ada, dec_qkv, dec_proj, dec_up, dec_down, cotangent,
):
    net.place()
    cap, features = enc_in.shape[1:]
    tokens = cotangent.shape[1]
    assert enc_in.shape[0] == 2
    width, units = enc_proj.shape[0], enc_up.shape[1]
    select = net.selection(features)
    enc_qkv, dec_qkv = (
        jnp.transpose(a, (1, 2, 0)).reshape(3 * width, features) for a in (enc_qkv, dec_qkv)
    )

    code = jnp.where(slot_live > 0, kept_pos, -1).astype(BF16)
    sent = jnp.concatenate([enc_in, jnp.broadcast_to(code[..., None], code.shape + (128,))], axis=2)
    slots = net.spread_images(sent)
    code = jnp.concatenate([part[:, features] for part in slots]).astype(jnp.int32)
    place = jnp.arange(2 * tokens)
    matches = (place[:, None] // tokens == jnp.arange(2 * cap)[None, :] // cap) & (
        code[None, :] == place[:, None] % tokens
    )
    matches = matches.astype(F32)

    silu = jax.nn.silu(condition.astype(F32)).astype(BF16)
    silu = in_order(silu, net.to_core(silu), net.core).reshape(4, features)
    cols = jnp.concatenate([dot(silu, enc_ada), dot(silu, dec_ada)], axis=1)
    block = enc_ada.shape[1]
    cols = cols.reshape(2, 2, 2 * block)
    got = net.to_near(lax.dynamic_index_in_dim(cols, 1 - net.z0, 1, False))
    cols = in_order(lax.dynamic_index_in_dim(cols, net.z0, 1, False), got, net.z0)
    got = net.to_far(lax.dynamic_index_in_dim(cols, 1 - net.z1, 1, False))
    cols = in_order(lax.dynamic_index_in_dim(cols, net.z1, 1, False), got, net.z1)
    cols = in_order(cols, net.to_heads(cols), net.y)
    cols = jnp.moveaxis(cols, 0, 2).reshape(8, 2, block)
    enc_mod = cols[:, 0].reshape(6, features)
    dec_mod = cols[:, 1].reshape(6, features)

    def attention(q, kv, kv_other, proj, hidden, *more):
        rows = q.shape[0]
        beside = [((rows, features), BF16)] if more else []
        return call(
            attention_kernel,
            [((rows, padded(width) + (1 + len(beside)) * features), BF16), ((rows, features), BF16)] + beside,
            q, kv, kv_other, proj, hidden, *more, late=(3,),
            flops=2 * rows * width * (features + 4 * rows), scratch=[pltpu.VMEM((rows, width), F32)],
        )

    def mlp(x, part, other, mod, up, down, *more):
        rows = x.shape[0]
        beside = units + features + sum(a.shape[1] for a in more)
        return call(
            mlp_kernel,
            [((rows, features), F32), ((rows, units), F32), ((rows, beside), BF16), ((rows, features), BF16)],
            x, part, other, mod, up, down, *more, flops=4 * rows * features * units,
        )

    def attention_back(grad_out, part, other, s, mod, proj):
        rows = grad_out.shape[0]
        return call(
            attention_back_kernel,
            [
                ((rows, features), F32), ((rows, features), BF16), ((rows, width), BF16),
                ((rows, 2 * width), F32), ((rows, 2 * width), BF16), ((3, features), F32),
            ],
            grad_out, part, other, s["residual"], s["branch"], s["branch_other"], mod, proj,
            s["q"], s["kv"], s["kv_other"], late=(3, 4, 5, 8, 9, 10),
            flops=2 * rows * width * (features + 10 * rows),
            scratch=[pltpu.VMEM((2 * rows, width), F32)] * 2,
        )

    def qkv_back(dq, dkv, dkv_other, grad_branch, qkv):
        rows = dq.shape[0]
        return call(
            qkv_back_kernel, [((rows, padded(3 * width) + features), BF16), ((rows, features), BF16)],
            dq, dkv, dkv_other, grad_branch, qkv, flops=6 * rows * features * width,
        )

    def end(kernel, grad_residual, part, other, grad_out, s, mod, *extra):
        return call(
            kernel, [((2 * cap, features), F32), ((4, features), F32)],
            part, other, grad_residual, s["x"], mod, grad_out, s["mlp"], s["mlp_other"], *extra,
            late=(3, 6, 7),
        )

    rows = 2 * cap
    x, hidden, q, kv = call(
        enc_qkv_kernel,
        [((rows, features), F32), ((rows, features), BF16), ((rows, width), BF16), ((rows, 2 * width + 128), BF16)],
        *slots, enc_mod, enc_qkv, flops=6 * rows * features * width,
    )
    kv_other = net.to_core(kv)
    enc_attn_rows, branch = attention(q, kv, kv_other, enc_proj, hidden)
    branch, up, down = load(branch, enc_up, enc_down)
    branch_other = net.to_heads(branch)
    residual, pre, enc_rows, mlp_part = mlp(
        x, branch, branch_other, enc_mod, up, down, enc_attn_rows
    )
    mlp_part, qkv = load(mlp_part, dec_qkv)
    mlp_other = net.to_heads(mlp_part)
    enc = dict(
        x=x, q=q, kv=kv, kv_other=kv_other, branch=branch, branch_other=branch_other,
        residual=residual, pre=pre, mlp=mlp_part, mlp_other=mlp_other,
    )
    enc_rows, enc_rows_near = net.gather(enc_rows)
    cotangent, _ = tie(cotangent, branch)
    grad_parts = net.spread_images(cotangent)

    rows = 2 * tokens
    mlp_other, *grad_parts = tie(mlp_other, *grad_parts)
    x, hidden, q, kv = call(
        dec_qkv_kernel,
        [((rows, features), F32), ((rows, features), BF16), ((rows, width), BF16), ((rows, 2 * width), BF16)],
        residual, mlp_part, mlp_other, enc_mod, matches, mask_token[None], dec_mod, qkv,
        flops=6 * rows * features * width,
    )
    kv_other = net.to_core(kv)
    attn_rows, branch, grad_out = attention(q, kv, kv_other, dec_proj, hidden, *grad_parts, dec_mod)
    branch, up, down = load(branch, dec_up, dec_down)
    branch_other = net.to_heads(branch)
    own_rows = attn_rows
    attn_rows, attn_rows_near = net.gather(attn_rows)
    residual, pre, mlp_rows, mlp_part = mlp(x, branch, branch_other, dec_mod, up, down)
    mlp_other = net.to_heads(mlp_part)
    dec = dict(
        x=x, q=q, kv=kv, kv_other=kv_other, branch=branch, branch_other=branch_other,
        residual=residual, pre=pre, mlp=mlp_part, mlp_other=mlp_other,
    )
    mlp_rows, mlp_rows_near = net.gather(mlp_rows)

    grad_rows, part = call(
        dec_mlp_back_kernel, [((rows, units), BF16), ((rows, features), BF16)],
        own_rows, pre, up, down, flops=4 * rows * features * units,
    )
    part, qkv, proj = load(part, dec_qkv, dec_proj)
    other = net.to_heads(part)
    (dec_out,) = call(
        out_kernel, [((rows, features), BF16)], residual, mlp_part, mlp_other, dec_mod
    )
    out_parts = net.collect_parts([dec_out[:tokens], dec_out[tokens:]])
    grad_rows, grad_rows_near = net.gather(grad_rows)
    other, attn_rows_near, enc_rows_near = tie(other, attn_rows_near, enc_rows_near)
    attn_rows = attn_rows, attn_rows_near, net.to_core(attn_rows), net.to_core(attn_rows_near)
    grad_residual, grad_branch, dq, dkv, dkv_other, dec_sums = attention_back(
        grad_out, part, other, dec, dec_mod, proj
    )
    dkv_other, *attn_rows = tie(net.to_core(dkv_other), *attn_rows)
    enc_rows = enc_rows, enc_rows_near, net.to_core(enc_rows), net.to_core(enc_rows_near)
    grad_attn_rows, part = qkv_back(dq, dkv, dkv_other, grad_branch, qkv)
    part, up, down = load(part, enc_up, enc_down)
    other = net.to_heads(part)
    grad_attn_rows, grad_attn_rows_near = net.gather(grad_attn_rows)
    other, mlp_rows_near, *rest = tie(other, mlp_rows_near, *out_parts, *enc_rows)
    out_parts, enc_rows = rest[:2], rest[2:]
    mlp_rows = mlp_rows, mlp_rows_near, net.to_core(mlp_rows), net.to_core(mlp_rows_near)
    grad_enc, dec_more = end(
        dec_end_kernel, grad_residual, part, other, grad_out, dec, dec_mod, matches
    )

    rows = 2 * cap
    grad_out, *mlp_rows = tie(grad_enc, *mlp_rows)
    enc_grad_rows, part = call(
        enc_mlp_back_kernel, [((rows, units + features), BF16), ((rows, features), BF16)],
        grad_out, enc["pre"], enc_mod, up, down, flops=4 * rows * features * units, late=(1,),
    )
    part, qkv, proj = load(part, enc_qkv, enc_proj)
    other = net.to_heads(part)
    enc_grad_rows, enc_grad_rows_near = net.gather(enc_grad_rows)
    down_sent, down_kept = weight_grads(
        (((0, features), (1, 0, units)),), (attn_rows, mlp_rows), select
    )
    down_got = net.first_half(down_sent)
    other, grad_rows_near, down_sent = tie(other, grad_rows_near, down_sent)
    grad_rows = grad_rows, grad_rows_near, net.to_core(grad_rows), net.to_core(grad_rows_near)
    grad_residual, grad_branch, dq, dkv, dkv_other, enc_sums = attention_back(
        grad_out, part, other, enc, enc_mod, proj
    )
    dkv_other, *grad_rows = tie(net.to_core(dkv_other), *grad_rows)
    enc_grad_attn_rows, part = qkv_back(dq, dkv, dkv_other, grad_branch, qkv)
    other = net.to_heads(part)
    enc_grad_attn_rows, enc_grad_attn_rows_near = net.gather(enc_grad_attn_rows)
    up_sent, up_kept = weight_grads(
        (((0, units), (1, 0, units)),), (mlp_rows, grad_rows), select
    )
    up_got = net.first_half(up_sent)
    other, up_sent, down_got, grad_attn_rows_near = tie(other, up_sent, down_got, grad_attn_rows_near)
    grad_attn_rows = (
        grad_attn_rows, grad_attn_rows_near, net.to_core(grad_attn_rows), net.to_core(grad_attn_rows_near)
    )
    down_sent, down_kept = halve(down_kept, down_got)
    down_got = net.to_far(down_sent)
    grad_in, enc_more = end(enc_end_kernel, grad_residual, part, other, grad_out, enc, enc_mod)

    grad_in, down_sent, *grad_attn_rows = tie(grad_in, down_sent, *grad_attn_rows)
    attn_sent, attn_kept = weight_grads(
        (((0, 0), (1, features, 3 * width)), ((1, 0), (0, 2 * features, width))),
        (attn_rows, grad_attn_rows), select,
    )
    attn_got = net.first_half(attn_sent)
    attn_sent, enc_grad_rows_near = tie(attn_sent, enc_grad_rows_near)
    enc_grad_rows = (
        enc_grad_rows, enc_grad_rows_near, net.to_core(enc_grad_rows), net.to_core(enc_grad_rows_near)
    )
    enc_up_sent, enc_up_kept = weight_grads(
        (((0, units), (1, 0, units)),), (enc_rows, enc_grad_rows), select
    )
    enc_up_got = net.first_half(enc_up_sent)
    up_got, enc_up_sent = tie(up_got, enc_up_sent)
    up_sent, up_kept = halve(up_kept, up_got)
    up_got = net.to_far(up_sent)
    up_sent, *enc_grad_rows = tie(up_sent, *enc_grad_rows)
    enc_down_sent, enc_down_kept = weight_grads(
        (((1, units), (0, 0, units)),), (enc_rows, enc_grad_rows), select
    )
    enc_down_got = net.first_half(enc_down_sent)
    enc_down_sent, enc_grad_attn_rows_near = tie(enc_down_sent, enc_grad_attn_rows_near)
    enc_grad_attn_rows = (
        enc_grad_attn_rows, enc_grad_attn_rows_near,
        net.to_core(enc_grad_attn_rows), net.to_core(enc_grad_attn_rows_near),
    )
    enc_attn_sent, enc_attn_kept = weight_grads(
        (
            ((0, units + features), (1, features, 3 * width)),
            ((1, 0), (0, units + 2 * features, width)),
        ),
        (enc_rows, enc_grad_attn_rows), select,
    )
    enc_attn_got = net.first_half(enc_attn_sent)
    attn_got, enc_attn_sent = tie(attn_got, enc_attn_sent)
    attn_sent, attn_kept = halve(attn_kept, attn_got)
    attn_got = net.to_far(attn_sent)
    enc_up_sent, enc_up_kept = halve(enc_up_kept, enc_up_got)
    enc_up_got = net.to_far(enc_up_sent)
    enc_down_sent, enc_down_kept = halve(enc_down_kept, enc_down_got)
    enc_down_got = net.to_far(enc_down_sent)
    enc_attn_sent, enc_attn_kept = halve(enc_attn_kept, enc_attn_got)
    enc_attn_got = net.to_far(enc_attn_sent)

    out = net.collected(out_parts)
    input_grad = net.collected(net.collect_parts([grad_in[:cap], grad_in[cap:]]))
    mask_part = dec_more[3]

    enc_mod_grad, dec_mod_grad = (
        jnp.concatenate([more[0], more[1], sums[2], sums[0], sums[1], more[2]])
        for more, sums in ((enc_more, enc_sums), (dec_more, dec_sums))
    )

    share = features // (net.ndp * 4)

    def attn_outs(kept, got):
        qkv_grad, proj_grad = finish(kept, got, (3, share, width), (share, width))
        return jnp.transpose(qkv_grad, (1, 0, 2)), proj_grad.T

    def mlp_outs(up_kept, up_got, down_kept, down_got):
        return (
            finish(up_kept, up_got, (share, units))[0], finish(down_kept, down_got, (share, units))[0].T
        )

    enc_grads = attn_outs(enc_attn_kept, enc_attn_got) + mlp_outs(
        enc_up_kept, enc_up_got, enc_down_kept, enc_down_got
    )
    dec_grads = attn_outs(attn_kept, attn_got) + mlp_outs(up_kept, up_got, down_kept, down_got)

    vector = jnp.concatenate([enc_mod_grad, dec_mod_grad, mask_part])
    vector = vector + net.to_core(vector)
    split = 6 * features
    own = features // (net.ndp * 4)
    rows = jnp.concatenate(
        [
            lax.dynamic_index_in_dim(vector[:split].reshape(4, 2, block), net.y, 1, False),
            lax.dynamic_index_in_dim(vector[split : 2 * split].reshape(4, 2, block), net.y, 1, False),
            jnp.moveaxis(vector[2 * split :].reshape(net.ndp, 4, own), 0, 1).reshape(4, -1),
        ],
        axis=1,
    )
    rows = rows.reshape(2, 2, -1)
    got = net.to_near(lax.dynamic_index_in_dim(rows, 1 - net.z0, 1, False))
    rows = in_order(lax.dynamic_index_in_dim(rows, net.z0, 1, False), got, net.z0)
    got = net.to_far(lax.dynamic_index_in_dim(rows, 1 - net.z1, 1, False))
    rows = in_order(lax.dynamic_index_in_dim(rows, net.z1, 1, False), got, net.z1)
    rows = net.gather_hi(rows.reshape(4, -1)).reshape(net.nhi * 4, -1)
    silu_all = net.gather_hi(silu).reshape(net.nhi * 4, features)
    share = features // net.ndp
    silu_own = lax.dynamic_slice_in_dim(silu_all, net.dp * share, share, 1)
    enc_ada_grad = dot(silu_own, rows[:, :block].astype(BF16), TN)
    dec_ada_grad = dot(silu_own, rows[:, block : 2 * block].astype(BF16), TN)
    mask_grad = lax.dynamic_slice_in_dim(jnp.sum(rows[:, 2 * block :], axis=0), net.dp * own, own, 0)
    return (out, input_grad, mask_grad, enc_ada_grad) + enc_grads + (dec_ada_grad,) + dec_grads

def solution(mesh):
    net = Net(mesh)
    in_specs = (
        P("dp", "region", None),
        P("dp", "region"),
        P("dp", "region"),
        P("dp", None),
        P(),
    ) + 2 * (
        P(None, ("region", "heads")),
        P(None, None, "heads"),
        P("heads", None),
        P(None, "heads"),
        P("heads", None),
    ) + (P("dp", "region", None),)
    out_specs = (
        P("dp", "region", None),
        P("dp", "region", None),
        P(("dp", "region")),
    ) + 2 * (
        P("dp", ("region", "heads")),
        P(("dp", "region"), None, "heads"),
        P("heads", ("dp", "region")),
        P(("dp", "region"), "heads"),
        P("heads", ("dp", "region")),
    )
    return jax.shard_map(
        lambda *args: shards(net, *args),
        mesh=mesh, in_specs=in_specs, out_specs=out_specs, check_vma=False,
    )
```

```python
import functools
import math

import jax
import jax.numpy as jnp
from jax import lax
from jax.experimental import pallas as pl
from jax.experimental.pallas import tpu as pltpu
from jax.sharding import PartitionSpec as P

HS = 72
SCALE = 1.0 / math.sqrt(HS)
EPSILON = 1e-06
BF16 = jnp.bfloat16
F32 = jnp.float32
VMEM_LIMIT = 16 * 2**20
NT = ((1,), (1,))
TN = ((0,), (0,))


def dot(a, b, dims=((1,), (0,)), **kw):
    return lax.dot_general(a, b, (dims, ((), ())), preferred_element_type=F32, **kw)


class Late:
    def __init__(self, copy, ref):
        self.copy, self.ref, self.waited = copy, ref, False
        copy.start()

    def get(self):
        if not self.waited:
            self.copy.wait()
            self.waited = True
        return self.ref


def here(ref):
    return ref.get() if isinstance(ref, Late) else ref


def call(kernel, outs, *ins, flops=0, scratch=(), late=(), limit=VMEM_LIMIT):
    shapes = [jax.ShapeDtypeStruct(shape, dtype) for shape, dtype in outs]
    fetched = [pltpu.VMEM(ins[i].shape, ins[i].dtype) for i in late]
    semaphores = [pltpu.SemaphoreType.DMA((len(late),))] if late else []

    def body(*refs):
        refs = list(refs)
        own = len(refs) - len(late) - len(semaphores)
        for at, i in enumerate(late):
            refs[i] = Late(pltpu.make_async_copy(refs[i], refs[own + at], refs[-1].at[at]), refs[own + at])
        kernel(*refs[:own])
        for i in late:
            refs[i].get()

    vmem, hbm = pl.BlockSpec(memory_space=pltpu.VMEM), pl.BlockSpec(memory_space=pl.ANY)
    ins = [in_hbm(a) if i in late else a for i, a in enumerate(ins)]
    return pl.pallas_call(
        body,
        out_shape=shapes,
        in_specs=[hbm if i in late else vmem for i in range(len(ins))],
        out_specs=[vmem] * len(outs),
        name=kernel.__name__,
        scratch_shapes=list(scratch) + fetched + semaphores,
        compiler_params=pltpu.CompilerParams(vmem_limit_bytes=limit),
        cost_estimate=pl.CostEstimate(flops=flops, bytes_accessed=0, transcendentals=0),
    )(*ins)


def in_hbm(a):
    return pltpu.with_memory_space_constraint(a, pltpu.HBM)


def load_kernel(*refs):
    count = len(refs) // 2
    copies = [
        pltpu.make_async_copy(refs[i], refs[count + i], refs[-1].at[i]) for i in range(count)
    ]
    for copy in copies:
        copy.start()
    for copy in copies:
        copy.wait()


def load(anchor, *weights, beside=()):
    anchor, *weights = tie(anchor, *weights, *beside)
    weights, beside = weights[: len(weights) - len(beside)], weights[len(weights) - len(beside) :]
    weights = [in_hbm(w) for w in weights]
    loaded = pl.pallas_call(
        load_kernel,
        out_shape=[jax.ShapeDtypeStruct(w.shape, w.dtype) for w in weights],
        in_specs=[pl.BlockSpec(memory_space=pl.ANY)] * len(weights),
        out_specs=[pl.BlockSpec(memory_space=pltpu.VMEM)] * len(weights),
        name="load",
        scratch_shapes=[pltpu.SemaphoreType.DMA((len(weights),))],
        compiler_params=pltpu.CompilerParams(vmem_limit_bytes=VMEM_LIMIT),
        cost_estimate=pl.CostEstimate(
            flops=3 * 10**9, bytes_accessed=0, transcendentals=0
        ),
    )(*weights)
    return anchor, *loaded, *beside


def tie(*arrays):
    return lax.optimization_barrier(arrays)


def norm(rows):
    mean = jnp.mean(rows, axis=-1, keepdims=True)
    centered = rows - mean
    inverse = lax.rsqrt(jnp.mean(centered * centered, axis=-1, keepdims=True) + EPSILON)
    return centered * inverse, inverse


def norm_back(grad, normed, inverse):
    return inverse * (
        grad
        - jnp.mean(grad, axis=-1, keepdims=True)
        - normed * jnp.mean(grad * normed, axis=-1, keepdims=True)
    )


def padded(width):
    return -(-width // 128) * 128


def side(a):
    more = padded(a.shape[1]) - a.shape[1]
    return jnp.concatenate([a, jnp.zeros((a.shape[0], more), a.dtype)], axis=1) if more else a


def wide(ref):
    return here(ref)[...].astype(F32)


def row(ref, i):
    return ref[i : i + 1, :]


def total(ref, *columns):
    return jnp.sum(ref, axis=0, keepdims=True)


def qkv_rows(x, mod, qkv, hidden_ref, q_ref, kv_ref):
    width = q_ref.shape[1]
    hidden = (norm(x)[0] * (1.0 + row(mod, 1)) + row(mod, 0)).astype(BF16)
    hidden_ref[...] = hidden
    projected = dot(hidden, here(qkv)[...], NT).astype(BF16)
    q_ref[...] = projected[:, :width]
    kv_ref[:, : 2 * width] = projected[:, width:]


def enc_qkv_kernel(first, second, mod, qkv, x_ref, hidden_ref, q_ref, kv_ref):
    features = x_ref.shape[1]
    both = jnp.concatenate([first[...], second[...]])
    x = both[:, :features].astype(F32)
    x_ref[...] = x
    qkv_rows(x, mod, qkv, hidden_ref, q_ref, kv_ref)
    width = q_ref.shape[1]
    kv_ref[:, 2 * width :] = (both[:, features:].astype(F32) >= 0.0).astype(F32).astype(BF16)


def block_end(residual, part, other, mod):
    return residual[...] + row(mod, 5) * (wide(part) + wide(other))


def dec_qkv_kernel(
    residual, part, other, enc_mod, matches, mask, mod, qkv, x_ref, hidden_ref, q_ref, kv_ref
):
    enc_out = block_end(residual, part, other, enc_mod)
    found = matches[...]
    uncovered = 1.0 - jnp.sum(found, axis=1, keepdims=True)
    x = dot(found, enc_out, precision=lax.Precision.HIGHEST) + uncovered * wide(mask)
    x_ref[...] = x
    qkv_rows(x, mod, qkv, hidden_ref, q_ref, kv_ref)


def window(head, width):
    first, last = head * HS, (head + 1) * HS
    start, stop = first // 128 * 128, min(-(-last // 128) * 128, width)
    lanes = lax.broadcasted_iota(jnp.int32, (1, stop - start), 1) + start
    return slice(start, stop), ((lanes >= first) & (lanes < last)).astype(F32)


def probs_of(queries, keys, live):
    scores = dot(keys, queries, NT) * SCALE
    if live is not None:
        scores = jnp.where(live, scores, -1e30)
    exponent = jnp.exp(scores - jnp.max(scores, axis=0, keepdims=True))
    return exponent / jnp.sum(exponent, axis=0, keepdims=True)


def live_of(kv, kv_other, width):
    if kv.shape[1] == 2 * width:
        return None
    own, other = (a[:, 2 * width : 2 * width + 128].astype(F32)[:, :1] for a in (kv, kv_other))
    return jnp.concatenate([own, other]) > 0.5


def attention_kernel(q, kv, kv_other, proj, hidden, *refs):
    width, features = q.shape[1], hidden.shape[1]
    if len(refs) > 3:
        first, second, mod, rows_ref, part_ref, grad_ref, total_ref = refs
        grad_out = jnp.concatenate([first[...], second[...]])
        grad_ref[...] = grad_out
        rows_ref[:, features : 2 * features] = (row(mod, 5) * grad_out.astype(F32)).astype(BF16)
    else:
        rows_ref, part_ref, total_ref = refs
    rows_ref[:, :features] = hidden[...]
    live = live_of(kv, kv_other, width)
    total_ref[...] = jnp.zeros_like(total_ref)
    for head in range(width // HS):
        at, mask = window(head, width)
        beside = slice(width + at.start, width + at.stop)
        queries = (wide(q.at[:, at]) * mask).astype(BF16)
        keys = jnp.concatenate([kv[:, at], kv_other[:, at]])
        values = jnp.concatenate([kv[:, beside], kv_other[:, beside]])
        probs = probs_of(queries, keys, live).astype(BF16)
        total_ref[:, at] += dot(probs, values, TN) * mask
    attended = total_ref[...].astype(BF16)
    rows_ref[:, rows_ref.shape[1] - padded(width) :] = side(attended)
    part_ref[...] = dot(attended, here(proj)[...]).astype(BF16)


def mlp_kernel(x, part, other, mod, up, down, *refs):
    before, (residual_ref, pre_ref, rows_ref, part_ref) = refs[:-4], refs[-4:]
    features = x.shape[1]
    if before:
        rows_ref[:, up.shape[1] + features :] = before[0][...]
    hidden_units = up.shape[1]
    residual = x[...] + row(mod, 2) * (wide(part) + wide(other))
    residual_ref[...] = residual
    mlp_input = (norm(residual)[0] * (1.0 + row(mod, 4)) + row(mod, 3)).astype(BF16)
    rows_ref[:, hidden_units : hidden_units + features] = mlp_input
    pre = dot(mlp_input, up[...])
    pre_ref[...] = pre
    activated = jax.nn.gelu(pre, approximate=True).astype(BF16)
    rows_ref[:, :hidden_units] = activated
    part_ref[...] = dot(activated, down[...]).astype(BF16)


def gelu_slope(u):
    c = math.sqrt(2.0 / math.pi)
    t = jnp.tanh(c * (u + 0.044715 * u * u * u))
    return 0.5 * (1.0 + t) + 0.5 * u * (1.0 - t * t) * c * (1.0 + 3 * 0.044715 * u * u)


def enc_mlp_back_kernel(grad_out, pre, mod, up, down, rows_ref, part_ref):
    hidden_units = up.shape[1]
    grad_mlp = (row(mod, 5) * wide(grad_out)).astype(BF16)
    rows_ref[:, hidden_units:] = grad_mlp
    mlp_back(grad_mlp, pre, up, down, rows_ref, part_ref)


def dec_mlp_back_kernel(attn_rows, pre, up, down, rows_ref, part_ref):
    features = up.shape[0]
    mlp_back(attn_rows[:, features : 2 * features], pre, up, down, rows_ref, part_ref)


def mlp_back(grad_mlp, pre, up, down, rows_ref, part_ref):
    hidden_units = up.shape[1]
    grad_pre = (dot(grad_mlp, down[...], NT) * gelu_slope(here(pre)[...])).astype(BF16)
    rows_ref[:, :hidden_units] = grad_pre
    part_ref[...] = dot(grad_pre, up[...], NT).astype(BF16)


def attention_back_kernel(
    grad_out, part, other, residual, branch, branch_other, mod, proj, q, kv, kv_other,
    grad_residual_ref, grad_branch_ref, dq_ref, dkv_ref, dkv_other_ref, sums_ref,
    dk_ref, dv_ref,
):
    rows, width = dq_ref.shape
    grad_input = wide(part) + wide(other)
    normed, inverse = norm(here(residual)[...])
    sums_ref[0:1, :] = jnp.sum(grad_input, axis=0, keepdims=True)
    sums_ref[1:2, :] = jnp.sum(grad_input * normed, axis=0, keepdims=True)
    grad_residual = wide(grad_out) + norm_back(grad_input * (1.0 + row(mod, 4)), normed, inverse)
    grad_residual_ref[...] = grad_residual
    sums_ref[2:3, :] = jnp.sum(
        grad_residual * (wide(branch) + wide(branch_other)), axis=0, keepdims=True
    )
    grad_branch = (row(mod, 2) * grad_residual).astype(BF16)
    grad_branch_ref[...] = grad_branch
    grad_attended = dot(grad_branch, here(proj)[...], NT).astype(BF16).astype(F32)
    q, kv, kv_other = here(q), here(kv), here(kv_other)

    live = live_of(kv, kv_other, width)
    dk_ref[...] = jnp.zeros_like(dk_ref)
    dv_ref[...] = jnp.zeros_like(dv_ref)
    dq_total = []
    for head in range(width // HS):
        at, mask = window(head, width)
        beside = slice(width + at.start, width + at.stop)
        queries = (wide(q.at[:, at]) * mask).astype(BF16)
        grad_head = (grad_attended[:, at] * mask).astype(BF16)
        keys = jnp.concatenate([kv[:, at], kv_other[:, at]])
        values = jnp.concatenate([kv[:, beside], kv_other[:, beside]])
        probs = probs_of(queries, keys, live)
        grad_probs = dot(values, grad_head, NT)
        inner = jnp.sum(probs * grad_probs, axis=0, keepdims=True)
        grad_scores = (probs * (grad_probs - inner)).astype(BF16)
        dk_ref[:, at] += dot(grad_scores, queries)
        dv_ref[:, at] += dot(probs.astype(BF16), grad_head)
        dq_total.append((at, dot(grad_scores, keys, TN) * (mask * SCALE)))
    for tile in range(0, width, 128):
        stop = min(tile + 128, width)
        terms = [
            part_[:, tile - at.start : stop - at.start]
            for at, part_ in dq_total
            if at.start <= tile and stop <= at.stop
        ]
        dq_ref[:, tile:stop] = functools.reduce(lambda a, b: a + b, terms).astype(BF16)
    dkv_ref[:, :width] = dk_ref[:rows, :] * SCALE
    dkv_ref[:, width:] = dv_ref[:rows, :]
    dkv_other_ref[:, :width] = (dk_ref[rows:, :] * SCALE).astype(BF16)
    dkv_other_ref[:, width:] = dv_ref[rows:, :].astype(BF16)


def qkv_back_kernel(dq, dkv, dkv_other, grad_branch, qkv, rows_ref, part_ref):
    features = grad_branch.shape[1]
    grad_projected = jnp.concatenate(
        [dq[...], (dkv[...] + wide(dkv_other)).astype(BF16)], axis=1
    )
    rows_ref[:, :features] = grad_branch[...]
    rows_ref[:, features:] = side(grad_projected)
    part_ref[...] = dot(grad_projected, here(qkv)[...]).astype(BF16)


def block_back(part, other, grad_residual, x, mod, sums_ref):
    grad_hidden = wide(part) + wide(other)
    normed, inverse = norm(here(x)[...])
    sums_ref[0:1, :] = jnp.sum(grad_hidden, axis=0, keepdims=True)
    sums_ref[1:2, :] = jnp.sum(grad_hidden * normed, axis=0, keepdims=True)
    return here(grad_residual)[...] + norm_back(grad_hidden * (1.0 + row(mod, 1)), normed, inverse)


def dec_end_kernel(part, other, grad_residual, x, mod, matches, grad_ref, sums_ref):
    grad_x = block_back(part, other, grad_residual, x, mod, sums_ref)
    found = matches[...]
    uncovered = 1.0 - jnp.sum(found, axis=1, keepdims=True)
    sums_ref[2:3, :] = jnp.sum(uncovered * grad_x, axis=0, keepdims=True)
    grad_ref[...] = dot(found, grad_x, TN, precision=lax.Precision.HIGHEST)


def enc_end_kernel(
    part, other, grad_residual, x, mod, grad_out, mlp, mlp_other, grad_ref, sums_ref
):
    grad_ref[...] = block_back(part, other, grad_residual, x, mod, sums_ref).astype(BF16)
    sums_ref[2:3, :] = jnp.sum(wide(grad_out) * (wide(mlp) + wide(mlp_other)), axis=0, keepdims=True)


def out_kernel(residual, part, other, mod, grad_out, out_ref, sums_ref):
    out_ref[...] = block_end(here(residual), here(part), other, mod).astype(BF16)
    sums_ref[...] = jnp.sum(wide(grad_out) * (wide(part) + wide(other)), axis=0, keepdims=True)


def weight_grad_kernel(products, *refs):
    count = 1 + max(max(p[0][0], p[1][0]) for p in products)
    bundles, refs = refs[: 4 * count], refs[4 * count :]
    select, sent_ref, kept_ref, *buffers, semaphores = refs
    features = select.shape[1]
    half = sent_ref.shape[0]
    copies = []
    for at, ((narrow, first), (full, start, span)) in enumerate(products):
        for bundle, begin, size, buffer in (
            (narrow, first, features, buffers[2 * at]),
            (full, start, padded(span), buffers[2 * at + 1]),
        ):
            for part in range(4):
                source = bundles[4 * bundle + part]
                rows = source.shape[0]
                copies.append(
                    pltpu.make_async_copy(
                        source.at[:, begin : begin + size],
                        buffer.at[part * rows : (part + 1) * rows, :],
                        semaphores.at[len(copies)],
                    )
                )
                copies[-1].start()
    column = 0
    for at, (_, (_, _, span)) in enumerate(products):
        features_all, rows_all = buffers[2 * at], buffers[2 * at + 1]
        for copy in copies[8 * at : 8 * at + 4]:
            copy.wait()
        chosen = dot(select[...], features_all[...], NT).astype(BF16)
        for copy in copies[8 * at + 4 : 8 * at + 8]:
            copy.wait()
        sent_ref[:, column : column + span] = dot(chosen[:half], rows_all[:, :span]).astype(BF16)
        kept_ref[:, column : column + span] = dot(chosen[half:], rows_all[:, :span])
        column += span


def halve_kernel(kept, got, sent_ref, kept_ref):
    rows = kept_ref.shape[0]
    sums = here(kept)[...] + wide(got)
    kept_ref[...] = sums[:rows]
    sent_ref[...] = sums[rows:].astype(BF16)


def finish_kernel(kept, got, *outs):
    kept = here(kept)
    at = 0
    for out in outs:
        for part in range(out.shape[0] if len(out.shape) == 3 else 1):
            span = out.shape[-1]
            place = (part,) if len(out.shape) == 3 else ()
            out[place + (...,)] = kept[:, at : at + span] + wide(got.at[:, at : at + span])
            at += span


def in_order(mine, other, bit):
    return jnp.stack([jnp.where(bit == 0, mine, other), jnp.where(bit == 0, other, mine)])


class Net:
    def __init__(self, mesh):
        self.ndp, self.nreg, self.nhead = (mesh.shape[a] for a in ("dp", "region", "heads"))
        assert self.nreg == 4 and self.nhead == 2 and self.ndp % 2 == 0
        self.nhi = self.ndp // 2
        self.core_perm = [(d, d ^ 1) for d in range(self.ndp)]
        self.near = [(z, z ^ 1) for z in range(4)]
        self.far = [(z, z ^ 2) for z in range(4)]
        self.spread = [
            [
                (d * 4 + r, (d - d % 2 + r // 2) * 4 + 2 * (d % 2) + (r + j) % 2)
                for d in range(self.ndp)
                for r in range(4)
            ]
            for j in range(2)
        ]

    def place(self):
        self.dp = lax.axis_index("dp")
        self.hi, self.core = self.dp // 2, self.dp % 2
        self.z = lax.axis_index("region")
        self.z1, self.z0 = self.z // 2, self.z % 2
        self.y = lax.axis_index("heads")

    def to_core(self, a):
        with jax.named_scope("core"):
            return lax.ppermute(a, "dp", self.core_perm)

    def to_near(self, a):
        with jax.named_scope("near"):
            return lax.ppermute(a, "region", self.near)

    def to_far(self, a):
        with jax.named_scope("far"):
            return lax.ppermute(a, "region", self.far)

    def to_heads(self, a):
        with jax.named_scope("heads"):
            return lax.ppermute(a, "heads", [(0, 1), (1, 0)])

    def to_hi(self, a):
        with jax.named_scope("hi"):
            return lax.ppermute(a, "dp", [(d, d ^ 2) for d in range(self.ndp)])

    def hi_groups(self):
        return [[c + 2 * h for h in range(self.nhi)] for c in range(2)]

    def gather_hi(self, a):
        if self.nhi == 1:
            return a[None]
        if self.nhi == 2:
            return in_order(a, self.to_hi(a), self.hi)
        return lax.all_gather(a, "dp", axis_index_groups=self.hi_groups(), axis=0)

    def spread_images(self, a):
        even = self.z0 == 0
        first, second = jnp.where(even, a[0], a[1]), jnp.where(even, a[1], a[0])
        with jax.named_scope("spread"):
          return [
            lax.ppermute(part, ("dp", "region"), perm)
            for part, perm in zip((first, second), self.spread)
        ]

    def collect_parts(self, parts):
        with jax.named_scope("collect"):
          return [
            lax.ppermute(part, ("dp", "region"), [(t, s) for s, t in perm])
            for part, perm in zip(parts, self.spread)
        ]

    def collected(self, back):
        even = self.z0 == 0
        return jnp.stack([jnp.where(even, back[0], back[1]), jnp.where(even, back[1], back[0])])

    def gather(self, rows, along_dp):
        if not along_dp:
            return rows, self.to_near(rows)
        if self.nhi == 2:
            return rows, self.to_hi(rows)
        if self.nhi > 2:
            rows = lax.all_gather(
                rows, "dp", axis_index_groups=self.hi_groups(), axis=0, tiled=True
            )
        half = rows.shape[0] // 2
        return rows[:half], rows[half:]

    def selection(self, features, along_dp):
        own = features // (self.ndp * 4)
        step = jnp.arange(4 * own)
        block = jnp.array([1, 3, 0, 2] if along_dp else [8, 10, 0, 2])[step // own]
        feature = ((self.dp * 4 + self.z) ^ block) * own + step % own
        return (feature[:, None] == jnp.arange(features)[None, :]).astype(BF16)

    def first_half(self, sent, along_dp):
        return self.to_near(sent) if along_dp else self.to_hi(sent)


def weight_grads(products, bundles, select):
    half = select.shape[0] // 2
    features = select.shape[1]
    width = sum(full[2] for _, full in products)
    rows = 4 * bundles[0][0].shape[0]
    operands = [in_hbm(a) for bundle in bundles for a in bundle]
    vmem, hbm = pl.BlockSpec(memory_space=pltpu.VMEM), pl.BlockSpec(memory_space=pl.ANY)
    buffers = [
        pltpu.VMEM((rows, padded(span)), BF16)
        for _, (_, _, size) in products
        for span in (features, size)
    ]
    held = sum(2 * math.prod(buffer.shape) for buffer in buffers) + 16 * 2**20
    return pl.pallas_call(
        functools.partial(weight_grad_kernel, products),
        out_shape=[
            jax.ShapeDtypeStruct((half, width), BF16), jax.ShapeDtypeStruct((half, width), F32)
        ],
        in_specs=[hbm] * len(operands) + [vmem],
        out_specs=[vmem] * 2,
        name="weight_grads",
        scratch_shapes=buffers + [pltpu.SemaphoreType.DMA((8 * len(products),))],
        compiler_params=pltpu.CompilerParams(vmem_limit_bytes=max(VMEM_LIMIT, held)),
        cost_estimate=pl.CostEstimate(
            flops=0,
            bytes_accessed=0,
            transcendentals=0,
        ),
    )(*operands, select)


def finish(kept, got, *shapes):
    return call(finish_kernel, [(shape, F32) for shape in shapes], kept, got)


def halve(kept, got):
    rows, width = kept.shape
    return call(halve_kernel, [((rows // 2, width), BF16), ((rows // 2, width), F32)], kept, got)


def shards(
    net, enc_in, kept_pos, slot_live, condition, mask_token, enc_ada, enc_qkv, enc_proj, enc_up,
    enc_down, dec_ada, dec_qkv, dec_proj, dec_up, dec_down, cotangent,
):
    net.place()
    cap, features = enc_in.shape[1:]
    tokens = cotangent.shape[1]
    assert enc_in.shape[0] == 2
    width, units = enc_proj.shape[0], enc_up.shape[1]
    dec_way, enc_way = True, net.nhi != 2
    dec_select, enc_select = net.selection(features, dec_way), net.selection(features, enc_way)
    enc_qkv, dec_qkv = (
        jnp.transpose(a, (1, 2, 0)).reshape(3 * width, features) for a in (enc_qkv, dec_qkv)
    )

    code = jnp.where(slot_live > 0, kept_pos, -1).astype(BF16)
    sent = jnp.concatenate([enc_in, jnp.broadcast_to(code[..., None], code.shape + (128,))], axis=2)
    slots = net.spread_images(sent)
    code = jnp.concatenate([part[:, features] for part in slots]).astype(jnp.int32)
    place = jnp.arange(2 * tokens)
    matches = (place[:, None] // tokens == jnp.arange(2 * cap)[None, :] // cap) & (
        code[None, :] == place[:, None] % tokens
    )
    matches = matches.astype(F32)

    silu = jax.nn.silu(condition.astype(F32)).astype(BF16)
    silu = in_order(silu, net.to_core(silu), net.core).reshape(4, features)
    cols = jnp.concatenate([dot(silu, enc_ada), dot(silu, dec_ada)], axis=1)
    block = enc_ada.shape[1]
    cols = cols.reshape(2, 2, 2 * block)
    got = net.to_near(lax.dynamic_index_in_dim(cols, 1 - net.z0, 1, False))
    got, *slots = tie(got, *slots)
    cols = in_order(lax.dynamic_index_in_dim(cols, net.z0, 1, False), got, net.z0)
    got = net.to_far(lax.dynamic_index_in_dim(cols, 1 - net.z1, 1, False))
    cols = in_order(lax.dynamic_index_in_dim(cols, net.z1, 1, False), got, net.z1)
    cols = in_order(cols, net.to_heads(cols), net.y)
    cols = jnp.moveaxis(cols, 0, 2).reshape(8, 2, block)
    enc_mod = cols[:, 0].reshape(6, features)
    dec_mod = cols[:, 1].reshape(6, features)

    def attention(q, kv, kv_other, proj, hidden, *more):
        rows = q.shape[0]
        beside = [((rows, features), BF16)] if more else []
        return call(
            attention_kernel,
            [((rows, padded(width) + (1 + len(beside)) * features), BF16), ((rows, features), BF16)] + beside,
            q, kv, kv_other, proj, hidden, *more,
            scratch=[pltpu.VMEM((rows, width), F32)],
        )

    def mlp(x, part, other, mod, up, down, *more):
        rows = x.shape[0]
        beside = units + features + sum(a.shape[1] for a in more)
        return call(
            mlp_kernel,
            [((rows, features), F32), ((rows, units), F32), ((rows, beside), BF16), ((rows, features), BF16)],
            x, part, other, mod, up, down, *more,
        )

    def attention_back(grad_out, part, other, s, mod, proj):
        rows = grad_out.shape[0]
        return call(
            attention_back_kernel,
            [
                ((rows, features), F32), ((rows, features), BF16), ((rows, width), BF16),
                ((rows, 2 * width), F32), ((rows, 2 * width), BF16), ((3, features), F32),
            ],
            grad_out, part, other, s["residual"], s["branch"], s["branch_other"], mod, proj,
            s["q"], s["kv"], s["kv_other"], late=(3, 4, 5, 8, 9, 10),
            scratch=[pltpu.VMEM((2 * rows, width), F32)] * 2,
        )

    def qkv_back(dq, dkv, dkv_other, grad_branch, qkv):
        rows = dq.shape[0]
        return call(
            qkv_back_kernel, [((rows, padded(3 * width) + features), BF16), ((rows, features), BF16)],
            dq, dkv, dkv_other, grad_branch, qkv,
        )

    rows = 2 * cap
    x, hidden, q, kv = call(
        enc_qkv_kernel,
        [((rows, features), F32), ((rows, features), BF16), ((rows, width), BF16), ((rows, 2 * width + 128), BF16)],
        *slots, enc_mod, enc_qkv, late=(3,),
    )
    cotangent, kv = tie(cotangent, kv)
    kv_other = net.to_core(kv)
    grad_parts = net.spread_images(cotangent)
    enc_attn_rows, branch = attention(q, kv, kv_other, enc_proj, hidden)
    branch, up, down = load(branch, enc_up, enc_down)
    branch_other = net.to_heads(branch)
    residual, pre, enc_rows, mlp_part = mlp(
        x, branch, branch_other, enc_mod, up, down, enc_attn_rows
    )
    mlp_part, qkv = load(mlp_part, dec_qkv)
    mlp_other = net.to_heads(mlp_part)
    enc = dict(
        x=x, q=q, kv=kv, kv_other=kv_other, branch=branch, branch_other=branch_other,
        residual=residual, pre=pre, mlp=mlp_part, mlp_other=mlp_other,
    )
    enc_rows, enc_rows_far = net.gather(enc_rows, enc_way)
    mlp_other, *grad_parts = tie(mlp_other, *grad_parts)

    rows = 2 * tokens
    x, hidden, q, kv = call(
        dec_qkv_kernel,
        [((rows, features), F32), ((rows, features), BF16), ((rows, width), BF16), ((rows, 2 * width), BF16)],
        residual, mlp_part, mlp_other, enc_mod, matches, mask_token[None], dec_mod, qkv,
    )
    kv_other = net.to_core(kv)
    attn_rows, branch, grad_out = attention(q, kv, kv_other, dec_proj, hidden, *grad_parts, dec_mod)
    branch, up, down = load(branch, dec_up, dec_down)
    branch_other = net.to_heads(branch)
    own_rows = attn_rows
    attn_rows, attn_rows_far = net.gather(attn_rows, dec_way)
    residual, pre, mlp_rows, mlp_part = mlp(x, branch, branch_other, dec_mod, up, down)
    dec = dict(
        x=x, q=q, kv=kv, kv_other=kv_other, branch=branch, branch_other=branch_other,
        residual=residual, pre=pre,
    )
    mlp_rows, mlp_rows_far = net.gather(mlp_rows, dec_way)

    mlp_other = net.to_heads(mlp_part)
    pre, enc_rows_far = tie(pre, enc_rows_far)
    grad_rows, part = call(
        dec_mlp_back_kernel, [((rows, units), BF16), ((rows, features), BF16)],
        own_rows, pre, up, down,
    )
    part, mlp_other = tie(part, mlp_other)
    part, proj = load(part, dec_proj)
    other = net.to_heads(part)
    grad_rows, grad_rows_far = net.gather(grad_rows, dec_way)
    other, attn_rows_far = tie(other, attn_rows_far)
    attn_rows = attn_rows, attn_rows_far, net.to_core(attn_rows), net.to_core(attn_rows_far)
    dec_out, dec_gate = call(
        out_kernel, [((rows, features), BF16), ((1, features), F32)],
        residual, mlp_part, mlp_other, dec_mod, grad_out, late=(0, 1, 4),
    )
    out_parts = net.collect_parts([dec_out[:tokens], dec_out[tokens:]])
    grad_residual, grad_branch, dq, dkv, dkv_other, dec_sums = attention_back(
        grad_out, part, other, dec, dec_mod, proj
    )
    dkv_other, qkv = load(dkv_other, dec_qkv)
    dkv_other, mlp_rows_far, *rest = tie(
        net.to_core(dkv_other), mlp_rows_far, *attn_rows, *out_parts
    )
    attn_rows, out_parts = rest[:4], rest[4:]
    mlp_rows = mlp_rows, mlp_rows_far, net.to_core(mlp_rows), net.to_core(mlp_rows_far)
    enc_rows = enc_rows, enc_rows_far, net.to_core(enc_rows), net.to_core(enc_rows_far)
    grad_attn_rows, part = qkv_back(dq, dkv, dkv_other, grad_branch, qkv)
    part, up, down = load(part, enc_up, enc_down)
    other = net.to_heads(part)
    grad_attn_rows, grad_attn_rows_far = net.gather(grad_attn_rows, dec_way)
    down_sent, down_kept = weight_grads(
        (((0, features), (1, 0, units)),), (attn_rows, mlp_rows), dec_select
    )
    down_got = net.first_half(down_sent, dec_way)
    other, down_sent = tie(other, down_sent)
    grad_enc, dec_more = call(
        dec_end_kernel, [((2 * cap, features), F32), ((3, features), F32)],
        part, other, grad_residual, dec["x"], dec_mod, matches, late=(2, 3),
    )

    rows = 2 * cap
    grad_out = grad_enc
    enc_grad_rows, part = call(
        enc_mlp_back_kernel, [((rows, units + features), BF16), ((rows, features), BF16)],
        grad_out, enc["pre"], enc_mod, up, down, late=(1,),
    )
    part, grad_rows_far = tie(part, grad_rows_far)
    grad_rows = grad_rows, grad_rows_far, net.to_core(grad_rows), net.to_core(grad_rows_far)
    part, proj = load(part, enc_proj)
    other = net.to_heads(part)
    enc_grad_rows, enc_grad_rows_far = net.gather(enc_grad_rows, enc_way)
    up_sent, up_kept = weight_grads(
        (((0, units), (1, 0, units)),), (mlp_rows, grad_rows), dec_select
    )
    up_got = net.first_half(up_sent, dec_way)
    other, up_sent, down_got, *enc_rows = tie(other, up_sent, down_got, *enc_rows)
    down_sent, down_kept = halve(down_kept, down_got)
    down_got = net.to_far(down_sent)
    grad_residual, grad_branch, dq, dkv, dkv_other, enc_sums = attention_back(
        grad_out, part, other, enc, enc_mod, proj
    )
    dkv_other, qkv = load(dkv_other, enc_qkv)
    dkv_other, down_sent, enc_grad_rows_far, grad_attn_rows_far = tie(
        net.to_core(dkv_other), down_sent, enc_grad_rows_far, grad_attn_rows_far
    )
    grad_attn_rows = (
        grad_attn_rows, grad_attn_rows_far, net.to_core(grad_attn_rows), net.to_core(grad_attn_rows_far)
    )
    enc_grad_rows = (
        enc_grad_rows, enc_grad_rows_far, net.to_core(enc_grad_rows), net.to_core(enc_grad_rows_far)
    )
    enc_grad_attn_rows, part = qkv_back(dq, dkv, dkv_other, grad_branch, qkv)
    other = net.to_heads(part)
    enc_grad_attn_rows, enc_grad_attn_rows_far = net.gather(enc_grad_attn_rows, enc_way)
    attn_sent, attn_kept = weight_grads(
        (((0, 0), (1, features, 3 * width)), ((1, 0), (0, 2 * features, width))),
        (attn_rows, grad_attn_rows), dec_select,
    )
    attn_got = net.first_half(attn_sent, dec_way)
    other, attn_sent, up_got, down_got, *enc_grad_rows = tie(
        other, attn_sent, up_got, down_got, *enc_grad_rows
    )
    grad_in, enc_more = call(
        enc_end_kernel, [((2 * cap, features), BF16), ((3, features), F32)],
        part, other, grad_residual, enc["x"], enc_mod, grad_out, enc["mlp"], enc["mlp_other"],
        late=(2, 3, 6, 7),
    )

    grad_in, up_got = tie(grad_in, up_got)
    up_sent, up_kept = halve(up_kept, up_got)
    up_got = net.to_far(up_sent)
    up_sent, *enc_grad_rows = tie(up_sent, *enc_grad_rows)
    enc_up_sent, enc_up_kept = weight_grads(
        (((0, units), (1, 0, units)),), (enc_rows, enc_grad_rows), enc_select
    )
    enc_up_got = net.first_half(enc_up_sent, enc_way)
    enc_up_sent, *enc_grad_rows = tie(enc_up_sent, *enc_grad_rows)
    enc_down_sent, enc_down_kept = weight_grads(
        (((1, units), (0, 0, units)),), (enc_rows, enc_grad_rows), enc_select
    )
    enc_down_got = net.first_half(enc_down_sent, enc_way)
    enc_down_sent, enc_grad_attn_rows_far, attn_got = tie(
        enc_down_sent, enc_grad_attn_rows_far, attn_got
    )
    enc_grad_attn_rows = (
        enc_grad_attn_rows, enc_grad_attn_rows_far,
        net.to_core(enc_grad_attn_rows), net.to_core(enc_grad_attn_rows_far),
    )
    attn_sent, attn_kept = halve(attn_kept, attn_got)
    attn_sent, down_got = tie(attn_sent, down_got)
    attn_got = net.to_far(attn_sent)
    enc_attn_sent, enc_attn_kept = weight_grads(
        (
            ((0, units + features), (1, features, 3 * width)),
            ((1, 0), (0, units + 2 * features, width)),
        ),
        (enc_rows, enc_grad_attn_rows), enc_select,
    )
    enc_attn_got = net.first_half(enc_attn_sent, enc_way)
    enc_up_got, enc_attn_sent = tie(enc_up_got, enc_attn_sent)
    enc_up_sent, enc_up_kept = halve(enc_up_kept, enc_up_got)
    enc_up_sent, up_got = tie(enc_up_sent, up_got)
    enc_up_got = net.to_far(enc_up_sent)
    grad_in, enc_sums, enc_more, enc_up_sent = tie(grad_in, enc_sums, enc_more, enc_up_sent)
    grad_in_parts = net.collect_parts([grad_in[:cap], grad_in[cap:]])
    enc_down_sent, enc_down_kept = halve(enc_down_kept, enc_down_got)
    enc_down_sent, attn_got = tie(enc_down_sent, attn_got)
    enc_down_got = net.to_far(enc_down_sent)
    enc_attn_sent, enc_attn_kept = halve(enc_attn_kept, enc_attn_got)
    enc_attn_sent, enc_up_got, *grad_in_parts = tie(enc_attn_sent, enc_up_got, *grad_in_parts)
    enc_attn_got = net.to_far(enc_attn_sent)

    out = net.collected(out_parts)
    input_grad = net.collected(grad_in_parts).astype(F32)
    mask_part = dec_more[2]

    enc_mod_grad, dec_mod_grad = (
        jnp.concatenate([more[0], more[1], sums[2], sums[0], sums[1], gate])
        for more, sums, gate in ((enc_more, enc_sums, enc_more[2]), (dec_more, dec_sums, dec_gate[0]))
    )

    share = features // (net.ndp * 4)

    def attn_outs(kept, got):
        qkv_grad, proj_grad = finish(kept, got, (3, share, width), (share, width))
        return jnp.transpose(qkv_grad, (1, 0, 2)), proj_grad.T

    def mlp_outs(up_kept, up_got, down_kept, down_got):
        return (
            finish(up_kept, up_got, (share, units))[0], finish(down_kept, down_got, (share, units))[0].T
        )

    enc_grads = attn_outs(enc_attn_kept, enc_attn_got) + mlp_outs(
        enc_up_kept, enc_up_got, enc_down_kept, enc_down_got
    )
    dec_grads = attn_outs(attn_kept, attn_got) + mlp_outs(up_kept, up_got, down_kept, down_got)

    vector = jnp.concatenate([enc_mod_grad, dec_mod_grad, mask_part])
    vector = vector + net.to_core(vector)
    split = 6 * features
    own = features // (net.ndp * 4)
    rows = jnp.concatenate(
        [
            lax.dynamic_index_in_dim(vector[:split].reshape(4, 2, block), net.y, 1, False),
            lax.dynamic_index_in_dim(vector[split : 2 * split].reshape(4, 2, block), net.y, 1, False),
            jnp.moveaxis(vector[2 * split :].reshape(net.ndp, 4, own), 0, 1).reshape(4, -1),
        ],
        axis=1,
    )
    rows = rows.reshape(2, 2, -1)
    got = net.to_near(lax.dynamic_index_in_dim(rows, 1 - net.z0, 1, False))
    rows = in_order(lax.dynamic_index_in_dim(rows, net.z0, 1, False), got, net.z0)
    got = net.to_far(lax.dynamic_index_in_dim(rows, 1 - net.z1, 1, False))
    rows = in_order(lax.dynamic_index_in_dim(rows, net.z1, 1, False), got, net.z1)
    rows = net.gather_hi(rows.reshape(4, -1)).reshape(net.nhi * 4, -1)
    silu_all = net.gather_hi(silu).reshape(net.nhi * 4, features)
    share = features // net.ndp
    silu_own = lax.dynamic_slice_in_dim(silu_all, net.dp * share, share, 1)
    enc_ada_grad = dot(silu_own, rows[:, :block].astype(BF16), TN)
    dec_ada_grad = dot(silu_own, rows[:, block : 2 * block].astype(BF16), TN)
    mask_grad = lax.dynamic_slice_in_dim(jnp.sum(rows[:, 2 * block :], axis=0), net.dp * own, own, 0)
    return (out, input_grad, mask_grad, enc_ada_grad) + enc_grads + (dec_ada_grad,) + dec_grads

def solution(mesh):
    net = Net(mesh)
    in_specs = (
        P("dp", "region", None),
        P("dp", "region"),
        P("dp", "region"),
        P("dp", None),
        P(),
    ) + 2 * (
        P(None, ("region", "heads")),
        P(None, None, "heads"),
        P("heads", None),
        P(None, "heads"),
        P("heads", None),
    ) + (P("dp", "region", None),)
    out_specs = (
        P("dp", "region", None),
        P("dp", "region", None),
        P(("dp", "region")),
    ) + 2 * (
        P("dp", ("region", "heads")),
        P(("dp", "region"), None, "heads"),
        P("heads", ("dp", "region")),
        P(("dp", "region"), "heads"),
        P("heads", ("dp", "region")),
    )
    return jax.shard_map(
        lambda *args: shards(net, *args),
        mesh=mesh, in_specs=in_specs, out_specs=out_specs, check_vma=False,
    )
```

```python
import functools
import math

import jax
import jax.numpy as jnp
from jax import lax
from jax.experimental import pallas as pl
from jax.experimental.pallas import tpu as pltpu
from jax.sharding import PartitionSpec as P

HS = 72
SCALE = 1.0 / math.sqrt(HS)
EPSILON = 1e-06
BF16 = jnp.bfloat16
F32 = jnp.float32
VMEM_LIMIT = 16 * 2**20
LOAD_CHUNKS = 4
NT = ((1,), (1,))
TN = ((0,), (0,))


def dot(a, b, dims=((1,), (0,)), **kw):
    return lax.dot_general(a, b, (dims, ((), ())), preferred_element_type=F32, **kw)


class Late:
    def __init__(self, copy, ref):
        self.copy, self.ref, self.waited = copy, ref, False
        copy.start()

    def get(self):
        if not self.waited:
            self.copy.wait()
            self.waited = True
        return self.ref


def here(ref):
    return ref.get() if isinstance(ref, Late) else ref


def call(kernel, outs, *ins, scratch=(), late=(), after=()):
    shapes = [jax.ShapeDtypeStruct(shape, dtype) for shape, dtype in outs]
    fetched = [pltpu.VMEM(ins[i].shape, ins[i].dtype) for i in late]
    semaphores = [pltpu.SemaphoreType.DMA((len(late),))] if late else []

    def body(*refs):
        refs = list(refs)
        own = len(refs) - len(late) - len(semaphores)
        for at, i in enumerate(late):
            refs[i] = Late(pltpu.make_async_copy(refs[i], refs[own + at], refs[-1].at[at]), refs[own + at])
        kernel(*refs[: len(ins)], *refs[len(ins) + len(after) : own])
        for i in late:
            refs[i].get()

    vmem, hbm = pl.BlockSpec(memory_space=pltpu.VMEM), pl.BlockSpec(memory_space=pl.ANY)
    ins = [in_hbm(a) if i in late else a for i, a in enumerate(ins)]
    return pl.pallas_call(
        body,
        out_shape=shapes,
        in_specs=[hbm if i in late else vmem for i in range(len(ins))] + [hbm] * len(after),
        out_specs=[vmem] * len(outs),
        name=kernel.__name__,
        scratch_shapes=list(scratch) + fetched + semaphores,
        compiler_params=pltpu.CompilerParams(vmem_limit_bytes=VMEM_LIMIT),
        cost_estimate=pl.CostEstimate(flops=0, bytes_accessed=0, transcendentals=0),
    )(*ins, *after)


def in_hbm(a):
    return pltpu.with_memory_space_constraint(a, pltpu.HBM)


def load_kernel(*refs):
    count = len(refs) // 2
    copies = []
    for source, target in zip(refs[:count], refs[count : 2 * count]):
        rows = source.shape[0]
        chunk = -(-rows // LOAD_CHUNKS // 16) * 16
        for start in range(0, rows, chunk):
            part = pl.ds(start, min(chunk, rows - start))
            copies.append(
                pltpu.make_async_copy(source.at[part], target.at[part], refs[-1].at[len(copies)])
            )
            copies[-1].start()
    for copy in copies:
        copy.wait()


def load(anchor, *weights, beside=()):
    anchor, *weights = tie(anchor, *weights, *beside)
    weights, beside = weights[: len(weights) - len(beside)], weights[len(weights) - len(beside) :]
    weights = [in_hbm(w) for w in weights]
    loaded = pl.pallas_call(
        load_kernel,
        out_shape=[jax.ShapeDtypeStruct(w.shape, w.dtype) for w in weights],
        in_specs=[pl.BlockSpec(memory_space=pl.ANY)] * len(weights),
        out_specs=[pl.BlockSpec(memory_space=pltpu.VMEM)] * len(weights),
        name="load",
        scratch_shapes=[pltpu.SemaphoreType.DMA((LOAD_CHUNKS * len(weights),))],
        compiler_params=pltpu.CompilerParams(vmem_limit_bytes=VMEM_LIMIT),
        cost_estimate=pl.CostEstimate(
            flops=0, bytes_accessed=0, transcendentals=0
        ),
    )(*weights)
    return anchor, *loaded, *beside


def tie(*arrays):
    return lax.optimization_barrier(arrays)


def norm(rows):
    mean = jnp.mean(rows, axis=-1, keepdims=True)
    centered = rows - mean
    inverse = lax.rsqrt(jnp.mean(centered * centered, axis=-1, keepdims=True) + EPSILON)
    return centered * inverse, inverse


def norm_back(grad, normed, inverse):
    return inverse * (
        grad
        - jnp.mean(grad, axis=-1, keepdims=True)
        - normed * jnp.mean(grad * normed, axis=-1, keepdims=True)
    )


def padded(width):
    return -(-width // 128) * 128


def side(a):
    more = padded(a.shape[1]) - a.shape[1]
    return jnp.concatenate([a, jnp.zeros((a.shape[0], more), a.dtype)], axis=1) if more else a


def wide(ref):
    return here(ref)[...].astype(F32)


def row(ref, i):
    return ref[i : i + 1, :]


def total(ref, *columns):
    return jnp.sum(ref, axis=0, keepdims=True)


def qkv_rows(x, mod, qkv, hidden_ref, q_ref, kv_ref):
    width = q_ref.shape[1]
    hidden = (norm(x)[0] * (1.0 + row(mod, 1)) + row(mod, 0)).astype(BF16)
    hidden_ref[...] = hidden
    projected = dot(hidden, here(qkv)[...], NT).astype(BF16)
    q_ref[...] = projected[:, :width]
    kv_ref[:, : 2 * width] = projected[:, width:]


def enc_qkv_kernel(first, second, mod, qkv, x_ref, hidden_ref, q_ref, kv_ref):
    features = x_ref.shape[1]
    both = jnp.concatenate([first[...], second[...]])
    x = both[:, :features].astype(F32)
    x_ref[...] = x
    qkv_rows(x, mod, qkv, hidden_ref, q_ref, kv_ref)
    width = q_ref.shape[1]
    kv_ref[:, 2 * width :] = (both[:, features:].astype(F32) >= 0.0).astype(F32).astype(BF16)


def block_end(residual, part, other, mod):
    return residual[...] + row(mod, 5) * (wide(part) + wide(other))


def dec_qkv_kernel(
    residual, part, other, enc_mod, matches, mask, mod, qkv, x_ref, hidden_ref, q_ref, kv_ref
):
    enc_out = block_end(residual, part, other, enc_mod)
    found = matches[...]
    uncovered = 1.0 - jnp.sum(found, axis=1, keepdims=True)
    x = dot(found, enc_out, precision=lax.Precision.HIGHEST) + uncovered * wide(mask)
    x_ref[...] = x
    qkv_rows(x, mod, qkv, hidden_ref, q_ref, kv_ref)


def window(head, width):
    first, last = head * HS, (head + 1) * HS
    start, stop = first // 128 * 128, min(-(-last // 128) * 128, width)
    lanes = lax.broadcasted_iota(jnp.int32, (1, stop - start), 1) + start
    return slice(start, stop), ((lanes >= first) & (lanes < last)).astype(F32)


def probs_of(queries, keys, live):
    scores = dot(keys, queries, NT) * SCALE
    if live is not None:
        scores = jnp.where(live, scores, -1e30)
    exponent = jnp.exp(scores - jnp.max(scores, axis=0, keepdims=True))
    return exponent / jnp.sum(exponent, axis=0, keepdims=True)


def live_of(kv, kv_other, width):
    if kv.shape[1] == 2 * width:
        return None
    own, other = (a[:, 2 * width : 2 * width + 128].astype(F32)[:, :1] for a in (kv, kv_other))
    return jnp.concatenate([own, other]) > 0.5


def attention_kernel(q, kv, kv_other, proj, hidden, *refs):
    width, features = q.shape[1], hidden.shape[1]
    if len(refs) > 3:
        first, second, mod, rows_ref, part_ref, grad_ref, total_ref = refs
        grad_out = jnp.concatenate([first[...], second[...]])
        grad_ref[...] = grad_out
        rows_ref[:, features : 2 * features] = (row(mod, 5) * grad_out.astype(F32)).astype(BF16)
    else:
        rows_ref, part_ref, total_ref = refs
    rows_ref[:, :features] = hidden[...]
    live = live_of(kv, kv_other, width)
    total_ref[...] = jnp.zeros_like(total_ref)
    for head in range(width // HS):
        at, mask = window(head, width)
        beside = slice(width + at.start, width + at.stop)
        queries = (wide(q.at[:, at]) * mask).astype(BF16)
        keys = jnp.concatenate([kv[:, at], kv_other[:, at]])
        values = jnp.concatenate([kv[:, beside], kv_other[:, beside]])
        probs = probs_of(queries, keys, live).astype(BF16)
        total_ref[:, at] += dot(probs, values, TN) * mask
    attended = total_ref[...].astype(BF16)
    rows_ref[:, rows_ref.shape[1] - padded(width) :] = side(attended)
    part_ref[...] = dot(attended, here(proj)[...]).astype(BF16)


def mlp_kernel(x, part, other, mod, up, down, *refs):
    before, (residual_ref, pre_ref, rows_ref, part_ref) = refs[:-4], refs[-4:]
    features = x.shape[1]
    if before:
        rows_ref[:, up.shape[1] + features :] = before[0][...]
    hidden_units = up.shape[1]
    residual = x[...] + row(mod, 2) * (wide(part) + wide(other))
    residual_ref[...] = residual
    mlp_input = (norm(residual)[0] * (1.0 + row(mod, 4)) + row(mod, 3)).astype(BF16)
    rows_ref[:, hidden_units : hidden_units + features] = mlp_input
    pre = dot(mlp_input, up[...])
    pre_ref[...] = pre
    activated = jax.nn.gelu(pre, approximate=True).astype(BF16)
    rows_ref[:, :hidden_units] = activated
    part_ref[...] = dot(activated, down[...]).astype(BF16)


def gelu_slope(u):
    c = math.sqrt(2.0 / math.pi)
    t = jnp.tanh(c * (u + 0.044715 * u * u * u))
    return 0.5 * (1.0 + t) + 0.5 * u * (1.0 - t * t) * c * (1.0 + 3 * 0.044715 * u * u)


def enc_mlp_back_kernel(grad_out, pre, mod, up, down, rows_ref, part_ref):
    hidden_units = up.shape[1]
    grad_mlp = (row(mod, 5) * wide(grad_out)).astype(BF16)
    rows_ref[:, hidden_units:] = grad_mlp
    mlp_back(grad_mlp, pre, up, down, rows_ref, part_ref)


def dec_mlp_back_kernel(attn_rows, pre, up, down, rows_ref, part_ref):
    features = up.shape[0]
    mlp_back(attn_rows[:, features : 2 * features], pre, up, down, rows_ref, part_ref)


def mlp_back(grad_mlp, pre, up, down, rows_ref, part_ref):
    hidden_units = up.shape[1]
    grad_pre = (dot(grad_mlp, down[...], NT) * gelu_slope(here(pre)[...])).astype(BF16)
    rows_ref[:, :hidden_units] = grad_pre
    part_ref[...] = dot(grad_pre, up[...], NT).astype(BF16)


def attention_back_kernel(
    grad_out, part, other, residual, branch, branch_other, mod, proj, q, kv, kv_other,
    grad_residual_ref, grad_branch_ref, dq_ref, dkv_ref, dkv_other_ref, sums_ref,
    dk_ref, dv_ref,
):
    rows, width = dq_ref.shape
    grad_input = wide(part) + wide(other)
    normed, inverse = norm(here(residual)[...])
    sums_ref[0:1, :] = jnp.sum(grad_input, axis=0, keepdims=True)
    sums_ref[1:2, :] = jnp.sum(grad_input * normed, axis=0, keepdims=True)
    grad_residual = wide(grad_out) + norm_back(grad_input * (1.0 + row(mod, 4)), normed, inverse)
    grad_residual_ref[...] = grad_residual
    sums_ref[2:3, :] = jnp.sum(
        grad_residual * (wide(branch) + wide(branch_other)), axis=0, keepdims=True
    )
    grad_branch = (row(mod, 2) * grad_residual).astype(BF16)
    grad_branch_ref[...] = grad_branch
    grad_attended = dot(grad_branch, here(proj)[...], NT).astype(BF16).astype(F32)
    q, kv, kv_other = here(q), here(kv), here(kv_other)

    live = live_of(kv, kv_other, width)
    dk_ref[...] = jnp.zeros_like(dk_ref)
    dv_ref[...] = jnp.zeros_like(dv_ref)
    dq_total = []
    for head in range(width // HS):
        at, mask = window(head, width)
        beside = slice(width + at.start, width + at.stop)
        queries = (wide(q.at[:, at]) * mask).astype(BF16)
        grad_head = (grad_attended[:, at] * mask).astype(BF16)
        keys = jnp.concatenate([kv[:, at], kv_other[:, at]])
        values = jnp.concatenate([kv[:, beside], kv_other[:, beside]])
        probs = probs_of(queries, keys, live)
        grad_probs = dot(values, grad_head, NT)
        inner = jnp.sum(probs * grad_probs, axis=0, keepdims=True)
        grad_scores = (probs * (grad_probs - inner)).astype(BF16)
        dk_ref[:, at] += dot(grad_scores, queries)
        dv_ref[:, at] += dot(probs.astype(BF16), grad_head)
        dq_total.append((at, dot(grad_scores, keys, TN) * (mask * SCALE)))
    for tile in range(0, width, 128):
        stop = min(tile + 128, width)
        terms = [
            part_[:, tile - at.start : stop - at.start]
            for at, part_ in dq_total
            if at.start <= tile and stop <= at.stop
        ]
        dq_ref[:, tile:stop] = functools.reduce(lambda a, b: a + b, terms).astype(BF16)
    dkv_ref[:, :width] = dk_ref[:rows, :] * SCALE
    dkv_ref[:, width:] = dv_ref[:rows, :]
    dkv_other_ref[:, :width] = (dk_ref[rows:, :] * SCALE).astype(BF16)
    dkv_other_ref[:, width:] = dv_ref[rows:, :].astype(BF16)


def qkv_back_kernel(dq, dkv, dkv_other, grad_branch, qkv, rows_ref, part_ref):
    features = grad_branch.shape[1]
    grad_projected = jnp.concatenate(
        [dq[...], (dkv[...] + wide(dkv_other)).astype(BF16)], axis=1
    )
    rows_ref[:, :features] = grad_branch[...]
    rows_ref[:, features:] = side(grad_projected)
    part_ref[...] = dot(grad_projected, here(qkv)[...]).astype(BF16)


def block_back(part, other, grad_residual, x, mod, sums_ref):
    grad_hidden = wide(part) + wide(other)
    normed, inverse = norm(here(x)[...])
    sums_ref[0:1, :] = jnp.sum(grad_hidden, axis=0, keepdims=True)
    sums_ref[1:2, :] = jnp.sum(grad_hidden * normed, axis=0, keepdims=True)
    return here(grad_residual)[...] + norm_back(grad_hidden * (1.0 + row(mod, 1)), normed, inverse)


def dec_end_kernel(part, other, grad_residual, x, mod, matches, grad_ref, sums_ref):
    grad_x = block_back(part, other, grad_residual, x, mod, sums_ref)
    found = matches[...]
    uncovered = 1.0 - jnp.sum(found, axis=1, keepdims=True)
    sums_ref[2:3, :] = jnp.sum(uncovered * grad_x, axis=0, keepdims=True)
    grad_ref[...] = dot(found, grad_x, TN, precision=lax.Precision.HIGHEST)


def enc_end_kernel(
    part, other, grad_residual, x, mod, grad_out, mlp, mlp_other, first_ref, second_ref, sums_ref
):
    grad = block_back(part, other, grad_residual, x, mod, sums_ref).astype(BF16)
    half = first_ref.shape[0]
    first_ref[...], second_ref[...] = grad[:half], grad[half:]
    sums_ref[2:3, :] = jnp.sum(wide(grad_out) * (wide(mlp) + wide(mlp_other)), axis=0, keepdims=True)


def out_kernel(residual, part, other, mod, grad_out, first_ref, second_ref, sums_ref):
    out = block_end(here(residual), here(part), other, mod).astype(BF16)
    half = first_ref.shape[0]
    first_ref[...], second_ref[...] = out[:half], out[half:]
    sums_ref[...] = jnp.sum(wide(grad_out) * (wide(part) + wide(other)), axis=0, keepdims=True)


def sums_kernel(enc_more, enc_sums, dec_more, dec_sums, dec_gate, out_ref):
    out_ref[0:2, :] = enc_more[0:2, :]
    out_ref[2:3, :] = enc_sums[2:3, :]
    out_ref[3:5, :] = enc_sums[0:2, :]
    out_ref[5:6, :] = enc_more[2:3, :]
    out_ref[6:8, :] = dec_more[0:2, :]
    out_ref[8:9, :] = dec_sums[2:3, :]
    out_ref[9:11, :] = dec_sums[0:2, :]
    out_ref[11:12, :] = dec_gate[...]
    out_ref[12:13, :] = dec_more[2:3, :]


def chosen(flags, i, first, second):
    return jnp.where(flags[i : i + 1, :1] > 0.5, first, second)


def columns_kernel(sums, other, flags, sent_ref, kept_ref):
    total = sums[...] + other[...]
    chunk = sent_ref.shape[2]
    across = total.shape[1] // chunk
    count = (sent_ref.shape[1] - across) // 2

    def piece(first_row, i):
        at, lane = first_row + i // across, i % across * chunk
        return total[at : at + 1, lane : lane + chunk]

    def message(z):
        parts = [
            chosen(
                flags, 4, piece(first_row, 2 * z * count + i), piece(first_row, (2 * z + 1) * count + i)
            )
            for first_row in (0, 6)
            for i in range(count)
        ]
        return jnp.concatenate(parts + [piece(12, i) for i in range(across)])

    for high in range(2):
        low, odd = message(2 * high), message(2 * high + 1)
        sent_ref[high] = chosen(flags, 3, odd, low)
        kept_ref[high] = chosen(flags, 3, low, odd)


def images_kernel(kept, got, flags, sent_ref, kept_ref):
    for bit in range(2):
        low, high = (
            chosen(flags, 3, kept[i], got[i]) if bit == 0 else chosen(flags, 3, got[i], kept[i])
            for i in range(2)
        )
        sent_ref[bit] = chosen(flags, 2, high, low)
        kept_ref[bit] = chosen(flags, 2, low, high)


def all_images_kernel(kept, got, flags, out_ref):
    for bit in range(2):
        out_ref[bit] = chosen(flags, 2, kept[bit], got[bit])
        out_ref[2 + bit] = chosen(flags, 2, got[bit], kept[bit])


def ada_kernel(rows, silu, enc_ref, dec_ref, mask_ref):
    chunk = rows.shape[2]
    count = enc_ref.shape[1] // chunk
    for first, out in ((0, enc_ref), (count, dec_ref)):
        for i in range(count):
            out[:, i * chunk : (i + 1) * chunk] = dot(
                silu[...], rows[:, first + i, :].astype(BF16), TN
            )
    mask_ref[...] = jnp.sum(rows[:, 2 * count :, :], axis=0)


def weight_grad_kernel(products, unread, *refs):
    count = 1 + max(max(p[0][0], p[1][0]) for p in products)
    bundles, refs = refs[: 4 * count], refs[4 * count :]
    select, refs = refs[0], refs[1 + unread :]
    sent_ref, kept_ref, *buffers, semaphores = refs
    features = select.shape[1]
    half = sent_ref.shape[0]
    copies = []
    for at, ((narrow, first), (full, start, span)) in enumerate(products):
        for bundle, begin, size, buffer in (
            (narrow, first, features, buffers[2 * at]),
            (full, start, padded(span), buffers[2 * at + 1]),
        ):
            for part in range(4):
                source = bundles[4 * bundle + part]
                rows = source.shape[0]
                copies.append(
                    pltpu.make_async_copy(
                        source.at[:, begin : begin + size],
                        buffer.at[part * rows : (part + 1) * rows, :],
                        semaphores.at[len(copies)],
                    )
                )
                copies[-1].start()
    column = 0
    for at, (_, (_, _, span)) in enumerate(products):
        features_all, rows_all = buffers[2 * at], buffers[2 * at + 1]
        for copy in copies[8 * at : 8 * at + 4]:
            copy.wait()
        chosen = dot(select[...], features_all[...], NT).astype(BF16)
        for copy in copies[8 * at + 4 : 8 * at + 8]:
            copy.wait()
        sent_ref[:, column : column + span] = dot(chosen[:half], rows_all[:, :span]).astype(BF16)
        kept_ref[:, column : column + span] = dot(chosen[half:], rows_all[:, :span])
        column += span


def halve_kernel(kept, got, sent_ref, kept_ref):
    rows = kept_ref.shape[0]
    sums = here(kept)[...] + wide(got)
    kept_ref[...] = sums[:rows]
    sent_ref[...] = sums[rows:].astype(BF16)


def finish_kernel(kept, got, *outs):
    kept = here(kept)
    at = 0
    for out in outs:
        for part in range(out.shape[0] if len(out.shape) == 3 else 1):
            span = out.shape[-1]
            place = (part,) if len(out.shape) == 3 else ()
            out[place + (...,)] = kept[:, at : at + span] + wide(got.at[:, at : at + span])
            at += span


def in_order(mine, other, first):
    return jnp.stack([jnp.where(first, mine, other), jnp.where(first, other, mine)])


class Net:
    def __init__(self, mesh):
        self.ndp, self.nreg, self.nhead = (mesh.shape[a] for a in ("dp", "region", "heads"))
        assert self.nreg == 4 and self.nhead == 2 and self.ndp % 2 == 0
        self.nhi = self.ndp // 2
        self.core_perm = [(d, d ^ 1) for d in range(self.ndp)]
        self.near = [(z, z ^ 1) for z in range(4)]
        self.far = [(z, z ^ 2) for z in range(4)]
        self.spread = [
            [
                (d * 4 + r, (d - d % 2 + r // 2) * 4 + 2 * (d % 2) + (r + j) % 2)
                for d in range(self.ndp)
                for r in range(4)
            ]
            for j in range(2)
        ]

    def place(self, anchor):
        dp, z, y = (lax.axis_index(a) for a in ("dp", "region", "heads"))
        numbers = (dp, z) + tuple(
            bit == 0 for bit in (dp // 2 % 2, dp % 2, z // 2, z % 2, y)
        )
        flags = jnp.stack([jnp.broadcast_to(a, (128,)) for a in numbers[2:]]).astype(F32)
        anchor, self.flags, *numbers = tie(anchor, flags, *numbers)
        self.dp, self.z, self.hi_first, self.core_first, self.z1_first, self.z0_first, self.y_first = numbers
        return anchor

    def to_core(self, a):
        with jax.named_scope("core"):
            return lax.ppermute(a, "dp", self.core_perm)

    def to_near(self, a):
        with jax.named_scope("near"):
            return lax.ppermute(a, "region", self.near)

    def to_far(self, a):
        with jax.named_scope("far"):
            return lax.ppermute(a, "region", self.far)

    def to_heads(self, a):
        with jax.named_scope("heads"):
            return lax.ppermute(a, "heads", [(0, 1), (1, 0)])

    def to_hi(self, a):
        with jax.named_scope("hi"):
            return lax.ppermute(a, "dp", [(d, d ^ 2) for d in range(self.ndp)])

    def hi_groups(self):
        return [[c + 2 * h for h in range(self.nhi)] for c in range(2)]

    def gather_hi(self, a):
        if self.nhi == 1:
            return a[None]
        if self.nhi == 2:
            return in_order(a, self.to_hi(a), self.hi_first)
        return lax.all_gather(a, "dp", axis_index_groups=self.hi_groups(), axis=0)

    def spread_halves(self, a):
        return jnp.where(self.z0_first, a[0], a[1]), jnp.where(self.z0_first, a[1], a[0])

    def spread_images(self, halves):
        with jax.named_scope("spread"):
            return [
                lax.ppermute(part, ("dp", "region"), perm)
                for part, perm in zip(halves, self.spread)
            ]

    def collect_parts(self, parts):
        with jax.named_scope("collect"):
            return [
                lax.ppermute(part, ("dp", "region"), [(t, s) for s, t in perm])
                for part, perm in zip(parts, self.spread)
            ]

    def collected(self, back):
        return in_order(back[0], back[1], self.z0_first)

    def gather(self, rows, along_dp):
        if not along_dp:
            return rows, self.to_near(rows)
        if self.nhi == 2:
            return rows, self.to_hi(rows)
        if self.nhi > 2:
            rows = lax.all_gather(
                rows, "dp", axis_index_groups=self.hi_groups(), axis=0, tiled=True
            )
        half = rows.shape[0] // 2
        return rows[:half], rows[half:]

    def selection(self, features, along_dp):
        own = features // (self.ndp * 4)
        step = jnp.arange(4 * own)
        block = jnp.array([1, 3, 0, 2] if along_dp else [8, 10, 0, 2])[step // own]
        feature = ((self.dp * 4 + self.z) ^ block) * own + step % own
        return (feature[:, None] == jnp.arange(features)[None, :]).astype(BF16)

    def first_half(self, sent, along_dp):
        return self.to_near(sent) if along_dp else self.to_hi(sent)


def weight_grads(products, bundles, select, after=()):
    half = select.shape[0] // 2
    features = select.shape[1]
    width = sum(full[2] for _, full in products)
    rows = 4 * bundles[0][0].shape[0]
    operands = [in_hbm(a) for bundle in bundles for a in bundle]
    vmem, hbm = pl.BlockSpec(memory_space=pltpu.VMEM), pl.BlockSpec(memory_space=pl.ANY)
    buffers = [
        pltpu.VMEM((rows, padded(span)), BF16)
        for _, (_, _, size) in products
        for span in (features, size)
    ]
    held = sum(2 * math.prod(buffer.shape) for buffer in buffers) + 16 * 2**20
    return pl.pallas_call(
        functools.partial(weight_grad_kernel, products, len(after)),
        out_shape=[
            jax.ShapeDtypeStruct((half, width), BF16), jax.ShapeDtypeStruct((half, width), F32)
        ],
        in_specs=[hbm] * len(operands) + [vmem] + [hbm] * len(after),
        out_specs=[vmem] * 2,
        name="weight_grads",
        scratch_shapes=buffers + [pltpu.SemaphoreType.DMA((8 * len(products),))],
        compiler_params=pltpu.CompilerParams(vmem_limit_bytes=max(VMEM_LIMIT, held)),
        cost_estimate=pl.CostEstimate(
            flops=0,
            bytes_accessed=0,
            transcendentals=0,
        ),
    )(*operands, select, *after)


def finish(kept, got, *shapes, after=()):
    return call(finish_kernel, [(shape, F32) for shape in shapes], kept, got, after=after)


def halve(kept, got, after=()):
    rows, width = kept.shape
    return call(halve_kernel, [((rows // 2, width), BF16), ((rows // 2, width), F32)], kept, got, after=after)


DUE = {
    "grad_parts": "e3", "F far": "d3", "A far": "b2", "M far": "b3", "G far": "c1", "H far": "c2",
    "E far": "c4", "K far": "grads enc_attn", "mlp_other": "c4", "out_kernel": "modulation",
    "down grads": "b4", "down first": "c3", "down halved": "c4", "up grads": "c2",
    "up first": "halve up", "attn grads": "c4", "mlp_part": "c2", "modulation": "finish attn",
    "silu": "e3", "images": "halve up", "parts": "finish down",
}
DEC_ALONG_DP, ENC_ALONG_DP, ENC_ROWS = False, False, "FEK"
TAIL = (
    "modulation", "collect", "halve up", "grads enc_up", "grads enc_down", "finish down",
    "halve attn", "grads enc_attn", "finish up", "halve enc_up", "halve enc_down", "finish attn",
    "halve enc_attn", "finish enc_up", "finish enc_down", "finish enc_attn",
)


class Plan:
    def __init__(self, net, features):
        self.net, self.values, self.makers = net, {}, {}
        self.ways = [net.nhi != 2 or along_dp for along_dp in (DEC_ALONG_DP, ENC_ALONG_DP)]
        self.selects = tie(*(net.selection(features, way) for way in self.ways))

    def put(self, name, *arrays):
        self.values[name] = arrays

    def later(self, name, maker):
        self.makers[name] = maker

    def get(self, name):
        if name not in self.values:
            with jax.named_scope(name.replace(" ", "_")):
                self.put(name, *self.makers[name]())
        return self.values[name]

    def tick(self, point, *chain):
        names = [n for n in DUE if DUE[n] == point and (n in self.values or n in self.makers)]
        counts = [len(self.get(name)) for name in names]
        tied = list(tie(*chain, *(a for name in names for a in self.get(name))))
        chain, tied = tied[: len(chain)], tied[len(chain) :]
        for name, count in zip(names, counts):
            self.put(name, *tied[:count])
            tied = tied[count:]
        return chain[0] if len(chain) == 1 else chain

    def place_rows(self, name, rows):
        with jax.named_scope(name + "_far"):
            own, far = self.net.gather(rows, self.ways[name in ENC_ROWS])
        self.put(name + " own", own)
        self.put(name + " far", far)
        self.later(name + " core", lambda: (self.net.to_core(own),))
        self.later(name + " both", lambda: (self.net.to_core(self.get(name + " far")[0]),))

    def weight_grads(self, name, products, bundles, after=()):
        enc = bundles[0] in ENC_ROWS
        sets = [
            tuple(self.get(bundle + kind)[0] for kind in (" own", " far", " core", " both"))
            for bundle in bundles
        ]
        sent, kept = weight_grads(products, sets, self.selects[enc], after)
        self.put(name + " grads", sent, kept)
        self.later(
            name + " first", lambda: (self.net.first_half(self.get(name + " grads")[0], self.ways[enc]),)
        )
        self.later(name + " halved", lambda: self.halved(name))
        self.later(name + " last", lambda: (self.net.to_far(self.get(name + " halved")[0]),))
        return sent

    def halved(self, name, after=()):
        (got,), (_, kept) = self.get(name + " first"), self.get(name + " grads")
        return halve(kept, got, after)

    def halve(self, name, after):
        self.put(name + " halved", *self.halved(name, after))
        return self.get(name + " halved")[0]

    def ends(self, name):
        return self.get(name + " halved")[1], self.get(name + " last")[0]


def shards(
    net, enc_in, kept_pos, slot_live, condition, mask_token, enc_ada, enc_qkv, enc_proj, enc_up,
    enc_down, dec_ada, dec_qkv, dec_proj, dec_up, dec_down, cotangent,
):
    condition = net.place(condition)
    cap, features = enc_in.shape[1:]
    tokens = cotangent.shape[1]
    assert enc_in.shape[0] == 2
    width, units, block = enc_proj.shape[0], enc_up.shape[1], enc_ada.shape[1]
    plan = Plan(net, features)
    enc_qkv, dec_qkv = (
        jnp.transpose(a, (1, 2, 0)).reshape(3 * width, features) for a in (enc_qkv, dec_qkv)
    )

    code = jnp.where(slot_live > 0, kept_pos, -1).astype(BF16)
    sent = jnp.concatenate([enc_in, jnp.broadcast_to(code[..., None], code.shape + (128,))], axis=2)
    slots = net.spread_images(net.spread_halves(sent))
    grad_parts = net.spread_halves(cotangent)

    silu = jax.nn.silu(condition.astype(F32)).astype(BF16)
    silu = in_order(silu, net.to_core(silu), net.core_first).reshape(4, features)
    cols = jnp.concatenate([dot(silu, enc_ada), dot(silu, dec_ada)], axis=1)
    cols = cols.reshape(2, 2, 2 * block)
    got = net.to_near(jnp.where(net.z0_first, cols[:, 1], cols[:, 0]))
    got, *rest = tie(got, *slots, *grad_parts, *plan.selects)
    slots, grad_parts, plan.selects = rest[:2], rest[2:4], rest[4:]
    code = jnp.concatenate([part[:, features] for part in slots]).astype(jnp.int32)
    place = jnp.arange(2 * tokens)
    matches = (place[:, None] // tokens == jnp.arange(2 * cap)[None, :] // cap) & (
        code[None, :] == place[:, None] % tokens
    )
    matches = matches.astype(F32)
    cols = in_order(jnp.where(net.z0_first, cols[:, 0], cols[:, 1]), got, net.z0_first)
    got = net.to_far(jnp.where(net.z1_first, cols[:, 1], cols[:, 0]))
    got, matches, *grad_parts = tie(got, matches, *grad_parts)
    cols = in_order(jnp.where(net.z1_first, cols[:, 0], cols[:, 1]), got, net.z1_first)
    grad_parts = net.spread_images(grad_parts)
    cols = in_order(cols, net.to_heads(cols), net.y_first)
    cols = jnp.moveaxis(cols, 0, 2).reshape(8, 2, block)
    enc_mod, dec_mod = tie(cols[:, 0].reshape(6, features), cols[:, 1].reshape(6, features))

    def attention(q, kv, kv_other, proj, hidden, *more):
        rows = q.shape[0]
        beside = [((rows, features), BF16)] if more else []
        return call(
            attention_kernel,
            [((rows, padded(width) + (1 + len(beside)) * features), BF16), ((rows, features), BF16)] + beside,
            q, kv, kv_other, proj, hidden, *more,
            scratch=[pltpu.VMEM((rows, width), F32)],
        )

    def mlp(x, part, other, mod, up, down, *more):
        rows = x.shape[0]
        beside = units + features + sum(a.shape[1] for a in more)
        return call(
            mlp_kernel,
            [((rows, features), F32), ((rows, units), F32), ((rows, beside), BF16), ((rows, features), BF16)],
            x, part, other, mod, up, down, *more,
        )

    def attention_back(grad_out, part, other, s, mod, proj):
        rows = grad_out.shape[0]
        return call(
            attention_back_kernel,
            [
                ((rows, features), F32), ((rows, features), BF16), ((rows, width), BF16),
                ((rows, 2 * width), F32), ((rows, 2 * width), BF16), ((3, features), F32),
            ],
            grad_out, part, other, s["residual"], s["branch"], s["branch_other"], mod, proj,
            s["q"], s["kv"], s["kv_other"], late=(3, 4, 5, 8, 9, 10),
            scratch=[pltpu.VMEM((2 * rows, width), F32)] * 2,
        )

    def qkv_back(dq, dkv, dkv_other, grad_branch, qkv):
        rows = dq.shape[0]
        return call(
            qkv_back_kernel, [((rows, padded(3 * width) + features), BF16), ((rows, features), BF16)],
            dq, dkv, dkv_other, grad_branch, qkv,
        )

    tick, place_rows = plan.tick, plan.place_rows

    rows = 2 * cap
    plan.put("grad_parts", *grad_parts)
    plan.later("silu", lambda: (net.gather_hi(silu).reshape(net.nhi * 4, features),))
    enc_mod, dec_mod = tick("e1", enc_mod, dec_mod)
    x, hidden, q, kv = call(
        enc_qkv_kernel,
        [((rows, features), F32), ((rows, features), BF16), ((rows, width), BF16), ((rows, 2 * width + 128), BF16)],
        *slots, enc_mod, enc_qkv, late=(3,),
    )
    kv_other = tick("e2", net.to_core(kv))
    enc_attn_rows, branch = attention(q, kv, kv_other, enc_proj, hidden)
    branch, up, down = load(branch, enc_up, enc_down)
    branch_other = tick("e3", net.to_heads(branch))
    residual, pre, enc_rows, mlp_part = mlp(
        x, branch, branch_other, enc_mod, up, down, enc_attn_rows
    )
    mlp_part, qkv = load(mlp_part, dec_qkv)
    mlp_other = net.to_heads(mlp_part)
    enc = dict(
        x=x, q=q, kv=kv, kv_other=kv_other, branch=branch, branch_other=branch_other,
        residual=residual, pre=pre, mlp=mlp_part, mlp_other=mlp_other,
    )
    place_rows("F", enc_rows)

    rows = 2 * tokens
    mlp_other = tick("d1", mlp_other)
    x, hidden, q, kv = call(
        dec_qkv_kernel,
        [((rows, features), F32), ((rows, features), BF16), ((rows, width), BF16), ((rows, 2 * width), BF16)],
        residual, mlp_part, mlp_other, enc_mod, matches, mask_token[None], dec_mod, qkv,
    )
    kv_other = tick("d2", net.to_core(kv))
    attn_rows, branch, grad_out = attention(
        q, kv, kv_other, dec_proj, hidden, *plan.get("grad_parts"), dec_mod
    )
    branch, up, down = load(branch, dec_up, dec_down)
    branch_other = net.to_heads(branch)
    place_rows("A", attn_rows)
    branch_other = tick("d3", branch_other)
    residual, pre, mlp_rows, mlp_part = mlp(x, branch, branch_other, dec_mod, up, down)
    dec = dict(
        x=x, q=q, kv=kv, kv_other=kv_other, branch=branch, branch_other=branch_other,
        residual=residual, pre=pre, grad_out=grad_out,
    )
    place_rows("M", mlp_rows)

    pre, mlp_part = tick("b1", pre, mlp_part)
    plan.put("mlp_part", mlp_part)
    plan.later("mlp_other", lambda: (net.to_heads(plan.get("mlp_part")[0]),))
    grad_rows, part = call(
        dec_mlp_back_kernel, [((rows, units), BF16), ((rows, features), BF16)],
        attn_rows, pre, up, down,
    )
    part = tick("b1x", part)
    part, proj = load(part, dec_proj)
    other = net.to_heads(part)
    place_rows("G", grad_rows)
    plan.later(
        "out_kernel",
        lambda: call(
            out_kernel, [((tokens, features), BF16)] * 2 + [((1, features), F32)],
            dec["residual"], *plan.get("mlp_part"), *plan.get("mlp_other"), dec_mod, dec["grad_out"],
            late=(0, 1, 4),
        ),
    )
    other = tick("b2", other)
    grad_residual, grad_branch, dq, dkv, dkv_other, dec_sums = attention_back(
        grad_out, part, other, dec, dec_mod, proj
    )
    dkv_other, qkv = load(dkv_other, dec_qkv)
    dkv_other = tick("b3", net.to_core(dkv_other))
    grad_attn_rows, part = qkv_back(dq, dkv, dkv_other, grad_branch, qkv)
    part, up, down = load(part, enc_up, enc_down)
    other = net.to_heads(part)
    place_rows("H", grad_attn_rows)
    plan.weight_grads("down", (((0, features), (1, 0, units)),), ("A", "M"))
    other = tick("b4", other)
    grad_enc, dec_more = call(
        dec_end_kernel, [((2 * cap, features), F32), ((3, features), F32)],
        part, other, grad_residual, dec["x"], dec_mod, matches, late=(2, 3),
    )

    rows = 2 * cap
    grad_out = tick("c1", grad_enc)
    enc_grad_rows, part = call(
        enc_mlp_back_kernel, [((rows, units + features), BF16), ((rows, features), BF16)],
        grad_out, enc["pre"], enc_mod, up, down, late=(1,),
    )
    part = tick("c1x", part)
    part, proj = load(part, enc_proj)
    other = net.to_heads(part)
    place_rows("E", enc_grad_rows)
    plan.weight_grads("up", (((0, units), (1, 0, units)),), ("M", "G"))
    other = tick("c2", other)
    grad_residual, grad_branch, dq, dkv, dkv_other, enc_sums = attention_back(
        grad_out, part, other, enc, enc_mod, proj
    )
    dkv_other, qkv = load(dkv_other, enc_qkv)
    dkv_other = tick("c3", net.to_core(dkv_other))
    enc_grad_attn_rows, part = qkv_back(dq, dkv, dkv_other, grad_branch, qkv)
    part = tick("c3x", part)
    other = net.to_heads(part)
    place_rows("K", enc_grad_attn_rows)
    plan.weight_grads(
        "attn", (((0, 0), (1, features, 3 * width)), ((1, 0), (0, 2 * features, width))),
        ("A", "H"),
    )
    other = tick("c4", other)
    *grad_in, enc_more = call(
        enc_end_kernel, [((cap, features), BF16)] * 2 + [((3, features), F32)],
        part, other, grad_residual, enc["x"], enc_mod, grad_out, enc["mlp"], enc["mlp_other"],
        late=(2, 3, 6, 7),
    )

    products = dict(
        enc_up=((((0, units), (1, 0, units)),), ("F", "E")),
        enc_down=((((1, units), (0, 0, units)),), ("F", "E")),
        enc_attn=(
            (
                ((0, units + features), (1, features, 3 * width)),
                ((1, 0), (0, units + 2 * features, width)),
            ),
            ("F", "K"),
        ),
    )
    share = features // (net.ndp * 4)
    shapes = {name: ((share, units),) for name in ("down", "up", "enc_down", "enc_up")}
    shapes["attn"] = shapes["enc_attn"] = ((3, share, width), (share, width))
    grads = {}
    chunk = features // 4
    assert 3 * chunk == block
    message = (2, 2 * 3 + 4, chunk)

    def modulation_rows(sums):
        sent, kept = call(
            columns_kernel, [(message, F32)] * 2, sums, net.to_core(sums), net.flags
        )
        sent, kept = call(images_kernel, [(message, F32)] * 2, kept, net.to_near(sent), net.flags)
        return call(
            all_images_kernel, [((4,) + message[1:], F32)], kept, net.to_far(sent), net.flags
        )

    plan.later(
        "modulation",
        lambda: (net.gather_hi(plan.get("images")[0]).reshape(net.nhi * 4, *message[1:]),),
    )

    last = enc_more
    for step in TAIL:
        kind, _, name = step.partition(" ")
        last = tick(step, last)
        if kind == "grads":
            last = plan.weight_grads(name, *products[name], after=(last,))
        elif kind == "halve":
            last = plan.halve(name, after=(last,))
        elif kind == "finish":
            grads[name] = finish(*plan.ends(name), *shapes[name], after=(last,))
            last = grads[name][0]
        elif step == "collect":
            last, *grad_in = tie(last, *grad_in)
            plan.later("parts", functools.partial(net.collect_parts, [
                jnp.concatenate([a, b]) for a, b in zip(plan.get("out_kernel")[:2], grad_in)
            ]))
        else:
            (vector,) = call(
                sums_kernel, [((13, features), F32)],
                enc_more, enc_sums, dec_more, dec_sums, plan.get("out_kernel")[2], after=(last,),
            )
            last = vector
            plan.later("images", functools.partial(modulation_rows, vector))

    both = plan.get("parts")
    out = net.collected([part[:tokens] for part in both])
    input_grad = net.collected([part[tokens:] for part in both]).astype(F32)
    enc_grads, dec_grads = (
        (
            jnp.transpose(grads[prefix + "attn"][0], (1, 0, 2)), grads[prefix + "attn"][1].T,
            grads[prefix + "up"][0], grads[prefix + "down"][0].T,
        )
        for prefix in ("enc_", "")
    )

    (rows,) = plan.get("modulation")
    (silu_all,) = plan.get("silu")
    silu_own = lax.dynamic_slice_in_dim(silu_all, net.dp * (4 * share), 4 * share, 1)
    enc_ada_grad, dec_ada_grad, mask_sum = call(
        ada_kernel, [((4 * share, block), F32)] * 2 + [((4, chunk), F32)], rows, silu_own
    )
    mask_grad = lax.dynamic_slice_in_dim(
        mask_sum.reshape(-1), (net.dp * 4 + net.z) * share, share, 0
    )
    return (out, input_grad, mask_grad, enc_ada_grad) + enc_grads + (dec_ada_grad,) + dec_grads

def solution(mesh):
    net = Net(mesh)
    in_specs = (
        P("dp", "region", None),
        P("dp", "region"),
        P("dp", "region"),
        P("dp", None),
        P(),
    ) + 2 * (
        P(None, ("region", "heads")),
        P(None, None, "heads"),
        P("heads", None),
        P(None, "heads"),
        P("heads", None),
    ) + (P("dp", "region", None),)
    out_specs = (
        P("dp", "region", None),
        P("dp", "region", None),
        P(("dp", "region")),
    ) + 2 * (
        P("dp", ("region", "heads")),
        P(("dp", "region"), None, "heads"),
        P("heads", ("dp", "region")),
        P(("dp", "region"), "heads"),
        P("heads", ("dp", "region")),
    )
    return jax.shard_map(
        lambda *args: shards(net, *args),
        mesh=mesh, in_specs=in_specs, out_specs=out_specs, check_vma=False,
    )
```

```python
import functools
import math

import jax
import jax.numpy as jnp
from jax import lax
from jax.experimental import pallas as pl
from jax.experimental.pallas import tpu as pltpu
from jax.sharding import PartitionSpec as P

HS = 72
SCALE = 1.0 / math.sqrt(HS)
EPSILON = 1e-06
BF16 = jnp.bfloat16
F32 = jnp.float32
VMEM_LIMIT = 16 * 2**20
LOAD_CHUNKS = 4
NT = ((1,), (1,))
TN = ((0,), (0,))


def dot(a, b, dims=((1,), (0,)), **kw):
    return lax.dot_general(a, b, (dims, ((), ())), preferred_element_type=F32, **kw)


class Late:
    def __init__(self, copy, ref):
        self.copy, self.ref, self.waited = copy, ref, False
        copy.start()

    def get(self):
        if not self.waited:
            self.copy.wait()
            self.waited = True
        return self.ref


def here(ref):
    return ref.get() if isinstance(ref, Late) else ref


def call(kernel, outs, *ins, scratch=(), late=(), after=()):
    shapes = [jax.ShapeDtypeStruct(shape, dtype) for shape, dtype in outs]
    fetched = [pltpu.VMEM(ins[i].shape, ins[i].dtype) for i in late]
    semaphores = [pltpu.SemaphoreType.DMA((len(late),))] if late else []

    def body(*refs):
        refs = list(refs)
        own = len(refs) - len(late) - len(semaphores)
        for at, i in enumerate(late):
            refs[i] = Late(pltpu.make_async_copy(refs[i], refs[own + at], refs[-1].at[at]), refs[own + at])
        kernel(*refs[: len(ins)], *refs[len(ins) + len(after) : own])
        for i in late:
            refs[i].get()

    vmem, hbm = pl.BlockSpec(memory_space=pltpu.VMEM), pl.BlockSpec(memory_space=pl.ANY)
    ins = [in_hbm(a) if i in late else a for i, a in enumerate(ins)]
    return pl.pallas_call(
        body,
        out_shape=shapes,
        in_specs=[hbm if i in late else vmem for i in range(len(ins))] + [hbm] * len(after),
        out_specs=[vmem] * len(outs),
        name=kernel.__name__,
        scratch_shapes=list(scratch) + fetched + semaphores,
        compiler_params=pltpu.CompilerParams(vmem_limit_bytes=VMEM_LIMIT),
        cost_estimate=pl.CostEstimate(flops=0, bytes_accessed=0, transcendentals=0),
    )(*ins, *after)


def in_hbm(a):
    return pltpu.with_memory_space_constraint(a, pltpu.HBM)


def load_kernel(*refs):
    count = len(refs) // 2
    copies = []
    for source, target in zip(refs[:count], refs[count : 2 * count]):
        rows = source.shape[0]
        chunk = -(-rows // LOAD_CHUNKS // 16) * 16
        for start in range(0, rows, chunk):
            part = pl.ds(start, min(chunk, rows - start))
            copies.append(
                pltpu.make_async_copy(source.at[part], target.at[part], refs[-1].at[len(copies)])
            )
            copies[-1].start()
    for copy in copies:
        copy.wait()


def load(anchor, *weights, beside=()):
    anchor, *weights = tie(anchor, *weights, *beside)
    weights, beside = weights[: len(weights) - len(beside)], weights[len(weights) - len(beside) :]
    weights = [in_hbm(w) for w in weights]
    loaded = pl.pallas_call(
        load_kernel,
        out_shape=[jax.ShapeDtypeStruct(w.shape, w.dtype) for w in weights],
        in_specs=[pl.BlockSpec(memory_space=pl.ANY)] * len(weights),
        out_specs=[pl.BlockSpec(memory_space=pltpu.VMEM)] * len(weights),
        name="load",
        scratch_shapes=[pltpu.SemaphoreType.DMA((LOAD_CHUNKS * len(weights),))],
        compiler_params=pltpu.CompilerParams(vmem_limit_bytes=VMEM_LIMIT),
        cost_estimate=pl.CostEstimate(
            flops=0, bytes_accessed=0, transcendentals=0
        ),
    )(*weights)
    return anchor, *loaded, *beside


def tie(*arrays):
    return lax.optimization_barrier(arrays)


def norm(rows):
    mean = jnp.mean(rows, axis=-1, keepdims=True)
    centered = rows - mean
    inverse = lax.rsqrt(jnp.mean(centered * centered, axis=-1, keepdims=True) + EPSILON)
    return centered * inverse, inverse


def norm_back(grad, normed, inverse):
    return inverse * (
        grad
        - jnp.mean(grad, axis=-1, keepdims=True)
        - normed * jnp.mean(grad * normed, axis=-1, keepdims=True)
    )


def padded(width):
    return -(-width // 128) * 128


def side(a):
    more = padded(a.shape[1]) - a.shape[1]
    return jnp.concatenate([a, jnp.zeros((a.shape[0], more), a.dtype)], axis=1) if more else a


def wide(ref):
    return here(ref)[...].astype(F32)


def row(ref, i):
    return ref[i : i + 1, :]


def total(ref, *columns):
    return jnp.sum(ref, axis=0, keepdims=True)


def qkv_rows(x, mod, qkv, hidden_ref, q_ref, kv_ref):
    width = q_ref.shape[1]
    hidden = (norm(x)[0] * (1.0 + row(mod, 1)) + row(mod, 0)).astype(BF16)
    hidden_ref[...] = hidden
    projected = dot(hidden, here(qkv)[...], NT).astype(BF16)
    q_ref[...] = projected[:, :width]
    kv_ref[:, : 2 * width] = projected[:, width:]


def enc_qkv_kernel(first, second, mod, qkv, x_ref, hidden_ref, q_ref, kv_ref):
    features = x_ref.shape[1]
    both = jnp.concatenate([first[...], second[...]])
    x = both[:, :features].astype(F32)
    x_ref[...] = x
    qkv_rows(x, mod, qkv, hidden_ref, q_ref, kv_ref)
    width = q_ref.shape[1]
    kv_ref[:, 2 * width :] = (both[:, features:].astype(F32) >= 0.0).astype(F32).astype(BF16)


def block_end(residual, part, other, mod):
    return residual[...] + row(mod, 5) * (wide(part) + wide(other))


def dec_qkv_kernel(
    residual, part, other, enc_mod, matches, mask, mod, qkv, x_ref, hidden_ref, q_ref, kv_ref
):
    enc_out = block_end(residual, part, other, enc_mod)
    found = matches[...]
    uncovered = 1.0 - jnp.sum(found, axis=1, keepdims=True)
    x = dot(found, enc_out, precision=lax.Precision.HIGHEST) + uncovered * wide(mask)
    x_ref[...] = x
    qkv_rows(x, mod, qkv, hidden_ref, q_ref, kv_ref)


def window(head, width):
    first, last = head * HS, (head + 1) * HS
    start, stop = first // 128 * 128, min(-(-last // 128) * 128, width)
    lanes = lax.broadcasted_iota(jnp.int32, (1, stop - start), 1) + start
    return slice(start, stop), ((lanes >= first) & (lanes < last)).astype(F32)


def probs_of(queries, keys, live):
    scores = dot(keys, queries, NT) * SCALE
    if live is not None:
        scores = jnp.where(live, scores, -1e30)
    exponent = jnp.exp(scores - jnp.max(scores, axis=0, keepdims=True))
    return exponent / jnp.sum(exponent, axis=0, keepdims=True)


def live_of(kv, kv_other, width):
    if kv.shape[1] == 2 * width:
        return None
    own, other = (a[:, 2 * width : 2 * width + 128].astype(F32)[:, :1] for a in (kv, kv_other))
    return jnp.concatenate([own, other]) > 0.5


def attention_kernel(q, kv, kv_other, proj, hidden, *refs):
    width, features = q.shape[1], hidden.shape[1]
    if len(refs) > 3:
        first, second, mod, rows_ref, part_ref, grad_ref, total_ref = refs
        grad_out = jnp.concatenate([first[...], second[...]])
        grad_ref[...] = grad_out
        rows_ref[:, features : 2 * features] = (row(mod, 5) * grad_out.astype(F32)).astype(BF16)
    else:
        rows_ref, part_ref, total_ref = refs
    rows_ref[:, :features] = hidden[...]
    live = live_of(kv, kv_other, width)
    total_ref[...] = jnp.zeros_like(total_ref)
    for head in range(width // HS):
        at, mask = window(head, width)
        beside = slice(width + at.start, width + at.stop)
        queries = (wide(q.at[:, at]) * mask).astype(BF16)
        keys = jnp.concatenate([kv[:, at], kv_other[:, at]])
        values = jnp.concatenate([kv[:, beside], kv_other[:, beside]])
        probs = probs_of(queries, keys, live).astype(BF16)
        total_ref[:, at] += dot(probs, values, TN) * mask
    attended = total_ref[...].astype(BF16)
    rows_ref[:, rows_ref.shape[1] - padded(width) :] = side(attended)
    part_ref[...] = dot(attended, here(proj)[...]).astype(BF16)


def mlp_kernel(x, part, other, mod, up, down, *refs):
    before, (residual_ref, pre_ref, rows_ref, part_ref) = refs[:-4], refs[-4:]
    features = x.shape[1]
    if before:
        rows_ref[:, up.shape[1] + features :] = before[0][...]
    hidden_units = up.shape[1]
    residual = x[...] + row(mod, 2) * (wide(part) + wide(other))
    residual_ref[...] = residual
    mlp_input = (norm(residual)[0] * (1.0 + row(mod, 4)) + row(mod, 3)).astype(BF16)
    rows_ref[:, hidden_units : hidden_units + features] = mlp_input
    pre = dot(mlp_input, up[...])
    pre_ref[...] = pre
    activated = jax.nn.gelu(pre, approximate=True).astype(BF16)
    rows_ref[:, :hidden_units] = activated
    part_ref[...] = dot(activated, down[...]).astype(BF16)


def gelu_slope(u):
    c = math.sqrt(2.0 / math.pi)
    t = jnp.tanh(c * (u + 0.044715 * u * u * u))
    return 0.5 * (1.0 + t) + 0.5 * u * (1.0 - t * t) * c * (1.0 + 3 * 0.044715 * u * u)


def enc_mlp_back_kernel(grad_out, pre, mod, up, down, rows_ref, part_ref):
    hidden_units = up.shape[1]
    grad_mlp = (row(mod, 5) * wide(grad_out)).astype(BF16)
    rows_ref[:, hidden_units:] = grad_mlp
    mlp_back(grad_mlp, pre, up, down, rows_ref, part_ref)


def dec_mlp_back_kernel(attn_rows, pre, up, down, rows_ref, part_ref):
    features = up.shape[0]
    mlp_back(attn_rows[:, features : 2 * features], pre, up, down, rows_ref, part_ref)


def mlp_back(grad_mlp, pre, up, down, rows_ref, part_ref):
    hidden_units = up.shape[1]
    grad_pre = (dot(grad_mlp, down[...], NT) * gelu_slope(here(pre)[...])).astype(BF16)
    rows_ref[:, :hidden_units] = grad_pre
    part_ref[...] = dot(grad_pre, up[...], NT).astype(BF16)


def attention_back_kernel(
    grad_out, part, other, residual, branch, branch_other, mod, proj, q, kv, kv_other,
    grad_residual_ref, grad_branch_ref, dq_ref, dkv_ref, dkv_other_ref, sums_ref,
    dk_ref, dv_ref,
):
    rows, width = dq_ref.shape
    grad_input = wide(part) + wide(other)
    normed, inverse = norm(here(residual)[...])
    sums_ref[0:1, :] = jnp.sum(grad_input, axis=0, keepdims=True)
    sums_ref[1:2, :] = jnp.sum(grad_input * normed, axis=0, keepdims=True)
    grad_residual = wide(grad_out) + norm_back(grad_input * (1.0 + row(mod, 4)), normed, inverse)
    grad_residual_ref[...] = grad_residual
    sums_ref[2:3, :] = jnp.sum(
        grad_residual * (wide(branch) + wide(branch_other)), axis=0, keepdims=True
    )
    grad_branch = (row(mod, 2) * grad_residual).astype(BF16)
    grad_branch_ref[...] = grad_branch
    grad_attended = dot(grad_branch, here(proj)[...], NT).astype(BF16).astype(F32)
    q, kv, kv_other = here(q), here(kv), here(kv_other)

    live = live_of(kv, kv_other, width)
    dk_ref[...] = jnp.zeros_like(dk_ref)
    dv_ref[...] = jnp.zeros_like(dv_ref)
    dq_total = []
    for head in range(width // HS):
        at, mask = window(head, width)
        beside = slice(width + at.start, width + at.stop)
        queries = (wide(q.at[:, at]) * mask).astype(BF16)
        grad_head = (grad_attended[:, at] * mask).astype(BF16)
        keys = jnp.concatenate([kv[:, at], kv_other[:, at]])
        values = jnp.concatenate([kv[:, beside], kv_other[:, beside]])
        probs = probs_of(queries, keys, live)
        grad_probs = dot(values, grad_head, NT)
        inner = jnp.sum(probs * grad_probs, axis=0, keepdims=True)
        grad_scores = (probs * (grad_probs - inner)).astype(BF16)
        dk_ref[:, at] += dot(grad_scores, queries)
        dv_ref[:, at] += dot(probs.astype(BF16), grad_head)
        dq_total.append((at, dot(grad_scores, keys, TN) * (mask * SCALE)))
    for tile in range(0, width, 128):
        stop = min(tile + 128, width)
        terms = [
            part_[:, tile - at.start : stop - at.start]
            for at, part_ in dq_total
            if at.start <= tile and stop <= at.stop
        ]
        dq_ref[:, tile:stop] = functools.reduce(lambda a, b: a + b, terms).astype(BF16)
    dkv_ref[:, :width] = dk_ref[:rows, :] * SCALE
    dkv_ref[:, width:] = dv_ref[:rows, :]
    dkv_other_ref[:, :width] = (dk_ref[rows:, :] * SCALE).astype(BF16)
    dkv_other_ref[:, width:] = dv_ref[rows:, :].astype(BF16)


def qkv_back_kernel(dq, dkv, dkv_other, grad_branch, qkv, rows_ref, part_ref):
    features = grad_branch.shape[1]
    grad_projected = jnp.concatenate(
        [dq[...], (dkv[...] + wide(dkv_other)).astype(BF16)], axis=1
    )
    rows_ref[:, :features] = grad_branch[...]
    rows_ref[:, features:] = side(grad_projected)
    part_ref[...] = dot(grad_projected, here(qkv)[...]).astype(BF16)


def block_back(part, other, grad_residual, x, mod, sums_ref):
    grad_hidden = wide(part) + wide(other)
    normed, inverse = norm(here(x)[...])
    sums_ref[0:1, :] = jnp.sum(grad_hidden, axis=0, keepdims=True)
    sums_ref[1:2, :] = jnp.sum(grad_hidden * normed, axis=0, keepdims=True)
    return here(grad_residual)[...] + norm_back(grad_hidden * (1.0 + row(mod, 1)), normed, inverse)


def dec_end_kernel(part, other, grad_residual, x, mod, matches, grad_ref, sums_ref):
    grad_x = block_back(part, other, grad_residual, x, mod, sums_ref)
    found = matches[...]
    uncovered = 1.0 - jnp.sum(found, axis=1, keepdims=True)
    sums_ref[2:3, :] = jnp.sum(uncovered * grad_x, axis=0, keepdims=True)
    grad_ref[...] = dot(found, grad_x, TN, precision=lax.Precision.HIGHEST)


def enc_end_kernel(
    part, other, grad_residual, x, mod, grad_out, mlp, mlp_other, first_ref, second_ref, sums_ref
):
    grad = block_back(part, other, grad_residual, x, mod, sums_ref).astype(BF16)
    half = first_ref.shape[0]
    first_ref[...], second_ref[...] = grad[:half], grad[half:]
    sums_ref[2:3, :] = jnp.sum(wide(grad_out) * (wide(mlp) + wide(mlp_other)), axis=0, keepdims=True)


def out_kernel(residual, part, other, mod, grad_out, first_ref, second_ref, sums_ref):
    out = block_end(here(residual), here(part), other, mod).astype(BF16)
    half = first_ref.shape[0]
    first_ref[...], second_ref[...] = out[:half], out[half:]
    sums_ref[...] = jnp.sum(wide(grad_out) * (wide(part) + wide(other)), axis=0, keepdims=True)


def sums_kernel(enc_more, enc_sums, dec_more, dec_sums, dec_gate, out_ref):
    out_ref[0:2, :] = enc_more[0:2, :]
    out_ref[2:3, :] = enc_sums[2:3, :]
    out_ref[3:5, :] = enc_sums[0:2, :]
    out_ref[5:6, :] = enc_more[2:3, :]
    out_ref[6:8, :] = dec_more[0:2, :]
    out_ref[8:9, :] = dec_sums[2:3, :]
    out_ref[9:11, :] = dec_sums[0:2, :]
    out_ref[11:12, :] = dec_gate[...]
    out_ref[12:13, :] = dec_more[2:3, :]


def chosen(flags, i, first, second):
    return jnp.where(flags[i : i + 1, :1] > 0.5, first, second)


def columns_kernel(sums, other, flags, sent_ref, kept_ref):
    total = sums[...] + other[...]
    chunk = sent_ref.shape[2]
    across = total.shape[1] // chunk
    count = (sent_ref.shape[1] - across) // 2

    def piece(first_row, i):
        at, lane = first_row + i // across, i % across * chunk
        return total[at : at + 1, lane : lane + chunk]

    def message(z):
        parts = [
            chosen(
                flags, 4, piece(first_row, 2 * z * count + i), piece(first_row, (2 * z + 1) * count + i)
            )
            for first_row in (0, 6)
            for i in range(count)
        ]
        return jnp.concatenate(parts + [piece(12, i) for i in range(across)])

    for high in range(2):
        low, odd = message(2 * high), message(2 * high + 1)
        sent_ref[high] = chosen(flags, 3, odd, low)
        kept_ref[high] = chosen(flags, 3, low, odd)


def images_kernel(kept, got, flags, sent_ref, kept_ref):
    for bit in range(2):
        low, high = (
            chosen(flags, 3, kept[i], got[i]) if bit == 0 else chosen(flags, 3, got[i], kept[i])
            for i in range(2)
        )
        sent_ref[bit] = chosen(flags, 2, high, low)
        kept_ref[bit] = chosen(flags, 2, low, high)


def all_images_kernel(kept, got, flags, out_ref):
    for bit in range(2):
        out_ref[bit] = chosen(flags, 2, kept[bit], got[bit])
        out_ref[2 + bit] = chosen(flags, 2, got[bit], kept[bit])


def ada_kernel(rows, silu, enc_ref, dec_ref, mask_ref):
    chunk = rows.shape[2]
    count = enc_ref.shape[1] // chunk
    for first, out in ((0, enc_ref), (count, dec_ref)):
        for i in range(count):
            out[:, i * chunk : (i + 1) * chunk] = dot(
                silu[...], rows[:, first + i, :].astype(BF16), TN
            )
    mask_ref[...] = jnp.sum(rows[:, 2 * count :, :], axis=0)


def weight_grad_kernel(products, unread, *refs):
    count = 1 + max(max(p[0][0], p[1][0]) for p in products)
    bundles, refs = refs[: 4 * count], refs[4 * count :]
    select, refs = refs[0], refs[1 + unread :]
    sent_ref, kept_ref, *buffers, semaphores = refs
    features = select.shape[1]
    half = sent_ref.shape[0]
    copies = []
    for at, ((narrow, first), (full, start, span)) in enumerate(products):
        for bundle, begin, size, buffer in (
            (narrow, first, features, buffers[2 * at]),
            (full, start, padded(span), buffers[2 * at + 1]),
        ):
            for part in range(4):
                source = bundles[4 * bundle + part]
                rows = source.shape[0]
                copies.append(
                    pltpu.make_async_copy(
                        source.at[:, begin : begin + size],
                        buffer.at[part * rows : (part + 1) * rows, :],
                        semaphores.at[len(copies)],
                    )
                )
                copies[-1].start()
    column = 0
    for at, (_, (_, _, span)) in enumerate(products):
        features_all, rows_all = buffers[2 * at], buffers[2 * at + 1]
        for copy in copies[8 * at : 8 * at + 4]:
            copy.wait()
        chosen = dot(select[...], features_all[...], NT).astype(BF16)
        for copy in copies[8 * at + 4 : 8 * at + 8]:
            copy.wait()
        sent_ref[:, column : column + span] = dot(chosen[:half], rows_all[:, :span]).astype(BF16)
        kept_ref[:, column : column + span] = dot(chosen[half:], rows_all[:, :span])
        column += span


def halve_kernel(kept, got, sent_ref, kept_ref):
    rows = kept_ref.shape[0]
    sums = here(kept)[...] + wide(got)
    kept_ref[...] = sums[:rows]
    sent_ref[...] = sums[rows:].astype(BF16)


def finish_kernel(kept, got, *outs):
    kept = here(kept)
    at = 0
    for out in outs:
        for part in range(out.shape[0] if len(out.shape) == 3 else 1):
            span = out.shape[-1]
            place = (part,) if len(out.shape) == 3 else ()
            out[place + (...,)] = kept[:, at : at + span] + wide(got.at[:, at : at + span])
            at += span


def in_order(mine, other, first):
    return jnp.stack([jnp.where(first, mine, other), jnp.where(first, other, mine)])


class Net:
    def __init__(self, mesh):
        self.ndp, self.nreg, self.nhead = (mesh.shape[a] for a in ("dp", "region", "heads"))
        assert self.nreg == 4 and self.nhead == 2 and self.ndp % 2 == 0
        self.nhi = self.ndp // 2
        self.core_perm = [(d, d ^ 1) for d in range(self.ndp)]
        self.near = [(z, z ^ 1) for z in range(4)]
        self.far = [(z, z ^ 2) for z in range(4)]
        self.spread = [
            [
                (d * 4 + r, (d - d % 2 + r // 2) * 4 + 2 * (d % 2) + (r + j) % 2)
                for d in range(self.ndp)
                for r in range(4)
            ]
            for j in range(2)
        ]

    def place(self, anchor):
        dp, z, y = (lax.axis_index(a) for a in ("dp", "region", "heads"))
        numbers = (dp, z) + tuple(
            bit == 0 for bit in (dp // 2 % 2, dp % 2, z // 2, z % 2, y)
        )
        flags = jnp.stack([jnp.broadcast_to(a, (128,)) for a in numbers[2:]]).astype(F32)
        anchor, self.flags, *numbers = tie(anchor, flags, *numbers)
        self.dp, self.z, self.hi_first, self.core_first, self.z1_first, self.z0_first, self.y_first = numbers
        return anchor

    def to_core(self, a):
        with jax.named_scope("core"):
            return lax.ppermute(a, "dp", self.core_perm)

    def to_near(self, a):
        with jax.named_scope("near"):
            return lax.ppermute(a, "region", self.near)

    def to_far(self, a):
        with jax.named_scope("far"):
            return lax.ppermute(a, "region", self.far)

    def to_heads(self, a):
        with jax.named_scope("heads"):
            return lax.ppermute(a, "heads", [(0, 1), (1, 0)])

    def to_hi(self, a):
        with jax.named_scope("hi"):
            return lax.ppermute(a, "dp", [(d, d ^ 2) for d in range(self.ndp)])

    def hi_groups(self):
        return [[c + 2 * h for h in range(self.nhi)] for c in range(2)]

    def gather_hi(self, a):
        if self.nhi == 1:
            return a[None]
        if self.nhi == 2:
            return in_order(a, self.to_hi(a), self.hi_first)
        return lax.all_gather(a, "dp", axis_index_groups=self.hi_groups(), axis=0)

    def spread_halves(self, a):
        return jnp.where(self.z0_first, a[0], a[1]), jnp.where(self.z0_first, a[1], a[0])

    def spread_images(self, halves):
        with jax.named_scope("spread"):
            return [
                lax.ppermute(part, ("dp", "region"), perm)
                for part, perm in zip(halves, self.spread)
            ]

    def collect_parts(self, parts):
        with jax.named_scope("collect"):
            return [
                lax.ppermute(part, ("dp", "region"), [(t, s) for s, t in perm])
                for part, perm in zip(parts, self.spread)
            ]

    def collected(self, back):
        return in_order(back[0], back[1], self.z0_first)

    def gather(self, rows, along_dp):
        if not along_dp:
            return rows, self.to_near(rows)
        if self.nhi == 2:
            return rows, self.to_hi(rows)
        if self.nhi > 2:
            rows = lax.all_gather(
                rows, "dp", axis_index_groups=self.hi_groups(), axis=0, tiled=True
            )
        half = rows.shape[0] // 2
        return rows[:half], rows[half:]

    def selection(self, features, along_dp):
        own = features // (self.ndp * 4)
        step = jnp.arange(4 * own)
        block = jnp.array([1, 3, 0, 2] if along_dp else [8, 10, 0, 2])[step // own]
        feature = ((self.dp * 4 + self.z) ^ block) * own + step % own
        return (feature[:, None] == jnp.arange(features)[None, :]).astype(BF16)

    def first_half(self, sent, along_dp):
        return self.to_near(sent) if along_dp else self.to_hi(sent)


def weight_grads(products, bundles, select, after=()):
    half = select.shape[0] // 2
    features = select.shape[1]
    width = sum(full[2] for _, full in products)
    rows = 4 * bundles[0][0].shape[0]
    operands = [in_hbm(a) for bundle in bundles for a in bundle]
    vmem, hbm = pl.BlockSpec(memory_space=pltpu.VMEM), pl.BlockSpec(memory_space=pl.ANY)
    buffers = [
        pltpu.VMEM((rows, padded(span)), BF16)
        for _, (_, _, size) in products
        for span in (features, size)
    ]
    held = sum(2 * math.prod(buffer.shape) for buffer in buffers) + 16 * 2**20
    return pl.pallas_call(
        functools.partial(weight_grad_kernel, products, len(after)),
        out_shape=[
            jax.ShapeDtypeStruct((half, width), BF16), jax.ShapeDtypeStruct((half, width), F32)
        ],
        in_specs=[hbm] * len(operands) + [vmem] + [hbm] * len(after),
        out_specs=[vmem] * 2,
        name="weight_grads",
        scratch_shapes=buffers + [pltpu.SemaphoreType.DMA((8 * len(products),))],
        compiler_params=pltpu.CompilerParams(vmem_limit_bytes=max(VMEM_LIMIT, held)),
        cost_estimate=pl.CostEstimate(
            flops=0,
            bytes_accessed=0,
            transcendentals=0,
        ),
    )(*operands, select, *after)


def finish(kept, got, *shapes, after=()):
    return call(finish_kernel, [(shape, F32) for shape in shapes], kept, got, after=after)


def halve(kept, got, after=()):
    rows, width = kept.shape
    return call(halve_kernel, [((rows // 2, width), BF16), ((rows // 2, width), F32)], kept, got, after=after)


DUE = {
    "grad_parts": "e3", "F far": "d3", "A far": "b2", "M far": "b3", "G far": "c1", "H far": "c2",
    "E far": "c4", "K far": "grads enc_attn", "mlp_other": "c4", "out_kernel": "modulation",
    "down grads": "b4", "down first": "c1x", "down halved": "c2", "down last": "c4",
    "up grads": "c2", "up first": "c4", "attn grads": "c4", "mlp_part": "c2",
    "modulation": "finish enc_down", "silu": "e3", "images": "grads enc_down", "parts": "finish up",
}
DEC_ALONG_DP, ENC_ALONG_DP, ENC_ROWS = False, False, "FEK"
TAIL = (
    "halve up", "modulation", "grads enc_up", "grads enc_down", "halve attn", "collect",
    "grads enc_attn", "finish up", "halve enc_up", "finish attn", "halve enc_down",
    "halve enc_attn", "finish down", "finish enc_up", "finish enc_down", "finish enc_attn",
)


class Plan:
    def __init__(self, net, features):
        self.net, self.values, self.makers = net, {}, {}
        self.ways = [net.nhi != 2 or along_dp for along_dp in (DEC_ALONG_DP, ENC_ALONG_DP)]
        self.selects = tie(*(net.selection(features, way) for way in self.ways))

    def put(self, name, *arrays):
        self.values[name] = arrays

    def later(self, name, maker):
        self.makers[name] = maker

    def get(self, name):
        if name not in self.values:
            with jax.named_scope(name.replace(" ", "_")):
                self.put(name, *self.makers[name]())
        return self.values[name]

    def tick(self, point, *chain):
        names = [n for n in DUE if DUE[n] == point and (n in self.values or n in self.makers)]
        counts = [len(self.get(name)) for name in names]
        tied = list(tie(*chain, *(a for name in names for a in self.get(name))))
        chain, tied = tied[: len(chain)], tied[len(chain) :]
        for name, count in zip(names, counts):
            self.put(name, *tied[:count])
            tied = tied[count:]
        return chain[0] if len(chain) == 1 else chain

    def place_rows(self, name, rows):
        with jax.named_scope(name + "_far"):
            own, far = self.net.gather(rows, self.ways[name in ENC_ROWS])
        self.put(name + " own", own)
        self.put(name + " far", far)
        self.later(name + " core", lambda: (self.net.to_core(own),))
        self.later(name + " both", lambda: (self.net.to_core(self.get(name + " far")[0]),))

    def weight_grads(self, name, products, bundles, after=()):
        enc = bundles[0] in ENC_ROWS
        sets = [
            tuple(self.get(bundle + kind)[0] for kind in (" own", " far", " core", " both"))
            for bundle in bundles
        ]
        sent, kept = weight_grads(products, sets, self.selects[enc], after)
        self.put(name + " grads", sent, kept)
        self.later(
            name + " first", lambda: (self.net.first_half(self.get(name + " grads")[0], self.ways[enc]),)
        )
        self.later(name + " halved", lambda: self.halved(name))
        self.later(name + " last", lambda: (self.net.to_far(self.get(name + " halved")[0]),))
        return sent

    def halved(self, name, after=()):
        (got,), (_, kept) = self.get(name + " first"), self.get(name + " grads")
        return halve(kept, got, after)

    def halve(self, name, after):
        self.put(name + " halved", *self.halved(name, after))
        return self.get(name + " halved")[0]

    def ends(self, name):
        return self.get(name + " halved")[1], self.get(name + " last")[0]


def shards(
    net, enc_in, kept_pos, slot_live, condition, mask_token, enc_ada, enc_qkv, enc_proj, enc_up,
    enc_down, dec_ada, dec_qkv, dec_proj, dec_up, dec_down, cotangent,
):
    condition = net.place(condition)
    cap, features = enc_in.shape[1:]
    tokens = cotangent.shape[1]
    assert enc_in.shape[0] == 2
    width, units, block = enc_proj.shape[0], enc_up.shape[1], enc_ada.shape[1]
    plan = Plan(net, features)
    enc_qkv, dec_qkv = (
        jnp.transpose(a, (1, 2, 0)).reshape(3 * width, features) for a in (enc_qkv, dec_qkv)
    )

    code = jnp.where(slot_live > 0, kept_pos, -1).astype(BF16)
    sent = jnp.concatenate([enc_in, jnp.broadcast_to(code[..., None], code.shape + (128,))], axis=2)
    slots = net.spread_images(net.spread_halves(sent))
    grad_parts = net.spread_halves(cotangent)

    silu = jax.nn.silu(condition.astype(F32)).astype(BF16)
    silu = in_order(silu, net.to_core(silu), net.core_first).reshape(4, features)
    cols = jnp.concatenate([dot(silu, enc_ada), dot(silu, dec_ada)], axis=1)
    cols = cols.reshape(2, 2, 2 * block)
    got = net.to_near(jnp.where(net.z0_first, cols[:, 1], cols[:, 0]))
    got, *rest = tie(got, *slots, *grad_parts, *plan.selects)
    slots, grad_parts, plan.selects = rest[:2], rest[2:4], rest[4:]
    code = jnp.concatenate([part[:, features] for part in slots]).astype(jnp.int32)
    place = jnp.arange(2 * tokens)
    matches = (place[:, None] // tokens == jnp.arange(2 * cap)[None, :] // cap) & (
        code[None, :] == place[:, None] % tokens
    )
    matches = matches.astype(F32)
    cols = in_order(jnp.where(net.z0_first, cols[:, 0], cols[:, 1]), got, net.z0_first)
    got = net.to_far(jnp.where(net.z1_first, cols[:, 1], cols[:, 0]))
    got, matches, *grad_parts = tie(got, matches, *grad_parts)
    cols = in_order(jnp.where(net.z1_first, cols[:, 0], cols[:, 1]), got, net.z1_first)
    grad_parts = net.spread_images(grad_parts)
    cols = in_order(cols, net.to_heads(cols), net.y_first)
    cols = jnp.moveaxis(cols, 0, 2).reshape(8, 2, block)
    enc_mod, dec_mod = tie(cols[:, 0].reshape(6, features), cols[:, 1].reshape(6, features))

    def attention(q, kv, kv_other, proj, hidden, *more):
        rows = q.shape[0]
        beside = [((rows, features), BF16)] if more else []
        return call(
            attention_kernel,
            [((rows, padded(width) + (1 + len(beside)) * features), BF16), ((rows, features), BF16)] + beside,
            q, kv, kv_other, proj, hidden, *more,
            scratch=[pltpu.VMEM((rows, width), F32)],
        )

    def mlp(x, part, other, mod, up, down, *more):
        rows = x.shape[0]
        beside = units + features + sum(a.shape[1] for a in more)
        return call(
            mlp_kernel,
            [((rows, features), F32), ((rows, units), F32), ((rows, beside), BF16), ((rows, features), BF16)],
            x, part, other, mod, up, down, *more,
        )

    def attention_back(grad_out, part, other, s, mod, proj):
        rows = grad_out.shape[0]
        return call(
            attention_back_kernel,
            [
                ((rows, features), F32), ((rows, features), BF16), ((rows, width), BF16),
                ((rows, 2 * width), F32), ((rows, 2 * width), BF16), ((3, features), F32),
            ],
            grad_out, part, other, s["residual"], s["branch"], s["branch_other"], mod, proj,
            s["q"], s["kv"], s["kv_other"], late=(3, 4, 5, 8, 9, 10),
            scratch=[pltpu.VMEM((2 * rows, width), F32)] * 2,
        )

    def qkv_back(dq, dkv, dkv_other, grad_branch, qkv):
        rows = dq.shape[0]
        return call(
            qkv_back_kernel, [((rows, padded(3 * width) + features), BF16), ((rows, features), BF16)],
            dq, dkv, dkv_other, grad_branch, qkv,
        )

    tick, place_rows = plan.tick, plan.place_rows

    rows = 2 * cap
    plan.put("grad_parts", *grad_parts)
    plan.later("silu", lambda: (net.gather_hi(silu).reshape(net.nhi * 4, features),))
    enc_mod, dec_mod = tick("e1", enc_mod, dec_mod)
    x, hidden, q, kv = call(
        enc_qkv_kernel,
        [((rows, features), F32), ((rows, features), BF16), ((rows, width), BF16), ((rows, 2 * width + 128), BF16)],
        *slots, enc_mod, enc_qkv, late=(3,),
    )
    kv_other = tick("e2", net.to_core(kv))
    enc_attn_rows, branch = attention(q, kv, kv_other, enc_proj, hidden)
    branch, up, down = load(branch, enc_up, enc_down)
    branch_other = tick("e3", net.to_heads(branch))
    residual, pre, enc_rows, mlp_part = mlp(
        x, branch, branch_other, enc_mod, up, down, enc_attn_rows
    )
    mlp_part, qkv = load(mlp_part, dec_qkv)
    mlp_other = net.to_heads(mlp_part)
    enc = dict(
        x=x, q=q, kv=kv, kv_other=kv_other, branch=branch, branch_other=branch_other,
        residual=residual, pre=pre, mlp=mlp_part, mlp_other=mlp_other,
    )
    place_rows("F", enc_rows)

    rows = 2 * tokens
    mlp_other = tick("d1", mlp_other)
    x, hidden, q, kv = call(
        dec_qkv_kernel,
        [((rows, features), F32), ((rows, features), BF16), ((rows, width), BF16), ((rows, 2 * width), BF16)],
        residual, mlp_part, mlp_other, enc_mod, matches, mask_token[None], dec_mod, qkv,
    )
    kv_other = tick("d2", net.to_core(kv))
    attn_rows, branch, grad_out = attention(
        q, kv, kv_other, dec_proj, hidden, *plan.get("grad_parts"), dec_mod
    )
    branch, up, down = load(branch, dec_up, dec_down)
    branch_other = net.to_heads(branch)
    place_rows("A", attn_rows)
    branch_other = tick("d3", branch_other)
    residual, pre, mlp_rows, mlp_part = mlp(x, branch, branch_other, dec_mod, up, down)
    dec = dict(
        x=x, q=q, kv=kv, kv_other=kv_other, branch=branch, branch_other=branch_other,
        residual=residual, pre=pre, grad_out=grad_out,
    )
    place_rows("M", mlp_rows)

    pre, mlp_part = tick("b1", pre, mlp_part)
    plan.put("mlp_part", mlp_part)
    plan.later("mlp_other", lambda: (net.to_heads(plan.get("mlp_part")[0]),))
    grad_rows, part = call(
        dec_mlp_back_kernel, [((rows, units), BF16), ((rows, features), BF16)],
        attn_rows, pre, up, down,
    )
    part = tick("b1x", part)
    part, proj = load(part, dec_proj)
    other = net.to_heads(part)
    place_rows("G", grad_rows)
    plan.later(
        "out_kernel",
        lambda: call(
            out_kernel, [((tokens, features), BF16)] * 2 + [((1, features), F32)],
            dec["residual"], *plan.get("mlp_part"), *plan.get("mlp_other"), dec_mod, dec["grad_out"],
            late=(0, 1, 4),
        ),
    )
    other = tick("b2", other)
    grad_residual, grad_branch, dq, dkv, dkv_other, dec_sums = attention_back(
        grad_out, part, other, dec, dec_mod, proj
    )
    dkv_other, qkv = load(dkv_other, dec_qkv)
    dkv_other = tick("b3", net.to_core(dkv_other))
    grad_attn_rows, part = qkv_back(dq, dkv, dkv_other, grad_branch, qkv)
    part, up, down = load(part, enc_up, enc_down)
    other = net.to_heads(part)
    place_rows("H", grad_attn_rows)
    plan.weight_grads("down", (((0, features), (1, 0, units)),), ("A", "M"))
    other = tick("b4", other)
    grad_enc, dec_more = call(
        dec_end_kernel, [((2 * cap, features), F32), ((3, features), F32)],
        part, other, grad_residual, dec["x"], dec_mod, matches, late=(2, 3),
    )

    rows = 2 * cap
    grad_out = tick("c1", grad_enc)
    enc_grad_rows, part = call(
        enc_mlp_back_kernel, [((rows, units + features), BF16), ((rows, features), BF16)],
        grad_out, enc["pre"], enc_mod, up, down, late=(1,),
    )
    part = tick("c1x", part)
    part, proj = load(part, enc_proj)
    other = net.to_heads(part)
    place_rows("E", enc_grad_rows)
    plan.weight_grads("up", (((0, units), (1, 0, units)),), ("M", "G"))
    other = tick("c2", other)
    grad_residual, grad_branch, dq, dkv, dkv_other, enc_sums = attention_back(
        grad_out, part, other, enc, enc_mod, proj
    )
    dkv_other, qkv = load(dkv_other, enc_qkv)
    dkv_other = tick("c3", net.to_core(dkv_other))
    enc_grad_attn_rows, part = qkv_back(dq, dkv, dkv_other, grad_branch, qkv)
    part = tick("c3x", part)
    other = net.to_heads(part)
    place_rows("K", enc_grad_attn_rows)
    plan.weight_grads(
        "attn", (((0, 0), (1, features, 3 * width)), ((1, 0), (0, 2 * features, width))),
        ("A", "H"),
    )
    other = tick("c4", other)
    *grad_in, enc_more = call(
        enc_end_kernel, [((cap, features), BF16)] * 2 + [((3, features), F32)],
        part, other, grad_residual, enc["x"], enc_mod, grad_out, enc["mlp"], enc["mlp_other"],
        late=(2, 3, 6, 7),
    )

    products = dict(
        enc_up=((((0, units), (1, 0, units)),), ("F", "E")),
        enc_down=((((1, units), (0, 0, units)),), ("F", "E")),
        enc_attn=(
            (
                ((0, units + features), (1, features, 3 * width)),
                ((1, 0), (0, units + 2 * features, width)),
            ),
            ("F", "K"),
        ),
    )
    share = features // (net.ndp * 4)
    shapes = {name: ((share, units),) for name in ("down", "up", "enc_down", "enc_up")}
    shapes["attn"] = shapes["enc_attn"] = ((3, share, width), (share, width))
    grads = {}
    chunk = features // 4
    assert 3 * chunk == block
    message = (2, 2 * 3 + 4, chunk)

    def modulation_rows(sums):
        sent, kept = call(
            columns_kernel, [(message, F32)] * 2, sums, net.to_core(sums), net.flags
        )
        sent, kept = call(images_kernel, [(message, F32)] * 2, kept, net.to_near(sent), net.flags)
        return call(
            all_images_kernel, [((4,) + message[1:], F32)], kept, net.to_far(sent), net.flags
        )

    plan.later(
        "modulation",
        lambda: (net.gather_hi(plan.get("images")[0]).reshape(net.nhi * 4, *message[1:]),),
    )

    last = enc_more
    for step in TAIL:
        kind, _, name = step.partition(" ")
        last = tick(step, last)
        if kind == "grads":
            last = plan.weight_grads(name, *products[name], after=(last,))
        elif kind == "halve":
            last = plan.halve(name, after=(last,))
        elif kind == "finish":
            grads[name] = finish(*plan.ends(name), *shapes[name], after=(last,))
            last = grads[name][0]
        elif step == "collect":
            last, *grad_in = tie(last, *grad_in)
            plan.later("parts", functools.partial(net.collect_parts, [
                jnp.concatenate([a, b]) for a, b in zip(plan.get("out_kernel")[:2], grad_in)
            ]))
        else:
            (vector,) = call(
                sums_kernel, [((13, features), F32)],
                enc_more, enc_sums, dec_more, dec_sums, plan.get("out_kernel")[2], after=(last,),
            )
            last = vector
            plan.later("images", functools.partial(modulation_rows, vector))

    both = plan.get("parts")
    out = net.collected([part[:tokens] for part in both])
    input_grad = net.collected([part[tokens:] for part in both]).astype(F32)
    enc_grads, dec_grads = (
        (
            jnp.transpose(grads[prefix + "attn"][0], (1, 0, 2)), grads[prefix + "attn"][1].T,
            grads[prefix + "up"][0], grads[prefix + "down"][0].T,
        )
        for prefix in ("enc_", "")
    )

    (rows,) = plan.get("modulation")
    (silu_all,) = plan.get("silu")
    silu_own = lax.dynamic_slice_in_dim(silu_all, net.dp * (4 * share), 4 * share, 1)
    enc_ada_grad, dec_ada_grad, mask_sum = call(
        ada_kernel, [((4 * share, block), F32)] * 2 + [((4, chunk), F32)], rows, silu_own
    )
    mask_grad = lax.dynamic_slice_in_dim(
        mask_sum.reshape(-1), (net.dp * 4 + net.z) * share, share, 0
    )
    return (out, input_grad, mask_grad, enc_ada_grad) + enc_grads + (dec_ada_grad,) + dec_grads

def solution(mesh):
    net = Net(mesh)
    in_specs = (
        P("dp", "region", None),
        P("dp", "region"),
        P("dp", "region"),
        P("dp", None),
        P(),
    ) + 2 * (
        P(None, ("region", "heads")),
        P(None, None, "heads"),
        P("heads", None),
        P(None, "heads"),
        P("heads", None),
    ) + (P("dp", "region", None),)
    out_specs = (
        P("dp", "region", None),
        P("dp", "region", None),
        P(("dp", "region")),
    ) + 2 * (
        P("dp", ("region", "heads")),
        P(("dp", "region"), None, "heads"),
        P("heads", ("dp", "region")),
        P(("dp", "region"), "heads"),
        P("heads", ("dp", "region")),
    )
    return jax.shard_map(
        lambda *args: shards(net, *args),
        mesh=mesh, in_specs=in_specs, out_specs=out_specs, check_vma=False,
    )
```

```python
import functools
import math

import jax
import jax.numpy as jnp
from jax import lax
from jax.experimental import pallas as pl
from jax.experimental.pallas import tpu as pltpu
from jax.sharding import PartitionSpec as P

HS = 72
SCALE = 1.0 / math.sqrt(HS)
EPSILON = 1e-06
BF16 = jnp.bfloat16
F32 = jnp.float32
VMEM_LIMIT = 16 * 2**20
LOAD_CHUNKS = 4
NT = ((1,), (1,))
TN = ((0,), (0,))


def dot(a, b, dims=((1,), (0,)), **kw):
    return lax.dot_general(a, b, (dims, ((), ())), preferred_element_type=F32, **kw)


class Late:
    def __init__(self, copy, ref):
        self.copy, self.ref, self.waited = copy, ref, False
        copy.start()

    def get(self):
        if not self.waited:
            self.copy.wait()
            self.waited = True
        return self.ref


def here(ref):
    return ref.get() if isinstance(ref, Late) else ref


def call(kernel, outs, *ins, scratch=(), late=(), after=()):
    shapes = [jax.ShapeDtypeStruct(shape, dtype) for shape, dtype in outs]
    fetched = [pltpu.VMEM(ins[i].shape, ins[i].dtype) for i in late]
    semaphores = [pltpu.SemaphoreType.DMA((len(late),))] if late else []

    def body(*refs):
        refs = list(refs)
        own = len(refs) - len(late) - len(semaphores)
        for at, i in enumerate(late):
            refs[i] = Late(pltpu.make_async_copy(refs[i], refs[own + at], refs[-1].at[at]), refs[own + at])
        kernel(*refs[: len(ins)], *refs[len(ins) + len(after) : own])
        for i in late:
            refs[i].get()

    vmem, hbm = pl.BlockSpec(memory_space=pltpu.VMEM), pl.BlockSpec(memory_space=pl.ANY)
    ins = [in_hbm(a) if i in late else a for i, a in enumerate(ins)]
    return pl.pallas_call(
        body,
        out_shape=shapes,
        in_specs=[hbm if i in late else vmem for i in range(len(ins))] + [hbm] * len(after),
        out_specs=[vmem] * len(outs),
        name=kernel.__name__,
        scratch_shapes=list(scratch) + fetched + semaphores,
        compiler_params=pltpu.CompilerParams(vmem_limit_bytes=VMEM_LIMIT),
        cost_estimate=pl.CostEstimate(flops=0, bytes_accessed=0, transcendentals=0),
    )(*ins, *after)


def in_hbm(a):
    return pltpu.with_memory_space_constraint(a, pltpu.HBM)


def load_kernel(*refs):
    count = len(refs) // 2
    copies = []
    for source, target in zip(refs[:count], refs[count : 2 * count]):
        rows = source.shape[0]
        chunk = -(-rows // LOAD_CHUNKS // 16) * 16
        for start in range(0, rows, chunk):
            part = pl.ds(start, min(chunk, rows - start))
            copies.append(
                pltpu.make_async_copy(source.at[part], target.at[part], refs[-1].at[len(copies)])
            )
            copies[-1].start()
    for copy in copies:
        copy.wait()


def load(anchor, *weights, beside=()):
    anchor, *weights = tie(anchor, *weights, *beside)
    weights, beside = weights[: len(weights) - len(beside)], weights[len(weights) - len(beside) :]
    weights = [in_hbm(w) for w in weights]
    loaded = pl.pallas_call(
        load_kernel,
        out_shape=[jax.ShapeDtypeStruct(w.shape, w.dtype) for w in weights],
        in_specs=[pl.BlockSpec(memory_space=pl.ANY)] * len(weights),
        out_specs=[pl.BlockSpec(memory_space=pltpu.VMEM)] * len(weights),
        name="load",
        scratch_shapes=[pltpu.SemaphoreType.DMA((LOAD_CHUNKS * len(weights),))],
        compiler_params=pltpu.CompilerParams(vmem_limit_bytes=VMEM_LIMIT),
        cost_estimate=pl.CostEstimate(
            flops=0, bytes_accessed=0, transcendentals=0
        ),
    )(*weights)
    return anchor, *loaded, *beside


def tie(*arrays):
    return lax.optimization_barrier(arrays)


def norm(rows):
    mean = jnp.mean(rows, axis=-1, keepdims=True)
    centered = rows - mean
    inverse = lax.rsqrt(jnp.mean(centered * centered, axis=-1, keepdims=True) + EPSILON)
    return centered * inverse, inverse


def norm_back(grad, normed, inverse):
    return inverse * (
        grad
        - jnp.mean(grad, axis=-1, keepdims=True)
        - normed * jnp.mean(grad * normed, axis=-1, keepdims=True)
    )


def padded(width):
    return -(-width // 128) * 128


def side(a):
    more = padded(a.shape[1]) - a.shape[1]
    return jnp.concatenate([a, jnp.zeros((a.shape[0], more), a.dtype)], axis=1) if more else a


def wide(ref):
    return here(ref)[...].astype(F32)


def row(ref, i):
    return ref[i : i + 1, :]


def total(ref, *columns):
    return jnp.sum(ref, axis=0, keepdims=True)


def qkv_rows(x, mod, qkv, hidden_ref, q_ref, kv_ref):
    width = q_ref.shape[1]
    hidden = (norm(x)[0] * (1.0 + row(mod, 1)) + row(mod, 0)).astype(BF16)
    hidden_ref[...] = hidden
    projected = dot(hidden, here(qkv)[...], NT).astype(BF16)
    q_ref[...] = projected[:, :width]
    kv_ref[:, : 2 * width] = projected[:, width:]


def enc_qkv_kernel(first, second, mod, qkv, x_ref, hidden_ref, q_ref, kv_ref):
    features = x_ref.shape[1]
    both = jnp.concatenate([first[...], second[...]])
    x = both[:, :features].astype(F32)
    x_ref[...] = x
    qkv_rows(x, mod, qkv, hidden_ref, q_ref, kv_ref)
    width = q_ref.shape[1]
    kv_ref[:, 2 * width :] = (both[:, features:].astype(F32) >= 0.0).astype(F32).astype(BF16)


def block_end(residual, part, other, mod):
    return residual[...] + row(mod, 5) * (wide(part) + wide(other))


def dec_qkv_kernel(
    residual, part, other, enc_mod, matches, mask, mod, qkv, x_ref, hidden_ref, q_ref, kv_ref
):
    enc_out = block_end(residual, part, other, enc_mod)
    found = matches[...]
    uncovered = 1.0 - jnp.sum(found, axis=1, keepdims=True)
    x = dot(found, enc_out, precision=lax.Precision.HIGHEST) + uncovered * wide(mask)
    x_ref[...] = x
    qkv_rows(x, mod, qkv, hidden_ref, q_ref, kv_ref)


def window(head, width):
    first, last = head * HS, (head + 1) * HS
    start, stop = first // 128 * 128, min(-(-last // 128) * 128, width)
    lanes = lax.broadcasted_iota(jnp.int32, (1, stop - start), 1) + start
    return slice(start, stop), ((lanes >= first) & (lanes < last)).astype(F32)


def probs_of(queries, keys, live):
    scores = dot(keys, queries, NT) * SCALE
    if live is not None:
        scores = jnp.where(live, scores, -1e30)
    exponent = jnp.exp(scores - jnp.max(scores, axis=0, keepdims=True))
    return exponent / jnp.sum(exponent, axis=0, keepdims=True)


def live_of(kv, kv_other, width):
    if kv.shape[1] == 2 * width:
        return None
    own, other = (a[:, 2 * width : 2 * width + 128].astype(F32)[:, :1] for a in (kv, kv_other))
    return jnp.concatenate([own, other]) > 0.5


def attention_kernel(q, kv, kv_other, proj, hidden, *refs):
    width, features = q.shape[1], hidden.shape[1]
    if len(refs) > 3:
        first, second, mod, rows_ref, part_ref, grad_ref, total_ref = refs
        grad_out = jnp.concatenate([first[...], second[...]])
        grad_ref[...] = grad_out
        rows_ref[:, features : 2 * features] = (row(mod, 5) * grad_out.astype(F32)).astype(BF16)
    else:
        rows_ref, part_ref, total_ref = refs
    rows_ref[:, :features] = hidden[...]
    live = live_of(kv, kv_other, width)
    total_ref[...] = jnp.zeros_like(total_ref)
    for head in range(width // HS):
        at, mask = window(head, width)
        beside = slice(width + at.start, width + at.stop)
        queries = (wide(q.at[:, at]) * mask).astype(BF16)
        keys = jnp.concatenate([kv[:, at], kv_other[:, at]])
        values = jnp.concatenate([kv[:, beside], kv_other[:, beside]])
        probs = probs_of(queries, keys, live).astype(BF16)
        total_ref[:, at] += dot(probs, values, TN) * mask
    attended = total_ref[...].astype(BF16)
    rows_ref[:, rows_ref.shape[1] - padded(width) :] = side(attended)
    part_ref[...] = dot(attended, here(proj)[...]).astype(BF16)


def mlp_kernel(x, part, other, mod, up, down, *refs):
    before, (residual_ref, pre_ref, rows_ref, part_ref) = refs[:-4], refs[-4:]
    features = x.shape[1]
    if before:
        rows_ref[:, up.shape[1] + features :] = before[0][...]
    hidden_units = up.shape[1]
    residual = x[...] + row(mod, 2) * (wide(part) + wide(other))
    residual_ref[...] = residual
    mlp_input = (norm(residual)[0] * (1.0 + row(mod, 4)) + row(mod, 3)).astype(BF16)
    rows_ref[:, hidden_units : hidden_units + features] = mlp_input
    pre = dot(mlp_input, up[...])
    pre_ref[...] = pre
    activated = jax.nn.gelu(pre, approximate=True).astype(BF16)
    rows_ref[:, :hidden_units] = activated
    part_ref[...] = dot(activated, down[...]).astype(BF16)


def gelu_slope(u):
    c = math.sqrt(2.0 / math.pi)
    t = jnp.tanh(c * (u + 0.044715 * u * u * u))
    return 0.5 * (1.0 + t) + 0.5 * u * (1.0 - t * t) * c * (1.0 + 3 * 0.044715 * u * u)


def enc_mlp_back_kernel(grad_out, pre, mod, up, down, rows_ref, part_ref):
    hidden_units = up.shape[1]
    grad_mlp = (row(mod, 5) * wide(grad_out)).astype(BF16)
    rows_ref[:, hidden_units:] = grad_mlp
    mlp_back(grad_mlp, pre, up, down, rows_ref, part_ref)


def dec_mlp_back_kernel(attn_rows, pre, up, down, rows_ref, part_ref):
    features = up.shape[0]
    mlp_back(attn_rows[:, features : 2 * features], pre, up, down, rows_ref, part_ref)


def mlp_back(grad_mlp, pre, up, down, rows_ref, part_ref):
    hidden_units = up.shape[1]
    grad_pre = (dot(grad_mlp, down[...], NT) * gelu_slope(here(pre)[...])).astype(BF16)
    rows_ref[:, :hidden_units] = grad_pre
    part_ref[...] = dot(grad_pre, up[...], NT).astype(BF16)


def attention_back_kernel(
    grad_out, part, other, residual, branch, branch_other, mod, proj, q, kv, kv_other,
    grad_residual_ref, grad_branch_ref, dq_ref, dkv_ref, dkv_other_ref, sums_ref,
    dk_ref, dv_ref,
):
    rows, width = dq_ref.shape
    grad_input = wide(part) + wide(other)
    normed, inverse = norm(here(residual)[...])
    sums_ref[0:1, :] = jnp.sum(grad_input, axis=0, keepdims=True)
    sums_ref[1:2, :] = jnp.sum(grad_input * normed, axis=0, keepdims=True)
    grad_residual = wide(grad_out) + norm_back(grad_input * (1.0 + row(mod, 4)), normed, inverse)
    grad_residual_ref[...] = grad_residual
    sums_ref[2:3, :] = jnp.sum(
        grad_residual * (wide(branch) + wide(branch_other)), axis=0, keepdims=True
    )
    grad_branch = (row(mod, 2) * grad_residual).astype(BF16)
    grad_branch_ref[...] = grad_branch
    grad_attended = dot(grad_branch, here(proj)[...], NT).astype(BF16).astype(F32)
    q, kv, kv_other = here(q), here(kv), here(kv_other)

    live = live_of(kv, kv_other, width)
    dk_ref[...] = jnp.zeros_like(dk_ref)
    dv_ref[...] = jnp.zeros_like(dv_ref)
    dq_total = []
    for head in range(width // HS):
        at, mask = window(head, width)
        beside = slice(width + at.start, width + at.stop)
        queries = (wide(q.at[:, at]) * mask).astype(BF16)
        grad_head = (grad_attended[:, at] * mask).astype(BF16)
        keys = jnp.concatenate([kv[:, at], kv_other[:, at]])
        values = jnp.concatenate([kv[:, beside], kv_other[:, beside]])
        probs = probs_of(queries, keys, live)
        grad_probs = dot(values, grad_head, NT)
        inner = jnp.sum(probs * grad_probs, axis=0, keepdims=True)
        grad_scores = (probs * (grad_probs - inner)).astype(BF16)
        dk_ref[:, at] += dot(grad_scores, queries)
        dv_ref[:, at] += dot(probs.astype(BF16), grad_head)
        dq_total.append((at, dot(grad_scores, keys, TN) * (mask * SCALE)))
    for tile in range(0, width, 128):
        stop = min(tile + 128, width)
        terms = [
            part_[:, tile - at.start : stop - at.start]
            for at, part_ in dq_total
            if at.start <= tile and stop <= at.stop
        ]
        dq_ref[:, tile:stop] = functools.reduce(lambda a, b: a + b, terms).astype(BF16)
    dkv_ref[:, :width] = dk_ref[:rows, :] * SCALE
    dkv_ref[:, width:] = dv_ref[:rows, :]
    dkv_other_ref[:, :width] = (dk_ref[rows:, :] * SCALE).astype(BF16)
    dkv_other_ref[:, width:] = dv_ref[rows:, :].astype(BF16)


def qkv_back_kernel(dq, dkv, dkv_other, grad_branch, qkv, rows_ref, part_ref):
    features = grad_branch.shape[1]
    grad_projected = jnp.concatenate(
        [dq[...], (dkv[...] + wide(dkv_other)).astype(BF16)], axis=1
    )
    rows_ref[:, :features] = grad_branch[...]
    rows_ref[:, features:] = side(grad_projected)
    part_ref[...] = dot(grad_projected, here(qkv)[...]).astype(BF16)


def block_back(part, other, grad_residual, x, mod, sums_ref):
    grad_hidden = wide(part) + wide(other)
    normed, inverse = norm(here(x)[...])
    sums_ref[0:1, :] = jnp.sum(grad_hidden, axis=0, keepdims=True)
    sums_ref[1:2, :] = jnp.sum(grad_hidden * normed, axis=0, keepdims=True)
    return here(grad_residual)[...] + norm_back(grad_hidden * (1.0 + row(mod, 1)), normed, inverse)


def dec_end_kernel(part, other, grad_residual, x, mod, matches, grad_ref, sums_ref):
    grad_x = block_back(part, other, grad_residual, x, mod, sums_ref)
    found = matches[...]
    uncovered = 1.0 - jnp.sum(found, axis=1, keepdims=True)
    sums_ref[2:3, :] = jnp.sum(uncovered * grad_x, axis=0, keepdims=True)
    grad_ref[...] = dot(found, grad_x, TN, precision=lax.Precision.HIGHEST)


def enc_end_kernel(
    part, other, grad_residual, x, mod, grad_out, mlp, mlp_other, first_ref, second_ref, sums_ref
):
    grad = block_back(part, other, grad_residual, x, mod, sums_ref).astype(BF16)
    half = first_ref.shape[0]
    first_ref[...], second_ref[...] = grad[:half], grad[half:]
    sums_ref[2:3, :] = jnp.sum(wide(grad_out) * (wide(mlp) + wide(mlp_other)), axis=0, keepdims=True)


def out_kernel(residual, part, other, mod, grad_out, first_ref, second_ref, sums_ref):
    out = block_end(here(residual), here(part), other, mod).astype(BF16)
    half = first_ref.shape[0]
    first_ref[...], second_ref[...] = out[:half], out[half:]
    sums_ref[...] = jnp.sum(wide(grad_out) * (wide(part) + wide(other)), axis=0, keepdims=True)


def sums_kernel(enc_more, enc_sums, dec_more, dec_sums, dec_gate, out_ref):
    out_ref[0:2, :] = enc_more[0:2, :]
    out_ref[2:3, :] = enc_sums[2:3, :]
    out_ref[3:5, :] = enc_sums[0:2, :]
    out_ref[5:6, :] = enc_more[2:3, :]
    out_ref[6:8, :] = dec_more[0:2, :]
    out_ref[8:9, :] = dec_sums[2:3, :]
    out_ref[9:11, :] = dec_sums[0:2, :]
    out_ref[11:12, :] = dec_gate[...]
    out_ref[12:13, :] = dec_more[2:3, :]


def chosen(flags, i, first, second):
    return jnp.where(flags[i : i + 1, :1] > 0.5, first, second)


def columns_kernel(sums, other, flags, sent_ref, kept_ref):
    total = sums[...] + other[...]
    chunk = sent_ref.shape[2]
    across = total.shape[1] // chunk
    count = (sent_ref.shape[1] - across) // 2

    def piece(first_row, i):
        at, lane = first_row + i // across, i % across * chunk
        return total[at : at + 1, lane : lane + chunk]

    def message(z):
        parts = [
            chosen(
                flags, 4, piece(first_row, 2 * z * count + i), piece(first_row, (2 * z + 1) * count + i)
            )
            for first_row in (0, 6)
            for i in range(count)
        ]
        return jnp.concatenate(parts + [piece(12, i) for i in range(across)])

    for high in range(2):
        low, odd = message(2 * high), message(2 * high + 1)
        sent_ref[high] = chosen(flags, 3, odd, low)
        kept_ref[high] = chosen(flags, 3, low, odd)


def images_kernel(kept, got, flags, sent_ref, kept_ref):
    for bit in range(2):
        low, high = (
            chosen(flags, 3, kept[i], got[i]) if bit == 0 else chosen(flags, 3, got[i], kept[i])
            for i in range(2)
        )
        sent_ref[bit] = chosen(flags, 2, high, low)
        kept_ref[bit] = chosen(flags, 2, low, high)


def all_images_kernel(kept, got, flags, out_ref):
    for bit in range(2):
        out_ref[bit] = chosen(flags, 2, kept[bit], got[bit])
        out_ref[2 + bit] = chosen(flags, 2, got[bit], kept[bit])


def ada_kernel(rows, silu, enc_ref, dec_ref, mask_ref):
    chunk = rows.shape[2]
    count = enc_ref.shape[1] // chunk
    for first, out in ((0, enc_ref), (count, dec_ref)):
        for i in range(count):
            out[:, i * chunk : (i + 1) * chunk] = dot(
                silu[...], rows[:, first + i, :].astype(BF16), TN
            )
    mask_ref[...] = jnp.sum(rows[:, 2 * count :, :], axis=0)


def weight_grad_kernel(products, unread, *refs):
    count = 1 + max(max(p[0][0], p[1][0]) for p in products)
    bundles, refs = refs[: 4 * count], refs[4 * count :]
    select, refs = refs[0], refs[1 + unread :]
    sent_ref, kept_ref, *buffers, semaphores = refs
    features = select.shape[1]
    half = sent_ref.shape[0]
    copies = []
    for at, ((narrow, first), (full, start, span)) in enumerate(products):
        for bundle, begin, size, buffer in (
            (narrow, first, features, buffers[2 * at]),
            (full, start, padded(span), buffers[2 * at + 1]),
        ):
            for part in range(4):
                source = bundles[4 * bundle + part]
                rows = source.shape[0]
                copies.append(
                    pltpu.make_async_copy(
                        source.at[:, begin : begin + size],
                        buffer.at[part * rows : (part + 1) * rows, :],
                        semaphores.at[len(copies)],
                    )
                )
                copies[-1].start()
    column = 0
    for at, (_, (_, _, span)) in enumerate(products):
        features_all, rows_all = buffers[2 * at], buffers[2 * at + 1]
        for copy in copies[8 * at : 8 * at + 4]:
            copy.wait()
        chosen = dot(select[...], features_all[...], NT).astype(BF16)
        for copy in copies[8 * at + 4 : 8 * at + 8]:
            copy.wait()
        sent_ref[:, column : column + span] = dot(chosen[:half], rows_all[:, :span]).astype(BF16)
        kept_ref[:, column : column + span] = dot(chosen[half:], rows_all[:, :span])
        column += span


def halve_kernel(kept, got, sent_ref, kept_ref):
    rows = kept_ref.shape[0]
    sums = here(kept)[...] + wide(got)
    kept_ref[...] = sums[:rows]
    sent_ref[...] = sums[rows:].astype(BF16)


def finish_kernel(kept, got, *outs):
    kept = here(kept)
    at = 0
    for out in outs:
        for part in range(out.shape[0] if len(out.shape) == 3 else 1):
            span = out.shape[-1]
            place = (part,) if len(out.shape) == 3 else ()
            out[place + (...,)] = kept[:, at : at + span] + wide(got.at[:, at : at + span])
            at += span


def in_order(mine, other, first):
    return jnp.stack([jnp.where(first, mine, other), jnp.where(first, other, mine)])


class Net:
    def __init__(self, mesh):
        self.ndp, self.nreg, self.nhead = (mesh.shape[a] for a in ("dp", "region", "heads"))
        assert self.nreg == 4 and self.nhead == 2 and self.ndp % 2 == 0
        self.nhi = self.ndp // 2
        self.core_perm = [(d, d ^ 1) for d in range(self.ndp)]
        self.near = [(z, z ^ 1) for z in range(4)]
        self.far = [(z, z ^ 2) for z in range(4)]
        self.spread = [
            [
                (d * 4 + r, (d - d % 2 + r // 2) * 4 + 2 * (d % 2) + (r + j) % 2)
                for d in range(self.ndp)
                for r in range(4)
            ]
            for j in range(2)
        ]

    def place(self, anchor):
        dp, z, y = (lax.axis_index(a) for a in ("dp", "region", "heads"))
        numbers = (dp, z) + tuple(
            bit == 0 for bit in (dp // 2 % 2, dp % 2, z // 2, z % 2, y)
        )
        flags = jnp.stack([jnp.broadcast_to(a, (128,)) for a in numbers[2:]]).astype(F32)
        anchor, self.flags, *numbers = tie(anchor, flags, *numbers)
        self.dp, self.z, self.hi_first, self.core_first, self.z1_first, self.z0_first, self.y_first = numbers
        return anchor

    def to_core(self, a):
        with jax.named_scope("core"):
            return lax.ppermute(a, "dp", self.core_perm)

    def to_near(self, a):
        with jax.named_scope("near"):
            return lax.ppermute(a, "region", self.near)

    def to_far(self, a):
        with jax.named_scope("far"):
            return lax.ppermute(a, "region", self.far)

    def to_heads(self, a):
        with jax.named_scope("heads"):
            return lax.ppermute(a, "heads", [(0, 1), (1, 0)])

    def to_hi(self, a):
        with jax.named_scope("hi"):
            return lax.ppermute(a, "dp", [(d, d ^ 2) for d in range(self.ndp)])

    def hi_groups(self):
        return [[c + 2 * h for h in range(self.nhi)] for c in range(2)]

    def gather_hi(self, a):
        if self.nhi == 1:
            return a[None]
        if self.nhi == 2:
            return in_order(a, self.to_hi(a), self.hi_first)
        return lax.all_gather(a, "dp", axis_index_groups=self.hi_groups(), axis=0)

    def spread_halves(self, a):
        return jnp.where(self.z0_first, a[0], a[1]), jnp.where(self.z0_first, a[1], a[0])

    def spread_images(self, halves):
        with jax.named_scope("spread"):
            return [
                lax.ppermute(part, ("dp", "region"), perm)
                for part, perm in zip(halves, self.spread)
            ]

    def collect_parts(self, parts):
        with jax.named_scope("collect"):
            return [
                lax.ppermute(part, ("dp", "region"), [(t, s) for s, t in perm])
                for part, perm in zip(parts, self.spread)
            ]

    def collected(self, back):
        return in_order(back[0], back[1], self.z0_first)

    def gather(self, rows, along_dp):
        if not along_dp:
            return rows, self.to_near(rows)
        if self.nhi == 2:
            return rows, self.to_hi(rows)
        if self.nhi > 2:
            rows = lax.all_gather(
                rows, "dp", axis_index_groups=self.hi_groups(), axis=0, tiled=True
            )
        half = rows.shape[0] // 2
        return rows[:half], rows[half:]

    def selection(self, features, along_dp):
        own = features // (self.ndp * 4)
        step = jnp.arange(4 * own)
        block = jnp.array([1, 3, 0, 2] if along_dp else [8, 10, 0, 2])[step // own]
        feature = ((self.dp * 4 + self.z) ^ block) * own + step % own
        return (feature[:, None] == jnp.arange(features)[None, :]).astype(BF16)

    def first_half(self, sent, along_dp):
        return self.to_near(sent) if along_dp else self.to_hi(sent)


def weight_grads(products, bundles, select, after=()):
    half = select.shape[0] // 2
    features = select.shape[1]
    width = sum(full[2] for _, full in products)
    rows = 4 * bundles[0][0].shape[0]
    operands = [in_hbm(a) for bundle in bundles for a in bundle]
    vmem, hbm = pl.BlockSpec(memory_space=pltpu.VMEM), pl.BlockSpec(memory_space=pl.ANY)
    buffers = [
        pltpu.VMEM((rows, padded(span)), BF16)
        for _, (_, _, size) in products
        for span in (features, size)
    ]
    held = sum(2 * math.prod(buffer.shape) for buffer in buffers) + 16 * 2**20
    return pl.pallas_call(
        functools.partial(weight_grad_kernel, products, len(after)),
        out_shape=[
            jax.ShapeDtypeStruct((half, width), BF16), jax.ShapeDtypeStruct((half, width), F32)
        ],
        in_specs=[hbm] * len(operands) + [vmem] + [hbm] * len(after),
        out_specs=[vmem] * 2,
        name="weight_grads",
        scratch_shapes=buffers + [pltpu.SemaphoreType.DMA((8 * len(products),))],
        compiler_params=pltpu.CompilerParams(vmem_limit_bytes=max(VMEM_LIMIT, held)),
        cost_estimate=pl.CostEstimate(
            flops=0,
            bytes_accessed=0,
            transcendentals=0,
        ),
    )(*operands, select, *after)


def finish(kept, got, *shapes, after=()):
    return call(finish_kernel, [(shape, F32) for shape in shapes], kept, got, after=after)


def halve(kept, got, after=()):
    rows, width = kept.shape
    return call(halve_kernel, [((rows // 2, width), BF16), ((rows // 2, width), F32)], kept, got, after=after)


DUE = {
    "grad_parts": "e3", "F far": "d3", "A far": "b2", "M far": "b3", "G far": "c1", "H far": "c2",
    "E far": "c4", "K far": "grads enc_attn", "mlp_other": "c4", "out_kernel": "modulation",
    "down grads": "b4", "down first": "c1x", "down halved": "c2", "down last": "c4",
    "up grads": "c2", "up first": "c4", "attn grads": "c4", "mlp_part": "c2",
    "modulation": "finish enc_down", "silu": "e3", "enc_down first": "halve enc_up", "images": "grads enc_down", "parts": "finish up",
}
DEC_ALONG_DP, ENC_ALONG_DP, ENC_ROWS = False, False, "FEK"
TAIL = (
    "halve up", "modulation", "grads enc_up", "grads enc_down", "halve attn", "collect",
    "grads enc_attn", "finish up", "halve enc_up", "finish attn", "halve enc_down",
    "halve enc_attn", "finish down", "finish enc_up", "finish enc_down", "finish enc_attn",
)


class Plan:
    def __init__(self, net, features):
        self.net, self.values, self.makers = net, {}, {}
        self.ways = [net.nhi != 2 or along_dp for along_dp in (DEC_ALONG_DP, ENC_ALONG_DP)]
        self.selects = tie(*(net.selection(features, way) for way in self.ways))

    def put(self, name, *arrays):
        self.values[name] = arrays

    def later(self, name, maker):
        self.makers[name] = maker

    def get(self, name):
        if name not in self.values:
            with jax.named_scope(name.replace(" ", "_")):
                self.put(name, *self.makers[name]())
        return self.values[name]

    def tick(self, point, *chain):
        names = [n for n in DUE if DUE[n] == point and (n in self.values or n in self.makers)]
        counts = [len(self.get(name)) for name in names]
        tied = list(tie(*chain, *(a for name in names for a in self.get(name))))
        chain, tied = tied[: len(chain)], tied[len(chain) :]
        for name, count in zip(names, counts):
            self.put(name, *tied[:count])
            tied = tied[count:]
        return chain[0] if len(chain) == 1 else chain

    def place_rows(self, name, rows):
        with jax.named_scope(name + "_far"):
            own, far = self.net.gather(rows, self.ways[name in ENC_ROWS])
        self.put(name + " own", own)
        self.put(name + " far", far)
        self.later(name + " core", lambda: (self.net.to_core(own),))
        self.later(name + " both", lambda: (self.net.to_core(self.get(name + " far")[0]),))

    def weight_grads(self, name, products, bundles, after=()):
        enc = bundles[0] in ENC_ROWS
        sets = [
            tuple(self.get(bundle + kind)[0] for kind in (" own", " far", " core", " both"))
            for bundle in bundles
        ]
        sent, kept = weight_grads(products, sets, self.selects[enc], after)
        self.put(name + " grads", sent, kept)
        self.later(
            name + " first", lambda: (self.net.first_half(self.get(name + " grads")[0], self.ways[enc]),)
        )
        self.later(name + " halved", lambda: self.halved(name))
        self.later(name + " last", lambda: (self.net.to_far(self.get(name + " halved")[0]),))
        return sent

    def halved(self, name, after=()):
        (got,), (_, kept) = self.get(name + " first"), self.get(name + " grads")
        return halve(kept, got, after)

    def halve(self, name, after):
        self.put(name + " halved", *self.halved(name, after))
        return self.get(name + " halved")[0]

    def ends(self, name):
        return self.get(name + " halved")[1], self.get(name + " last")[0]


def shards(
    net, enc_in, kept_pos, slot_live, condition, mask_token, enc_ada, enc_qkv, enc_proj, enc_up,
    enc_down, dec_ada, dec_qkv, dec_proj, dec_up, dec_down, cotangent,
):
    condition = net.place(condition)
    cap, features = enc_in.shape[1:]
    tokens = cotangent.shape[1]
    assert enc_in.shape[0] == 2
    width, units, block = enc_proj.shape[0], enc_up.shape[1], enc_ada.shape[1]
    plan = Plan(net, features)
    enc_qkv, dec_qkv = (
        jnp.transpose(a, (1, 2, 0)).reshape(3 * width, features) for a in (enc_qkv, dec_qkv)
    )

    code = jnp.where(slot_live > 0, kept_pos, -1).astype(BF16)
    sent = jnp.concatenate([enc_in, jnp.broadcast_to(code[..., None], code.shape + (128,))], axis=2)
    slots = net.spread_images(net.spread_halves(sent))
    grad_parts = net.spread_halves(cotangent)

    silu = jax.nn.silu(condition.astype(F32)).astype(BF16)
    silu = in_order(silu, net.to_core(silu), net.core_first).reshape(4, features)
    cols = jnp.concatenate([dot(silu, enc_ada), dot(silu, dec_ada)], axis=1)
    cols = cols.reshape(2, 2, 2 * block)
    got = net.to_near(jnp.where(net.z0_first, cols[:, 1], cols[:, 0]))
    got, *rest = tie(got, *slots, *grad_parts, *plan.selects)
    slots, grad_parts, plan.selects = rest[:2], rest[2:4], rest[4:]
    code = jnp.concatenate([part[:, features] for part in slots]).astype(jnp.int32)
    place = jnp.arange(2 * tokens)
    matches = (place[:, None] // tokens == jnp.arange(2 * cap)[None, :] // cap) & (
        code[None, :] == place[:, None] % tokens
    )
    matches = matches.astype(F32)
    cols = in_order(jnp.where(net.z0_first, cols[:, 0], cols[:, 1]), got, net.z0_first)
    got = net.to_far(jnp.where(net.z1_first, cols[:, 1], cols[:, 0]))
    got, matches, *grad_parts = tie(got, matches, *grad_parts)
    cols = in_order(jnp.where(net.z1_first, cols[:, 0], cols[:, 1]), got, net.z1_first)
    grad_parts = net.spread_images(grad_parts)
    cols = in_order(cols, net.to_heads(cols), net.y_first)
    cols = jnp.moveaxis(cols, 0, 2).reshape(8, 2, block)
    enc_mod, dec_mod = tie(cols[:, 0].reshape(6, features), cols[:, 1].reshape(6, features))

    def attention(q, kv, kv_other, proj, hidden, *more):
        rows = q.shape[0]
        beside = [((rows, features), BF16)] if more else []
        return call(
            attention_kernel,
            [((rows, padded(width) + (1 + len(beside)) * features), BF16), ((rows, features), BF16)] + beside,
            q, kv, kv_other, proj, hidden, *more,
            scratch=[pltpu.VMEM((rows, width), F32)],
        )

    def mlp(x, part, other, mod, up, down, *more):
        rows = x.shape[0]
        beside = units + features + sum(a.shape[1] for a in more)
        return call(
            mlp_kernel,
            [((rows, features), F32), ((rows, units), F32), ((rows, beside), BF16), ((rows, features), BF16)],
            x, part, other, mod, up, down, *more,
        )

    def attention_back(grad_out, part, other, s, mod, proj):
        rows = grad_out.shape[0]
        return call(
            attention_back_kernel,
            [
                ((rows, features), F32), ((rows, features), BF16), ((rows, width), BF16),
                ((rows, 2 * width), F32), ((rows, 2 * width), BF16), ((3, features), F32),
            ],
            grad_out, part, other, s["residual"], s["branch"], s["branch_other"], mod, proj,
            s["q"], s["kv"], s["kv_other"], late=(3, 4, 5, 8, 9, 10),
            scratch=[pltpu.VMEM((2 * rows, width), F32)] * 2,
        )

    def qkv_back(dq, dkv, dkv_other, grad_branch, qkv):
        rows = dq.shape[0]
        return call(
            qkv_back_kernel, [((rows, padded(3 * width) + features), BF16), ((rows, features), BF16)],
            dq, dkv, dkv_other, grad_branch, qkv,
        )

    tick, place_rows = plan.tick, plan.place_rows

    rows = 2 * cap
    plan.put("grad_parts", *grad_parts)
    plan.later("silu", lambda: (net.gather_hi(silu).reshape(net.nhi * 4, features),))
    enc_mod, dec_mod = tick("e1", enc_mod, dec_mod)
    x, hidden, q, kv = call(
        enc_qkv_kernel,
        [((rows, features), F32), ((rows, features), BF16), ((rows, width), BF16), ((rows, 2 * width + 128), BF16)],
        *slots, enc_mod, enc_qkv, late=(3,),
    )
    kv_other = tick("e2", net.to_core(kv))
    enc_attn_rows, branch = attention(q, kv, kv_other, enc_proj, hidden)
    branch, up, down = load(branch, enc_up, enc_down)
    branch_other = tick("e3", net.to_heads(branch))
    residual, pre, enc_rows, mlp_part = mlp(
        x, branch, branch_other, enc_mod, up, down, enc_attn_rows
    )
    mlp_part, qkv = load(mlp_part, dec_qkv)
    mlp_other = net.to_heads(mlp_part)
    enc = dict(
        x=x, q=q, kv=kv, kv_other=kv_other, branch=branch, branch_other=branch_other,
        residual=residual, pre=pre, mlp=mlp_part, mlp_other=mlp_other,
    )
    place_rows("F", enc_rows)

    rows = 2 * tokens
    mlp_other = tick("d1", mlp_other)
    x, hidden, q, kv = call(
        dec_qkv_kernel,
        [((rows, features), F32), ((rows, features), BF16), ((rows, width), BF16), ((rows, 2 * width), BF16)],
        residual, mlp_part, mlp_other, enc_mod, matches, mask_token[None], dec_mod, qkv,
    )
    kv_other = tick("d2", net.to_core(kv))
    attn_rows, branch, grad_out = attention(
        q, kv, kv_other, dec_proj, hidden, *plan.get("grad_parts"), dec_mod
    )
    branch, up, down = load(branch, dec_up, dec_down)
    branch_other = net.to_heads(branch)
    place_rows("A", attn_rows)
    branch_other = tick("d3", branch_other)
    residual, pre, mlp_rows, mlp_part = mlp(x, branch, branch_other, dec_mod, up, down)
    dec = dict(
        x=x, q=q, kv=kv, kv_other=kv_other, branch=branch, branch_other=branch_other,
        residual=residual, pre=pre, grad_out=grad_out,
    )
    place_rows("M", mlp_rows)

    pre, mlp_part = tick("b1", pre, mlp_part)
    plan.put("mlp_part", mlp_part)
    plan.later("mlp_other", lambda: (net.to_heads(plan.get("mlp_part")[0]),))
    grad_rows, part = call(
        dec_mlp_back_kernel, [((rows, units), BF16), ((rows, features), BF16)],
        attn_rows, pre, up, down,
    )
    part = tick("b1x", part)
    part, proj = load(part, dec_proj)
    other = net.to_heads(part)
    place_rows("G", grad_rows)
    plan.later(
        "out_kernel",
        lambda: call(
            out_kernel, [((tokens, features), BF16)] * 2 + [((1, features), F32)],
            dec["residual"], *plan.get("mlp_part"), *plan.get("mlp_other"), dec_mod, dec["grad_out"],
            late=(0, 1, 4),
        ),
    )
    other = tick("b2", other)
    grad_residual, grad_branch, dq, dkv, dkv_other, dec_sums = attention_back(
        grad_out, part, other, dec, dec_mod, proj
    )
    dkv_other, qkv = load(dkv_other, dec_qkv)
    dkv_other = tick("b3", net.to_core(dkv_other))
    grad_attn_rows, part = qkv_back(dq, dkv, dkv_other, grad_branch, qkv)
    part, up, down = load(part, enc_up, enc_down)
    other = net.to_heads(part)
    place_rows("H", grad_attn_rows)
    plan.weight_grads("down", (((0, features), (1, 0, units)),), ("A", "M"))
    other = tick("b4", other)
    grad_enc, dec_more = call(
        dec_end_kernel, [((2 * cap, features), F32), ((3, features), F32)],
        part, other, grad_residual, dec["x"], dec_mod, matches, late=(2, 3),
    )

    rows = 2 * cap
    grad_out = tick("c1", grad_enc)
    enc_grad_rows, part = call(
        enc_mlp_back_kernel, [((rows, units + features), BF16), ((rows, features), BF16)],
        grad_out, enc["pre"], enc_mod, up, down, late=(1,),
    )
    part = tick("c1x", part)
    part, proj = load(part, enc_proj)
    other = net.to_heads(part)
    place_rows("E", enc_grad_rows)
    plan.weight_grads("up", (((0, units), (1, 0, units)),), ("M", "G"))
    other = tick("c2", other)
    grad_residual, grad_branch, dq, dkv, dkv_other, enc_sums = attention_back(
        grad_out, part, other, enc, enc_mod, proj
    )
    dkv_other, qkv = load(dkv_other, enc_qkv)
    dkv_other = tick("c3", net.to_core(dkv_other))
    enc_grad_attn_rows, part = qkv_back(dq, dkv, dkv_other, grad_branch, qkv)
    part = tick("c3x", part)
    other = net.to_heads(part)
    place_rows("K", enc_grad_attn_rows)
    plan.weight_grads(
        "attn", (((0, 0), (1, features, 3 * width)), ((1, 0), (0, 2 * features, width))),
        ("A", "H"),
    )
    other = tick("c4", other)
    *grad_in, enc_more = call(
        enc_end_kernel, [((cap, features), BF16)] * 2 + [((3, features), F32)],
        part, other, grad_residual, enc["x"], enc_mod, grad_out, enc["mlp"], enc["mlp_other"],
        late=(2, 3, 6, 7),
    )

    products = dict(
        enc_up=((((0, units), (1, 0, units)),), ("F", "E")),
        enc_down=((((1, units), (0, 0, units)),), ("F", "E")),
        enc_attn=(
            (
                ((0, units + features), (1, features, 3 * width)),
                ((1, 0), (0, units + 2 * features, width)),
            ),
            ("F", "K"),
        ),
    )
    share = features // (net.ndp * 4)
    shapes = {name: ((share, units),) for name in ("down", "up", "enc_down", "enc_up")}
    shapes["attn"] = shapes["enc_attn"] = ((3, share, width), (share, width))
    grads = {}
    chunk = features // 4
    assert 3 * chunk == block
    message = (2, 2 * 3 + 4, chunk)

    def modulation_rows(sums):
        sent, kept = call(
            columns_kernel, [(message, F32)] * 2, sums, net.to_core(sums), net.flags
        )
        sent, kept = call(images_kernel, [(message, F32)] * 2, kept, net.to_near(sent), net.flags)
        return call(
            all_images_kernel, [((4,) + message[1:], F32)], kept, net.to_far(sent), net.flags
        )

    plan.later(
        "modulation",
        lambda: (net.gather_hi(plan.get("images")[0]).reshape(net.nhi * 4, *message[1:]),),
    )

    last = enc_more
    for step in TAIL:
        kind, _, name = step.partition(" ")
        last = tick(step, last)
        if kind == "grads":
            last = plan.weight_grads(name, *products[name], after=(last,))
        elif kind == "halve":
            last = plan.halve(name, after=(last,))
        elif kind == "finish":
            grads[name] = finish(*plan.ends(name), *shapes[name], after=(last,))
            last = grads[name][0]
        elif step == "collect":
            last, *grad_in = tie(last, *grad_in)
            plan.later("parts", functools.partial(net.collect_parts, [
                jnp.concatenate([a, b]) for a, b in zip(plan.get("out_kernel")[:2], grad_in)
            ]))
        else:
            (vector,) = call(
                sums_kernel, [((13, features), F32)],
                enc_more, enc_sums, dec_more, dec_sums, plan.get("out_kernel")[2], after=(last,),
            )
            last = vector
            plan.later("images", functools.partial(modulation_rows, vector))

    both = plan.get("parts")
    out = net.collected([part[:tokens] for part in both])
    input_grad = net.collected([part[tokens:] for part in both]).astype(F32)
    enc_grads, dec_grads = (
        (
            jnp.transpose(grads[prefix + "attn"][0], (1, 0, 2)), grads[prefix + "attn"][1].T,
            grads[prefix + "up"][0], grads[prefix + "down"][0].T,
        )
        for prefix in ("enc_", "")
    )

    (rows,) = plan.get("modulation")
    (silu_all,) = plan.get("silu")
    silu_own = lax.dynamic_slice_in_dim(silu_all, net.dp * (4 * share), 4 * share, 1)
    enc_ada_grad, dec_ada_grad, mask_sum = call(
        ada_kernel, [((4 * share, block), F32)] * 2 + [((4, chunk), F32)], rows, silu_own
    )
    mask_grad = lax.dynamic_slice_in_dim(
        mask_sum.reshape(-1), (net.dp * 4 + net.z) * share, share, 0
    )
    return (out, input_grad, mask_grad, enc_ada_grad) + enc_grads + (dec_ada_grad,) + dec_grads

def solution(mesh):
    net = Net(mesh)
    in_specs = (
        P("dp", "region", None),
        P("dp", "region"),
        P("dp", "region"),
        P("dp", None),
        P(),
    ) + 2 * (
        P(None, ("region", "heads")),
        P(None, None, "heads"),
        P("heads", None),
        P(None, "heads"),
        P("heads", None),
    ) + (P("dp", "region", None),)
    out_specs = (
        P("dp", "region", None),
        P("dp", "region", None),
        P(("dp", "region")),
    ) + 2 * (
        P("dp", ("region", "heads")),
        P(("dp", "region"), None, "heads"),
        P("heads", ("dp", "region")),
        P(("dp", "region"), "heads"),
        P("heads", ("dp", "region")),
    )
    return jax.shard_map(
        lambda *args: shards(net, *args),
        mesh=mesh, in_specs=in_specs, out_specs=out_specs, check_vma=False,
    )
```
